512 devices in a mesh: space: 64 (over x, z_hi, y, core), vec: 8 (over z_lo).
Axes of the slice: x: 4, y: 4, z: 16 (z_hi: 2, z_lo: 8; z = z_hi * 8 + z_lo), core: 2. Of those that a mesh axis runs over, the one named last changes fastest.
Arguments:
- vectors: bfloat16 [64, 3, 2, 256, 1024], P('space', None, None, 'vec'), may hold values from -6 to 6
- links: float32 [64, 3, 3, 3, 2, 1024], P('space'), may hold values from -2.5 to 2.5
- directions: int32 [3], replicated, may hold values from 0 to 2, each once
- offsets: int32 [5], replicated, may hold values from 0 to 4, each once
Outputs:
- elementals: float32 [3, 5, 2, 8, 1024], P(None, None, None, 'vec', 'space')
The draws below stay inside these ranges and needn't reach their ends.
Inputs may be any that keep to these rules, and one draw needn't show every extreme that they name: Each of the three lattice directions appears once. `offsets`: each block offset 0 to 4 appears once.
All inputs are finite; a program needn't handle non-finite values.
Results may differ from the reference program's by a relative error of at most 0.0029.
Values may be sent and summed in bfloat16 or wider, within the bound.
A program may use at most 64 MiB of HBM per device.

```python
import math
import jax
import jax.numpy as jnp
from jax import lax

VB = 32
NV = 256
LY = 64
LZ = 16
LX = 64
NDIR = 3
NOFF = 5


def block_levels(key, dims, split, low, top_value):
    gain = 1.0
    for axis_at, blocks in split:
        steps = jax.random.uniform(jax.random.fold_in(jax.random.fold_in(key, 6), axis_at), (blocks,), jnp.float32, low / len(split), top_value / len(split))
        gain = gain * jnp.repeat(jnp.exp(steps), dims[axis_at] // blocks).reshape((-1,) + (1,) * (len(dims) - 1 - axis_at))
    return gain


def normal_values(rng, extent, deviation, bound, pieces=(), kind=jnp.bfloat16):
    gain = block_levels(rng, extent, pieces, -0.22, 0.18) if pieces else 1.0
    array = jax.random.normal(rng, extent, jnp.float32) * deviation * gain
    return jnp.minimum(jnp.maximum(array, -bound), bound).astype(kind)


def setup_inputs(seed: int = 0) -> dict:
    key_list = jax.random.split(jax.random.key(seed), 5)
    vectors = normal_values(key_list[0], (LX, 3, 2, NV, LY * LZ), 1.0, 6.0, ((0, 64), (3, 8)))
    links = normal_values(key_list[1], (LX, 3, 3, 3, 2, LY * LZ), 0.4, 2.5, ((0, 64),), jnp.float32)
    directions = jax.random.permutation(key_list[2], 3).astype(jnp.int32)
    offsets = jax.random.permutation(key_list[3], NOFF).astype(jnp.int32)
    return dict(vectors=vectors, links=links, directions=directions, offsets=offsets)


def apply_link(link, vec):
    terms_re = []
    terms_im = []
    for col in range(3):
        link_re = link[:, col, 0][:, None, :]
        link_im = link[:, col, 1][:, None, :]
        vec_re = vec[col, 0][None]
        vec_im = vec[col, 1][None]
        terms_re.append(link_re * vec_re - link_im * vec_im)
        terms_im.append(link_re * vec_im + link_im * vec_re)
    real_part = terms_re[0] + terms_re[1] + terms_re[2]
    imag_part = terms_im[0] + terms_im[1] + terms_im[2]
    return jnp.stack([real_part, imag_part], axis=1)

def apply_dagger(link, vec):
    terms_re = []
    terms_im = []
    for col in range(3):
        link_re = link[col, :, 0][:, None, :]
        link_im = link[col, :, 1][:, None, :]
        vec_re = vec[col, 0][None]
        vec_im = vec[col, 1][None]
        terms_re.append(link_re * vec_re + link_im * vec_im)
        terms_im.append(link_re * vec_im - link_im * vec_re)
    real_part = terms_re[0] + terms_re[1] + terms_re[2]
    imag_part = terms_im[0] + terms_im[1] + terms_im[2]
    return jnp.stack([real_part, imag_part], axis=1)

def shift_plane(field, axis_mu, step):
    if axis_mu == 1:
        return jnp.roll(field, -step * LZ, axis=-1)
    shaped = field.reshape(field.shape[:-1] + (LY, LZ))
    return jnp.roll(shaped, -step, axis=-1).reshape(field.shape)

def displace(centre, above, below, plane_links, lower_x):
    results = [apply_link(plane_links[0], above) + apply_dagger(lower_x, below)]
    for axis_mu in (1, 2):
        forward = apply_link(plane_links[axis_mu], shift_plane(centre, axis_mu, 1))
        backward = apply_dagger(shift_plane(plane_links[axis_mu], axis_mu, -1), shift_plane(centre, axis_mu, -1))
        results.append(forward + backward)
    return jnp.stack(results).astype(jnp.bfloat16)

def reference(vectors, links, directions, offsets):
    blocks_count = NV // VB
    scale = 1.0 / math.sqrt(6.0 * LX * LY * LZ)

    def step(total, plane):
        upper = (plane + 1) % LX
        lower = (plane + LX - 1) % LX
        own = lax.dynamic_index_in_dim(vectors, plane, 0, keepdims=False)
        above = lax.dynamic_index_in_dim(vectors, upper, 0, keepdims=False).astype(jnp.float32)
        below = lax.dynamic_index_in_dim(vectors, lower, 0, keepdims=False).astype(jnp.float32)
        plane_links = lax.dynamic_index_in_dim(links, plane, 0, keepdims=False)
        lower_x = lax.dynamic_index_in_dim(links, lower, 0, keepdims=False)[0]
        shifted = displace(own.astype(jnp.float32), above, below, plane_links, lower_x)
        swapped = jnp.stack([-shifted[:, :, 1], shifted[:, :, 0]], axis=2)
        stacked = jnp.stack([shifted, swapped], axis=1).astype(jnp.float32)
        return (total + jnp.einsum('mtcprs,cpqs->mtrq', stacked, own.astype(jnp.float32)), None)
    start = jnp.zeros((NDIR, 2, NV, NV), jnp.float32)
    phi = lax.scan(step, start, jnp.arange(LX, dtype=jnp.int32))[0] * scale
    blocks = phi.reshape(NDIR, 2, blocks_count, VB, blocks_count, VB).transpose(0, 1, 2, 4, 3, 5)
    a_index = jnp.arange(blocks_count, dtype=jnp.int32)
    k_index = jnp.arange(NOFF, dtype=jnp.int32)
    b_index = (a_index[None, :] - k_index[:, None]) % blocks_count
    picked = blocks[:, :, a_index[None, :], b_index]
    picked = picked.transpose(0, 2, 1, 3, 4, 5)
    chosen = picked[directions[:, None], offsets[None, :]]
    return chosen.reshape(NDIR, NOFF, 2, blocks_count, VB * VB)
```

```python
import functools
import math

import jax
import jax.numpy as jnp
from jax import lax
from jax.experimental import pallas as pl
from jax.experimental.pallas import tpu as pltpu
from jax.sharding import PartitionSpec as P

LY = 64
LZ = 16
SITES = LY * LZ
VB = 32
HOPS = 4
NX, NH, NY, NC = 4, 2, 4, 2
CHIPS = NX * NH * NY


def send(src, dst, send_sem, recv_sem, **where):
    return pltpu.make_async_remote_copy(
        src_ref=src,
        dst_ref=dst,
        send_sem=send_sem,
        recv_sem=recv_sem,
        device_id=where,
        device_id_type=pl.DeviceIdType.MESH,
    )


def displace(rows, above, below, forward, backward, shifted):
    row0 = rows * 2 * VB

    def step(at, carry):
        half = lax.rem(at, 2)
        first = pl.multiple_of(half * 16, 16)
        lanes = pl.ds(pl.multiple_of(lax.div(at, 2) * 128, 128), 128)
        up = [[above[c, p, pl.ds(first, 16), lanes].astype(jnp.float32) for p in range(2)] for c in range(3)]
        down = [[below[c, p, pl.ds(first, 16), lanes].astype(jnp.float32) for p in range(2)] for c in range(3)]
        for row in range(3):
            terms_re = []
            terms_im = []
            back_re = []
            back_im = []
            for col in range(3):
                link_re = forward[row, col, pl.ds(0, 1), lanes]
                link_im = forward[row, col, pl.ds(1, 1), lanes]
                vec_re, vec_im = up[col]
                terms_re.append(link_re * vec_re - link_im * vec_im)
                terms_im.append(link_re * vec_im + link_im * vec_re)
                link_re = backward[col, row, pl.ds(0, 1), lanes]
                link_im = backward[col, row, pl.ds(1, 1), lanes]
                vec_re, vec_im = down[col]
                back_re.append(link_re * vec_re + link_im * vec_im)
                back_im.append(link_re * vec_im - link_im * vec_re)
            real = (terms_re[0] + terms_re[1] + terms_re[2]) + (back_re[0] + back_re[1] + back_re[2])
            imag = (terms_im[0] + terms_im[1] + terms_im[2]) + (back_im[0] + back_im[1] + back_im[2])
            shifted[row, pl.ds(row0 + first, 16), lanes] = real.astype(jnp.bfloat16)
            shifted[row, pl.ds(row0 + VB + first, 16), lanes] = imag.astype(jnp.bfloat16)
        return carry

    lax.fori_loop(0, 2 * SITES // 128, step, 0)


def z_moved(field, step):
    lane = lax.broadcasted_iota(jnp.int32, field.shape, field.ndim - 1)
    place = jnp.bitwise_and(lane, LZ - 1)
    last = field.ndim - 1
    if step == 1:
        return jnp.where(place == LZ - 1, pltpu.roll(field, LZ - 1, last), pltpu.roll(field, SITES - 1, last))
    return jnp.where(place == 0, pltpu.roll(field, SITES - LZ + 1, last), pltpu.roll(field, 1, last))


def kernel(
    vec_hbm,
    link_hbm,
    directions,
    offsets,
    out,
    blocks,
    above,
    below,
    links,
    lower,
    back,
    moved,
    shifted,
    acc,
    tiles,
    got_y,
    sum_y,
    got_x,
    sum_x,
    got_z,
    sum_z,
    got_c,
    picked,
    local_sem,
    ring_send,
    ring_recv,
    halo_send,
    halo_recv,
    y_send,
    y_recv,
    x_send,
    x_recv,
    pair_send,
    pair_recv,
    *,
    scale,
):
    space = lax.axis_index("space")
    vec = lax.axis_index("vec")
    planes = lax.axis_size("space")
    nvec = lax.axis_size("vec")
    core = lax.rem(space, NC)
    chip = lax.div(space, NC)
    y = lax.rem(chip, NY)
    z_hi = lax.rem(lax.div(chip, NY), NH)
    x = lax.div(chip, NY * NH)

    def at(x, z_hi, y, core):
        return ((x * NH + z_hi) * NY + y) * NC + core

    up = lax.rem(space + 1, planes)
    down = lax.rem(space + planes - 1, planes)
    after = lax.rem(vec + 1, nvec)
    before = lax.rem(vec + nvec - 1, nvec)
    y_peers = [at(x, z_hi, lax.rem(y + i, NY), core) for i in range(1, NY)]
    x_peers = [at(lax.rem(x + i, NX), z_hi, y, core) for i in range(1, NX)]
    z_peer = at(x, 1 - z_hi, y, core)
    c_peer = at(x, z_hi, y, 1 - core)

    own = pltpu.make_async_copy(vec_hbm.at[0], blocks.at[0], local_sem.at[0])
    own.start()
    links_in = pltpu.make_async_copy(link_hbm.at[0], links, local_sem.at[1])
    links_in.start()

    barrier = pltpu.get_barrier_semaphore()
    peers = [up, down, z_peer] + y_peers + x_peers
    for peer in peers:
        pl.semaphore_signal(barrier, inc=1, device_id={"space": peer}, device_id_type=pl.DeviceIdType.MESH)
    for peer in (after, before):
        pl.semaphore_signal(barrier, inc=1, device_id={"vec": peer}, device_id_type=pl.DeviceIdType.MESH)
    pl.semaphore_wait(barrier, len(peers) + 2)

    def hop(k, c):
        return send(blocks.at[k, c], blocks.at[k + 1, c], ring_send.at[k, c], ring_recv.at[k, c], vec=after)

    firsts = [
        send(vec_hbm.at[0, c], blocks.at[1, c], ring_send.at[0, c], ring_recv.at[0, c], vec=after) for c in range(3)
    ]
    for copy in firsts:
        copy.start()
    to_up = send(vec_hbm.at[0], below, halo_send.at[0], halo_recv.at[0], space=up)
    to_down = send(vec_hbm.at[0], above, halo_send.at[1], halo_recv.at[1], space=down)
    link_up = send(link_hbm.at[0, 0], lower, halo_send.at[2], halo_recv.at[2], space=up)
    to_up.start()
    to_down.start()
    link_up.start()

    own.wait()

    def move(i, carry):
        c = lax.div(i, 4)
        p = lax.rem(lax.div(i, 2), 2)
        rows = pl.ds(pl.multiple_of(lax.rem(i, 2) * 16, 16), 16)
        field = blocks[0, c, p, rows, :].astype(jnp.float32)
        moved[0, c, p, rows, :] = pltpu.roll(field, SITES - LZ, 1).astype(jnp.bfloat16)
        moved[1, c, p, rows, :] = pltpu.roll(field, LZ, 1).astype(jnp.bfloat16)
        moved[2, c, p, rows, :] = z_moved(field, 1).astype(jnp.bfloat16)
        moved[3, c, p, rows, :] = z_moved(field, -1).astype(jnp.bfloat16)
        return carry

    lax.fori_loop(0, 12, move, 0)
    links_in.wait()
    for row in range(3):
        for col in range(3):
            back[0, row, col] = pltpu.roll(links[1, row, col], LZ, 1)
            back[1, row, col] = z_moved(links[2, row, col], -1)
    displace(1, moved.at[0], moved.at[1], links.at[1], back.at[0], shifted)
    displace(2, moved.at[2], moved.at[3], links.at[2], back.at[1], shifted)

    def product(k, c, first, count):
        left = shifted[c, first : first + count, :]
        right = blocks[k, c].reshape(2 * VB, SITES)
        return lax.dot_general(left, right, (((1,), (1,)), ((), ())), preferred_element_type=jnp.float32)

    acc[...] = jnp.zeros_like(acc)
    yz = (2 * VB, 4 * VB)
    xs = (0, 2 * VB)

    def add(k, c, part):
        first, count = part
        acc[k, first : first + count, :] += product(k, c, first, count)

    def own_step(c, carry):
        add(0, c, yz)
        return carry

    lax.fori_loop(0, 3, own_step, 0)

    def ring_step(i, carry):
        k = lax.div(i, 3)
        c = lax.rem(i, 3)
        hop(k, c).wait_recv()
        hop(k + 1, c).start()
        add(k + 1, c, yz)
        return carry

    lax.fori_loop(0, 3 * (HOPS - 1), ring_step, 0)

    to_up.wait_recv()
    to_down.wait_recv()
    link_up.wait_recv()
    displace(0, above, below, links.at[0], lower, shifted)

    def x_step(i, carry):
        add(lax.div(i, 3), lax.rem(i, 3), xs)
        return carry

    lax.fori_loop(0, 3 * HOPS, x_step, 0)

    def last_step(c, carry):
        hop(HOPS - 1, c).wait_recv()
        add(HOPS, c, (0, 6 * VB))
        return carry

    lax.fori_loop(0, 3, last_step, 0)

    wide = [[] for _ in range(6)]
    tail = []
    for k in range(HOPS + 1):
        for mu in range(3):
            first = acc[k, mu * 2 * VB : mu * 2 * VB + VB, :]
            second = acc[k, mu * 2 * VB + VB : (mu + 1) * 2 * VB, :]
            real = first[:, :VB] + second[:, VB:]
            imag = first[:, VB:] - second[:, :VB]
            if k < HOPS:
                wide[2 * mu].append(real)
                wide[2 * mu + 1].append(imag)
            else:
                tail += [real, imag]
    for j in range(6):
        tiles[pl.ds(j, CHIPS, stride=8), :] = jnp.concatenate(wide[j], axis=1) * scale
    tiles[pl.ds(6, CHIPS, stride=8), :] = jnp.concatenate(tail[:4], axis=1) * scale
    empty = jnp.zeros((VB, 2 * VB), jnp.float32)
    tiles[pl.ds(7, CHIPS, stride=8), :] = jnp.concatenate(tail[4:] + [empty], axis=1) * scale

    sends = []

    def tile(xx, hh, yy):
        return pl.ds(pl.multiple_of(((xx * NH + hh) * NY + yy) * 8, 8), 8)

    for i in range(1, NY):
        yy = lax.rem(y + i, NY)
        for g in range(NX * NH):
            sends.append(
                send(
                    tiles.at[tile(0, g, yy)],
                    got_y.at[i - 1, pl.ds(g * 8, 8)],
                    y_send.at[i - 1, g],
                    y_recv.at[i - 1, g],
                    space=y_peers[i - 1],
                )
            )
            sends[-1].start()
    for copy in sends:
        copy.wait_recv()
    for g in range(NX * NH):
        total = tiles[tile(0, g, y), :]
        for i in range(NY - 1):
            total = total + got_y[i, pl.ds(g * 8, 8), :]
        sum_y[pl.ds(g * 8, 8), :] = total

    x_sends = []
    for i in range(1, NX):
        xx = lax.rem(x + i, NX)
        rows = pl.ds(pl.multiple_of(xx * NH * 8, 8), NH * 8)
        x_sends.append(
            send(sum_y.at[rows], got_x.at[i - 1], x_send.at[i - 1], x_recv.at[i - 1], space=x_peers[i - 1])
        )
        x_sends[-1].start()
    for copy in x_sends:
        copy.wait_recv()
    total = sum_y[pl.ds(pl.multiple_of(x * NH * 8, 8), NH * 8), :]
    for i in range(NX - 1):
        total = total + got_x[i]
    sum_x[...] = total

    z_copy = send(
        sum_x.at[pl.ds(pl.multiple_of((1 - z_hi) * 8, 8), 8)], got_z, pair_send.at[0], pair_recv.at[0], space=z_peer
    )
    z_copy.start()
    z_copy.wait_recv()
    sum_z[...] = sum_x[pl.ds(pl.multiple_of(z_hi * 8, 8), 8), :] + got_z[...]
    c_copy = send(sum_z, got_c, pair_send.at[1], pair_recv.at[1], space=c_peer)
    c_copy.start()
    c_copy.wait_recv()
    total = sum_z[...] + got_c[...]

    half = VB // 2
    for mu in range(3):
        for t in range(2):
            j = 2 * mu + t
            for k in range(HOPS + 1):
                row, lane = (j, k * VB) if k < HOPS else (6 + j // 4, (j % 4) * VB)
                low = total[row : row + 1, lane : lane + half]
                high = total[row : row + 1, lane + half : lane + VB]
                at_row = (mu * (HOPS + 1) + k) * 2 + t
                picked[at_row : at_row + 1, :half] = jnp.where(core == 0, low, high)
    for d in range(3):
        mu = directions[d]
        for q in range(HOPS + 1):
            rows = pl.ds((mu * (HOPS + 1) + offsets[q]) * 2, 2)
            out[d, q, :, 0, :] = picked[rows, :half]

    for copy in firsts + [to_up, to_down, link_up] + sends + x_sends + [z_copy, c_copy]:
        copy.wait_send()

    def drain(i, carry):
        hop(lax.div(i, 3) + 1, lax.rem(i, 3)).wait_send()
        return carry

    lax.fori_loop(0, 3 * (HOPS - 1), drain, 0)


def body(vectors, links, directions, offsets):
    planes = lax.axis_size("space")
    scale = 1.0 / math.sqrt(6.0 * planes * SITES)
    bf16, f32 = jnp.bfloat16, jnp.float32
    block = (3, 2, VB, SITES)
    dma = pltpu.SemaphoreType.DMA
    return pl.pallas_call(
        functools.partial(kernel, scale=scale),
        out_shape=jax.ShapeDtypeStruct((3, HOPS + 1, 2, 1, VB // 2), f32),
        in_specs=[
            pl.BlockSpec(memory_space=pl.ANY),
            pl.BlockSpec(memory_space=pl.ANY),
            pl.BlockSpec(memory_space=pltpu.SMEM),
            pl.BlockSpec(memory_space=pltpu.SMEM),
        ],
        out_specs=pl.BlockSpec(memory_space=pltpu.VMEM),
        scratch_shapes=[
            pltpu.VMEM((HOPS + 1,) + block, bf16),
            pltpu.VMEM(block, bf16),
            pltpu.VMEM(block, bf16),
            pltpu.VMEM((3, 3, 3, 2, SITES), f32),
            pltpu.VMEM((3, 3, 2, SITES), f32),
            pltpu.VMEM((2, 3, 3, 2, SITES), f32),
            pltpu.VMEM((4,) + block, bf16),
            pltpu.VMEM((3, 6 * VB, SITES), bf16),
            pltpu.VMEM((HOPS + 1, 6 * VB, 2 * VB), f32),
            pltpu.VMEM((CHIPS * 8, 128), f32),
            pltpu.VMEM((NY - 1, NX * NH * 8, 128), f32),
            pltpu.VMEM((NX * NH * 8, 128), f32),
            pltpu.VMEM((NX - 1, NH * 8, 128), f32),
            pltpu.VMEM((NH * 8, 128), f32),
            pltpu.VMEM((8, 128), f32),
            pltpu.VMEM((8, 128), f32),
            pltpu.VMEM((8, 128), f32),
            pltpu.VMEM((6 * (HOPS + 1) + 2, 128), f32),
            dma((2,)),
            dma((HOPS, 3)),
            dma((HOPS, 3)),
            dma((3,)),
            dma((3,)),
            dma((NY - 1, NX * NH)),
            dma((NY - 1, NX * NH)),
            dma((NX - 1,)),
            dma((NX - 1,)),
            dma((2,)),
            dma((2,)),
        ],
        compiler_params=pltpu.CompilerParams(
            collective_id=0, has_side_effects=True, vmem_limit_bytes=40 * 1024 * 1024
        ),
        name="elementals",
    )(vectors, links, directions, offsets)


def solution(mesh):
    placed = (
        P("space", None, None, "vec", None),
        P("space", None, None, None, None, None),
        P(),
        P(),
    )
    return jax.shard_map(
        body,
        mesh=mesh,
        in_specs=placed,
        out_specs=P(None, None, None, "vec", "space"),
        check_vma=False,
    )
```

```python
import functools
import math

import jax
import jax.numpy as jnp
from jax import lax
from jax.experimental import pallas as pl
from jax.experimental.pallas import tpu as pltpu
from jax.sharding import PartitionSpec as P

LY = 64
LZ = 16
SITES = LY * LZ
VB = 32
HOPS = 4
NX, NH, NY, NC = 4, 2, 4, 2
CHIPS = NX * NH * NY


def send(src, dst, send_sem, recv_sem, **where):
    return pltpu.make_async_remote_copy(
        src_ref=src,
        dst_ref=dst,
        send_sem=send_sem,
        recv_sem=recv_sem,
        device_id=where,
        device_id_type=pl.DeviceIdType.MESH,
    )


def displace(rows, above, below, forward, backward, shifted):
    row0 = rows * 2 * VB

    def step(at, carry):
        half = lax.rem(at, 2)
        first = pl.multiple_of(half * 16, 16)
        lanes = pl.ds(pl.multiple_of(lax.div(at, 2) * 128, 128), 128)
        up = [[above[c, p, pl.ds(first, 16), lanes].astype(jnp.float32) for p in range(2)] for c in range(3)]
        down = [[below[c, p, pl.ds(first, 16), lanes].astype(jnp.float32) for p in range(2)] for c in range(3)]
        for row in range(3):
            terms_re = []
            terms_im = []
            back_re = []
            back_im = []
            for col in range(3):
                link_re = forward[row, col, pl.ds(0, 1), lanes]
                link_im = forward[row, col, pl.ds(1, 1), lanes]
                vec_re, vec_im = up[col]
                terms_re.append(link_re * vec_re - link_im * vec_im)
                terms_im.append(link_re * vec_im + link_im * vec_re)
                link_re = backward[col, row, pl.ds(0, 1), lanes]
                link_im = backward[col, row, pl.ds(1, 1), lanes]
                vec_re, vec_im = down[col]
                back_re.append(link_re * vec_re + link_im * vec_im)
                back_im.append(link_re * vec_im - link_im * vec_re)
            real = (terms_re[0] + terms_re[1] + terms_re[2]) + (back_re[0] + back_re[1] + back_re[2])
            imag = (terms_im[0] + terms_im[1] + terms_im[2]) + (back_im[0] + back_im[1] + back_im[2])
            shifted[row, pl.ds(row0 + first, 16), lanes] = real.astype(jnp.bfloat16)
            shifted[row, pl.ds(row0 + VB + first, 16), lanes] = imag.astype(jnp.bfloat16)
        return carry

    lax.fori_loop(0, 2 * SITES // 128, step, 0)


def z_moved(field, step):
    lane = lax.broadcasted_iota(jnp.int32, field.shape, field.ndim - 1)
    place = jnp.bitwise_and(lane, LZ - 1)
    last = field.ndim - 1
    if step == 1:
        return jnp.where(place == LZ - 1, pltpu.roll(field, LZ - 1, last), pltpu.roll(field, SITES - 1, last))
    return jnp.where(place == 0, pltpu.roll(field, SITES - LZ + 1, last), pltpu.roll(field, 1, last))


def kernel(
    vec_hbm,
    link_hbm,
    directions,
    offsets,
    out,
    blocks,
    above,
    below,
    links,
    lower,
    back,
    moved,
    shifted,
    acc,
    shares,
    swapped,
    sums,
    arrived,
    picked,
    local_sem,
    ring_send,
    ring_recv,
    halo_send,
    halo_recv,
    pair_send,
    pair_recv,
    share_send,
    share_recv,
    *,
    scale,
):
    space = lax.axis_index("space")
    vec = lax.axis_index("vec")
    planes = lax.axis_size("space")
    nvec = lax.axis_size("vec")
    core = lax.rem(space, NC)
    chip = lax.div(space, NC)
    y = lax.rem(chip, NY)
    z_hi = lax.rem(lax.div(chip, NY), NH)
    x = lax.div(chip, NY * NH)

    def at(x, z_hi, y, core):
        return ((x * NH + z_hi) * NY + y) * NC + core

    up = lax.rem(space + 1, planes)
    down = lax.rem(space + planes - 1, planes)
    after = lax.rem(vec + 1, nvec)
    before = lax.rem(vec + nvec - 1, nvec)
    sibling = at(x, z_hi, y, 1 - core)

    def peer_chip(j):
        near = (j >= CHIPS // 2).astype(jnp.int32)
        step = j - near * (CHIPS // 2 - 1)
        dx, dy = lax.div(step, NY), lax.rem(step, NY)
        return (lax.rem(x + dx, NX) * NH + lax.rem(z_hi + 1 - near, NH)) * NY + lax.rem(y + dy, NY)

    own = pltpu.make_async_copy(vec_hbm.at[0], blocks.at[0], local_sem.at[0])
    own.start()
    links_in = pltpu.make_async_copy(link_hbm.at[0], links, local_sem.at[1])
    links_in.start()

    barrier = pltpu.get_barrier_semaphore()
    def greet(j, carry):
        peer = peer_chip(j) * NC + core
        pl.semaphore_signal(barrier, inc=1, device_id={"space": peer}, device_id_type=pl.DeviceIdType.MESH)
        return carry

    for peer in (up, down):
        pl.semaphore_signal(barrier, inc=1, device_id={"space": peer}, device_id_type=pl.DeviceIdType.MESH)
    for peer in (after, before):
        pl.semaphore_signal(barrier, inc=1, device_id={"vec": peer}, device_id_type=pl.DeviceIdType.MESH)
    lax.fori_loop(0, CHIPS - 1, greet, 0)
    pl.semaphore_wait(barrier, CHIPS + 3)

    def hop(k, c):
        return send(blocks.at[k, c], blocks.at[k + 1, c], ring_send.at[k, c], ring_recv.at[k, c], vec=after)

    firsts = [
        send(vec_hbm.at[0, c], blocks.at[1, c], ring_send.at[0, c], ring_recv.at[0, c], vec=after) for c in range(3)
    ]
    for copy in firsts:
        copy.start()
    to_up = send(vec_hbm.at[0], below, halo_send.at[0], halo_recv.at[0], space=up)
    to_down = send(vec_hbm.at[0], above, halo_send.at[1], halo_recv.at[1], space=down)
    link_up = send(link_hbm.at[0, 0], lower, halo_send.at[2], halo_recv.at[2], space=up)
    to_up.start()
    to_down.start()
    link_up.start()

    own.wait()

    def move(i, carry):
        c = lax.div(i, 4)
        p = lax.rem(lax.div(i, 2), 2)
        rows = pl.ds(pl.multiple_of(lax.rem(i, 2) * 16, 16), 16)
        field = blocks[0, c, p, rows, :].astype(jnp.float32)
        moved[0, c, p, rows, :] = pltpu.roll(field, SITES - LZ, 1).astype(jnp.bfloat16)
        moved[1, c, p, rows, :] = pltpu.roll(field, LZ, 1).astype(jnp.bfloat16)
        moved[2, c, p, rows, :] = z_moved(field, 1).astype(jnp.bfloat16)
        moved[3, c, p, rows, :] = z_moved(field, -1).astype(jnp.bfloat16)
        return carry

    lax.fori_loop(0, 12, move, 0)
    links_in.wait()
    for row in range(3):
        for col in range(3):
            back[0, row, col] = pltpu.roll(links[1, row, col], LZ, 1)
            back[1, row, col] = z_moved(links[2, row, col], -1)
    displace(1, moved.at[0], moved.at[1], links.at[1], back.at[0], shifted)
    displace(2, moved.at[2], moved.at[3], links.at[2], back.at[1], shifted)

    def product(k, c, first, count):
        left = shifted[c, first : first + count, :]
        half = VB // 2
        right = jnp.concatenate(
            [blocks[k, c, q, h * half : (h + 1) * half, :] for h in range(NC) for q in range(2)], axis=0
        )
        return lax.dot_general(left, right, (((1,), (1,)), ((), ())), preferred_element_type=jnp.float32)

    acc[...] = jnp.zeros_like(acc)
    yz = (2 * VB, 4 * VB)
    xs = (0, 2 * VB)

    def add(k, c, part):
        first, count = part
        acc[k, first : first + count, :] += product(k, c, first, count)

    def own_step(c, carry):
        add(0, c, yz)
        return carry

    lax.fori_loop(0, 3, own_step, 0)

    def ring_step(i, carry):
        k = lax.div(i, 3)
        c = lax.rem(i, 3)
        hop(k, c).wait_recv()
        hop(k + 1, c).start()
        add(k + 1, c, yz)
        return carry

    lax.fori_loop(0, 3 * (HOPS - 1), ring_step, 0)

    to_up.wait_recv()
    to_down.wait_recv()
    link_up.wait_recv()
    displace(0, above, below, links.at[0], lower, shifted)

    def x_step(i, carry):
        add(lax.div(i, 3), lax.rem(i, 3), xs)
        return carry

    lax.fori_loop(0, 3 * HOPS, x_step, 0)

    def groups(k, h):
        found = []
        for mu in range(3):
            first = acc[k, mu * 2 * VB : mu * 2 * VB + VB, :]
            second = acc[k, mu * 2 * VB + VB : (mu + 1) * 2 * VB, :]
            lane = h * VB
            half = VB // 2
            found.append(first[:, lane : lane + half] + second[:, lane + half : lane + VB])
            found.append(first[:, lane + half : lane + VB] - second[:, lane : lane + half])
        return found

    for h in range(NC):
        found = [g for k in range(HOPS) for g in groups(k, h)]
        for j in range(3):
            shares[h, :, j, :] = jnp.concatenate(found[8 * j : 8 * j + 8], axis=1)

    def last_step(c, carry):
        hop(HOPS - 1, c).wait_recv()
        add(HOPS, c, (0, 6 * VB))
        return carry

    lax.fori_loop(0, 3, last_step, 0)
    empty = jnp.zeros((VB, VB), jnp.float32)
    for h in range(NC):
        shares[h, :, 3, :] = jnp.concatenate(groups(HOPS, h) + [empty], axis=1)

    swap = send(shares.at[1 - core], swapped, pair_send, pair_recv, space=sibling)
    swap.start()
    swap.wait_recv()
    sums[...] = shares[core] + swapped[...]

    def share(j):
        dest = peer_chip(j)
        return send(sums.at[dest], arrived.at[j], share_send.at[j], share_recv.at[j], space=dest * NC + core)

    def share_start(j, carry):
        share(j).start()
        return carry

    def share_add(j, total):
        share(j).wait_recv()
        return total + arrived[j]

    lax.fori_loop(0, CHIPS - 1, share_start, 0)
    total = lax.fori_loop(0, CHIPS - 1, share_add, sums[chip]) * scale

    half = VB // 2
    for k in range(HOPS + 1):
        for j in range(6):
            group = k * 6 + j
            row, lane = group // 8, (group % 8) * half
            at_row = ((j // 2) * (HOPS + 1) + k) * 2 + j % 2
            picked[at_row : at_row + 1, :half] = total[row : row + 1, lane : lane + half]
    for d in range(3):
        mu = directions[d]
        for q in range(HOPS + 1):
            rows = pl.ds((mu * (HOPS + 1) + offsets[q]) * 2, 2)
            out[d, q, :, 0, :] = picked[rows, :half]

    for copy in firsts + [to_up, to_down, link_up, swap]:
        copy.wait_send()

    def share_drain(j, carry):
        share(j).wait_send()
        return carry

    lax.fori_loop(0, CHIPS - 1, share_drain, 0)

    def drain(i, carry):
        hop(lax.div(i, 3) + 1, lax.rem(i, 3)).wait_send()
        return carry

    lax.fori_loop(0, 3 * (HOPS - 1), drain, 0)


def body(vectors, links, directions, offsets):
    planes = lax.axis_size("space")
    scale = 1.0 / math.sqrt(6.0 * planes * SITES)
    bf16, f32 = jnp.bfloat16, jnp.float32
    block = (3, 2, VB, SITES)
    dma = pltpu.SemaphoreType.DMA
    return pl.pallas_call(
        functools.partial(kernel, scale=scale),
        out_shape=jax.ShapeDtypeStruct((3, HOPS + 1, 2, 1, VB // 2), f32),
        in_specs=[
            pl.BlockSpec(memory_space=pl.ANY),
            pl.BlockSpec(memory_space=pl.ANY),
            pl.BlockSpec(memory_space=pltpu.SMEM),
            pl.BlockSpec(memory_space=pltpu.SMEM),
        ],
        out_specs=pl.BlockSpec(memory_space=pltpu.VMEM),
        scratch_shapes=[
            pltpu.VMEM((HOPS + 1,) + block, bf16),
            pltpu.VMEM(block, bf16),
            pltpu.VMEM(block, bf16),
            pltpu.VMEM((3, 3, 3, 2, SITES), f32),
            pltpu.VMEM((3, 3, 2, SITES), f32),
            pltpu.VMEM((2, 3, 3, 2, SITES), f32),
            pltpu.VMEM((4,) + block, bf16),
            pltpu.VMEM((3, 6 * VB, SITES), bf16),
            pltpu.VMEM((HOPS + 1, 6 * VB, 2 * VB), f32),
            pltpu.VMEM((NC, CHIPS, 4, 128), f32),
            pltpu.VMEM((CHIPS, 4, 128), f32),
            pltpu.VMEM((CHIPS, 4, 128), f32),
            pltpu.VMEM((CHIPS - 1, 4, 128), f32),
            pltpu.VMEM((6 * (HOPS + 1) + 2, 128), f32),
            dma((2,)),
            dma((HOPS, 3)),
            dma((HOPS, 3)),
            dma((3,)),
            dma((3,)),
            dma,
            dma,
            dma((CHIPS - 1,)),
            dma((CHIPS - 1,)),
        ],
        compiler_params=pltpu.CompilerParams(
            collective_id=0, has_side_effects=True, vmem_limit_bytes=63 * 1024 * 1024
        ),
        name="elementals",
    )(vectors, links, directions, offsets)


def solution(mesh):
    placed = (
        P("space", None, None, "vec", None),
        P("space", None, None, None, None, None),
        P(),
        P(),
    )
    return jax.shard_map(
        body,
        mesh=mesh,
        in_specs=placed,
        out_specs=P(None, None, None, "vec", "space"),
        check_vma=False,
    )
```

```python
import functools
import math

import jax
import jax.numpy as jnp
from jax import lax
from jax.experimental import pallas as pl
from jax.experimental.pallas import tpu as pltpu
from jax.sharding import PartitionSpec as P

LZ = 16
SITES = 1024
VB = 32
NV = 256
NB = NV // VB
NK = 5
CHUNK = SITES // NB
NX, NH, NY, NC = 4, 2, 4, 2
ROWS = NX * NH * NY


def send(src, dst, send_sem, recv_sem, **where):
    return pltpu.make_async_remote_copy(
        src_ref=src,
        dst_ref=dst,
        send_sem=send_sem,
        recv_sem=recv_sem,
        device_id=where,
        device_id_type=pl.DeviceIdType.MESH,
    )


def kernel(
    vec_hbm,
    link_hbm,
    directions,
    offsets,
    out,
    own,
    held,
    above,
    edges,
    edge,
    links,
    moved,
    phi,
    parts,
    swapped,
    got_y,
    sum_y,
    got_x,
    sum_x,
    got_z,
    both,
    picked,
    local_sem,
    vec_send,
    vec_recv,
    edge_send,
    edge_recv,
    halo_send,
    halo_recv,
    swap_send,
    swap_recv,
    y_send,
    y_recv,
    x_send,
    x_recv,
    z_send,
    z_recv,
    last_send,
    last_recv,
    *,
    scale,
):
    space = lax.axis_index("space")
    lane = lax.axis_index("vec")
    planes = lax.axis_size("space")
    core = lax.rem(space, NC)
    y = lax.rem(lax.div(space, NC), NY)
    z_hi = lax.rem(lax.div(space, NC * NY), NH)
    x = lax.div(space, NC * NY * NH)
    up = lax.rem(space + 1, planes)
    down = lax.rem(space + planes - 1, planes)

    def at(x, z_hi, y, core):
        return ((x * NH + z_hi) * NY + y) * NC + core

    def flip(z_hi, lane):
        return lane + z_hi * (NB - 1 - 2 * lane)

    def half_of(space):
        return lax.rem(lax.div(space, NC * NY), NH)

    chunk = flip(z_hi, lane)
    up_lane = flip(half_of(up), chunk)
    down_lane = flip(half_of(down), chunk)
    sibling = at(x, z_hi, y, 1 - core)

    def lanes_of(chunk):
        return pl.ds(pl.multiple_of(chunk * CHUNK, CHUNK), CHUNK)

    def rows_of(block):
        return pl.ds(pl.multiple_of(block * VB, VB), VB)

    own_in = pltpu.make_async_copy(vec_hbm.at[0], own, local_sem.at[0])
    links_in = pltpu.make_async_copy(link_hbm.at[0, :, :, :, :, lanes_of(chunk)], links, local_sem.at[1])
    mine_in = pltpu.make_async_copy(
        vec_hbm.at[0, :, :, :, lanes_of(chunk)], held.at[:, :, rows_of(lane), :], local_sem.at[2]
    )
    own_in.start()
    links_in.start()
    mine_in.start()

    def z_peer(j):
        near = (j >= NB).astype(jnp.int32)
        return lax.rem(z_hi + 1 - near, NH), lax.rem(lane + j + near, NB)

    barrier = pltpu.get_barrier_semaphore()

    def greet(space, lane):
        pl.semaphore_signal(
            barrier, inc=1, device_id={"space": space, "vec": lane}, device_id_type=pl.DeviceIdType.MESH
        )

    def greet_z(j, carry):
        there, peer = z_peer(j)
        greet(at(x, there, y, core), peer)
        return carry

    lax.fori_loop(0, NH * NB - 1, greet_z, 0)
    for i in range(1, NY):
        greet(at(x, z_hi, lax.rem(y + i, NY), core), lane)
    for i in range(1, NX):
        greet(at(lax.rem(x + i, NX), z_hi, y, core), lane)
    greet(up, up_lane)
    greet(down, down_lane)

    place = lax.broadcasted_iota(jnp.int32, (16, CHUNK), 1)
    own_in.wait()

    def pack(i, carry):
        to = lax.div(i, 2)
        rows = pl.ds(pl.multiple_of(lax.rem(i, 2) * 16, 16), 16)
        found = jnp.zeros((16, CHUNK), jnp.float32)
        for n in range(6):
            field = own[n // 2, n % 2, rows, lanes_of(lax.rem(to + 1, NB))].astype(jnp.float32)
            found = jnp.where(place // LZ == n, pltpu.roll(field, n * LZ, 1) if n else field, found)
        edges[to, rows, :] = found.astype(jnp.bfloat16)
        return carry

    lax.fori_loop(0, 2 * NB, pack, 0)
    edge[lane] = edges[chunk]
    mine_in.wait()
    links_in.wait()

    pl.semaphore_wait(barrier, NH * NB - 1 + NY - 1 + NX - 1 + 2)

    def piece(j):
        to = lax.rem(lane + j, NB)
        return send(
            vec_hbm.at[0, :, :, :, lanes_of(flip(z_hi, to))],
            held.at[:, :, rows_of(lane), :],
            vec_send.at[j - 1],
            vec_recv.at[j - 1],
            vec=to,
        )

    def edge_piece(j):
        to = lax.rem(lane + j, NB)
        return send(edges.at[flip(z_hi, to)], edge.at[lane], edge_send.at[j - 1], edge_recv.at[j - 1], vec=to)

    def from_lane(j):
        block = lax.rem(lane + NB - j, NB)
        return (
            send(held.at[:, :, rows_of(block), :], held.at[:, :, rows_of(block), :], vec_send.at[j - 1], vec_recv.at[j - 1], vec=block),
            send(edges.at[0], edge.at[block], edge_send.at[j - 1], edge_recv.at[j - 1], vec=block),
        )

    def start_pieces(j, carry):
        piece(j).start()
        return carry

    def start_edges(j, carry):
        edge_piece(j).start()
        return carry

    lax.fori_loop(1, NB, start_pieces, 0)
    lax.fori_loop(1, NB, start_edges, 0)

    def halo(block):
        rows = rows_of(block)
        return pltpu.make_async_remote_copy(
            src_ref=held.at[:, :, rows, :],
            dst_ref=above.at[:, :, rows, :],
            send_sem=halo_send.at[block],
            recv_sem=halo_recv.at[block],
            device_id={"space": down, "vec": down_lane},
            device_id_type=pl.DeviceIdType.MESH,
        )

    def forward(mu, rows, vecs):
        for row in range(3):
            real = []
            imag = []
            for col in range(3):
                link_re = links[mu, row, col, pl.ds(0, 1), :]
                link_im = links[mu, row, col, pl.ds(1, 1), :]
                vec_re, vec_im = vecs[col]
                real.append(link_re * vec_re - link_im * vec_im)
                imag.append(link_re * vec_im + link_im * vec_re)
            moved[mu, row, 0, rows, :] = (real[0] + real[1] + real[2]).astype(jnp.bfloat16)
            moved[mu, row, 1, rows, :] = (imag[0] + imag[1] + imag[2]).astype(jnp.bfloat16)

    def move_yz(block):
        def step(i, carry):
            first = pl.multiple_of(i * 16, 16)
            rows = pl.ds(pl.multiple_of(block * VB + first, 16), 16)
            vecs = [[held[c, p, rows, :].astype(jnp.float32) for p in range(2)] for c in range(3)]
            border = edge[block, pl.ds(first, 16), :].astype(jnp.float32)
            along_y = [
                [
                    jnp.where(
                        place < CHUNK - LZ,
                        pltpu.roll(vecs[c][p], CHUNK - LZ, 1),
                        pltpu.roll(border, CHUNK - LZ - LZ * (2 * c + p), 1),
                    )
                    for p in range(2)
                ]
                for c in range(3)
            ]
            forward(1, rows, along_y)
            along_z = [
                [
                    jnp.where(place % LZ == LZ - 1, pltpu.roll(v, LZ - 1, 1), pltpu.roll(v, CHUNK - 1, 1))
                    for v in vecs[c]
                ]
                for c in range(3)
            ]
            forward(2, rows, along_z)
            return carry

        lax.fori_loop(0, 2, step, 0)

    def move_x(block):
        def step(i, carry):
            rows = pl.ds(pl.multiple_of(block * VB + i * 16, 16), 16)
            forward(0, rows, [[above[c, p, rows, :].astype(jnp.float32) for p in range(2)] for c in range(3)])
            return carry

        lax.fori_loop(0, 2, step, 0)

    halo(lane).start()
    move_yz(lane)

    def arrive(j, carry):
        block = lax.rem(lane + NB - j, NB)
        for copy in from_lane(j):
            copy.wait_recv()
        halo(block).start()
        move_yz(block)
        return carry

    lax.fori_loop(1, NB, arrive, 0)

    def product(mu):
        left = [
            jnp.concatenate([moved[mu, c, p] for c in range(3)] + [held[c, p] for c in range(3)], axis=1)
            for p in range(2)
        ]
        right = [
            jnp.concatenate([held[c, p] for c in range(3)] + [moved[mu, c, p] for c in range(3)], axis=1)
            for p in range(2)
        ]

        def dot(p, q):
            return lax.dot_general(
                left[p], right[q], (((1,), (1,)), ((), ())), preferred_element_type=jnp.float32
            )

        for t, total in enumerate((dot(0, 0) + dot(1, 1), dot(0, 1) - dot(1, 0))):
            for n in range(2):
                phi[mu, t, n] = total[:, n * 128 : (n + 1) * 128]

    product(1)
    product(2)

    def arrive_x(j, carry):
        block = lax.rem(up_lane + NB - j, NB)
        halo(block).wait_recv()
        move_x(block)
        return carry

    lax.fori_loop(0, NB, arrive_x, 0)
    product(0)

    wide = lax.broadcasted_iota(jnp.int32, (8, 128), 1)
    for t in range(2):
        for a in range(NB):
            turn = ((a + NB - 3) % NB) * VB
            for yy in range(NY):
                last = []
                for mu in range(3):
                    first, second = (
                        phi[mu, t, (n + turn // 128) % 2, pl.ds(a * VB + yy, 8, stride=NY), :] for n in range(2)
                    )
                    stay = 128 - turn % 128
                    if stay < 128:
                        first, second = pltpu.roll(first, stay, 1), pltpu.roll(second, stay, 1)
                        first, second = jnp.where(wide < stay, first, second), jnp.where(wide < stay, second, first)
                    parts[t, yy, mu, pl.ds(a, 8, stride=8), :] = first
                    shift = (mu * VB + VB) % 128
                    last.append(pltpu.roll(second, shift, 1))
                parts[t, yy, 3, pl.ds(a, 8, stride=8), :] = jnp.where(
                    wide < VB, last[0], jnp.where(wide < 2 * VB, last[1], last[2])
                )

    def swap(i):
        yy = lax.rem(y + i, NY)
        return send(parts.at[1 - core, yy], swapped.at[yy], swap_send.at[yy], swap_recv.at[yy], space=sibling)

    def to_y(i):
        yy = lax.rem(y + i, NY)
        return send(
            parts.at[core, yy], got_y.at[i - 1], y_send.at[i - 1], y_recv.at[i - 1], space=at(x, z_hi, yy, core)
        )

    def swap_start(i, carry):
        swap(i).start()
        return carry

    lax.fori_loop(1, NY + 1, swap_start, 0)

    def swap_add(i):
        yy = lax.rem(y + i, NY)
        swap(i).wait_recv()
        parts[core, yy] = parts[core, yy] + swapped[yy]

    def y_start(i, carry):
        swap_add(i)
        to_y(i).start()
        return carry

    lax.fori_loop(1, NY, y_start, 0)
    swap_add(NY)
    for i in range(1, NY):
        to_y(i).wait_recv()
    for b in range(4):
        for xx in range(NX):
            rows = pl.ds(xx * 16, 16)
            total = parts[core, y, b, rows, :]
            for i in range(NY - 1):
                total = total + got_y[i, b, rows, :]
            sum_y[xx, b] = total

    def to_x(i):
        xx = lax.rem(x + i, NX)
        return send(sum_y.at[xx], got_x.at[i - 1], x_send.at[i - 1], x_recv.at[i - 1], space=at(xx, z_hi, y, core))

    for i in range(1, NX):
        to_x(i).start()
    for i in range(1, NX):
        to_x(i).wait_recv()
    for b in range(4):
        total = sum_y[x, b]
        for i in range(NX - 1):
            total = total + got_x[i, b]
        sum_x[:, b, :] = total

    def to_z(j):
        there, peer = z_peer(j)
        return pltpu.make_async_remote_copy(
            src_ref=sum_x.at[there * NB + peer],
            dst_ref=got_z.at[j],
            send_sem=z_send.at[j],
            recv_sem=z_recv.at[j],
            device_id={"space": at(x, there, y, core), "vec": peer},
            device_id_type=pl.DeviceIdType.MESH,
        )

    def z_start(j, carry):
        to_z(j).start()
        return carry

    def z_add(j, total):
        to_z(j).wait_recv()
        return total + got_z[j]

    lax.fori_loop(0, NH * NB - 1, z_start, 0)
    both[core] = lax.fori_loop(0, NH * NB - 1, z_add, sum_x[z_hi * NB + lane]) * scale
    last = send(both.at[core], both.at[core], last_send, last_recv, space=sibling)
    last.start()
    last_in = send(both.at[1 - core], both.at[1 - core], last_send, last_recv, space=sibling)
    last_in.wait_recv()

    half = VB // 2
    for t in range(2):
        total = both[t]
        for mu in range(3):
            for k in range(NK):
                row, first = (mu, (3 - k) * VB) if k < 4 else (3, mu * VB)
                low = total[row : row + 1, first : first + half]
                high = total[row : row + 1, first + half : first + VB]
                at_row = (mu * NK + k) * 2 + t
                picked[at_row : at_row + 1, :half] = jnp.where(core == 0, low, high)
    for d in range(3):
        mu = directions[d]
        for q in range(NK):
            rows = pl.ds((mu * NK + offsets[q]) * 2, 2)
            out[d, q, :, 0, :] = picked[rows, :half]

    def drain(j, carry):
        piece(j).wait_send()
        edge_piece(j).wait_send()
        return carry

    def drain_halo(block, carry):
        halo(block).wait_send()
        return carry

    def drain_z(j, carry):
        to_z(j).wait_send()
        return carry

    lax.fori_loop(1, NB, drain, 0)
    lax.fori_loop(0, NB, drain_halo, 0)
    for i in range(1, NY + 1):
        swap(i).wait_send()
    for i in range(1, NY):
        to_y(i).wait_send()
    for i in range(1, NX):
        to_x(i).wait_send()
    lax.fori_loop(0, NH * NB - 1, drain_z, 0)
    last.wait_send()


def body(vectors, links, directions, offsets):
    planes = lax.axis_size("space")
    scale = 1.0 / math.sqrt(6.0 * planes * SITES)
    bf16, f32 = jnp.bfloat16, jnp.float32
    dma = pltpu.SemaphoreType.DMA
    zs = NH * NB - 1
    return pl.pallas_call(
        functools.partial(kernel, scale=scale),
        out_shape=jax.ShapeDtypeStruct((3, NK, 2, 1, VB // 2), f32),
        in_specs=[
            pl.BlockSpec(memory_space=pl.ANY),
            pl.BlockSpec(memory_space=pl.ANY),
            pl.BlockSpec(memory_space=pltpu.SMEM),
            pl.BlockSpec(memory_space=pltpu.SMEM),
        ],
        out_specs=pl.BlockSpec(memory_space=pltpu.VMEM),
        scratch_shapes=[
            pltpu.VMEM((3, 2, VB, SITES), bf16),
            pltpu.VMEM((3, 2, NV, CHUNK), bf16),
            pltpu.VMEM((3, 2, NV, CHUNK), bf16),
            pltpu.VMEM((NB, VB, CHUNK), bf16),
            pltpu.VMEM((NB, VB, CHUNK), bf16),
            pltpu.VMEM((3, 3, 3, 2, CHUNK), f32),
            pltpu.VMEM((3, 3, 2, NV, CHUNK), bf16),
            pltpu.VMEM((3, 2, 2, NV, 128), f32),
            pltpu.VMEM((2, NY, 4, 64, 128), f32),
            pltpu.VMEM((NY, 4, 64, 128), f32),
            pltpu.VMEM((NY - 1, 4, 64, 128), f32),
            pltpu.VMEM((NX, 4, 16, 128), f32),
            pltpu.VMEM((NX - 1, 4, 16, 128), f32),
            pltpu.VMEM((16, 4, 128), f32),
            pltpu.VMEM((zs, 4, 128), f32),
            pltpu.VMEM((2, 4, 128), f32),
            pltpu.VMEM((6 * NK + 2, 128), f32),
            dma((3,)),
            dma((NB - 1,)),
            dma((NB - 1,)),
            dma((NB - 1,)),
            dma((NB - 1,)),
            dma((NB,)),
            dma((NB,)),
            dma((NY,)),
            dma((NY,)),
            dma((NY - 1,)),
            dma((NY - 1,)),
            dma((NX - 1,)),
            dma((NX - 1,)),
            dma((zs,)),
            dma((zs,)),
            dma,
            dma,
        ],
        compiler_params=pltpu.CompilerParams(
            collective_id=0, has_side_effects=True, vmem_limit_bytes=63 * 1024 * 1024
        ),
        name="elementals",
    )(vectors, links, directions, offsets)


def solution(mesh):
    placed = (
        P("space", None, None, "vec", None),
        P("space", None, None, None, None, None),
        P(),
        P(),
    )
    return jax.shard_map(
        body,
        mesh=mesh,
        in_specs=placed,
        out_specs=P(None, None, None, "vec", "space"),
        check_vma=False,
    )
```

```python
import functools
import math

import jax
import jax.numpy as jnp
from jax import lax
from jax.experimental import pallas as pl
from jax.experimental.pallas import tpu as pltpu
from jax.sharding import PartitionSpec as P

LZ = 16
SITES = 1024
VB = 32
NV = 256
NB = NV // VB
NK = 5
CHUNK = SITES // NB
NX, NH, NY, NC = 4, 2, 4, 2
ROWS = NX * NH * NY


def send(src, dst, send_sem, recv_sem, **where):
    return pltpu.make_async_remote_copy(
        src_ref=src,
        dst_ref=dst,
        send_sem=send_sem,
        recv_sem=recv_sem,
        device_id=where,
        device_id_type=pl.DeviceIdType.MESH,
    )


def kernel(
    vec_hbm,
    link_hbm,
    directions,
    offsets,
    out,
    own,
    held,
    above,
    hold,
    edges,
    edge,
    links,
    moved,
    phi,
    parts,
    swapped,
    got_xy,
    sum_xy,
    got_z,
    both,
    picked,
    local_sem,
    vec_send,
    vec_recv,
    edge_send,
    edge_recv,
    halo_send,
    halo_recv,
    hold_send,
    hold_recv,
    swap_send,
    swap_recv,
    xy_send,
    xy_recv,
    z_send,
    z_recv,
    last_send,
    last_recv,
    *,
    scale,
):
    space = lax.axis_index("space")
    lane = lax.axis_index("vec")
    planes = lax.axis_size("space")
    core = lax.rem(space, NC)
    y = lax.rem(lax.div(space, NC), NY)
    z_hi = lax.rem(lax.div(space, NC * NY), NH)
    x = lax.div(space, NC * NY * NH)
    up = lax.rem(space + 1, planes)
    down = lax.rem(space + planes - 1, planes)

    def at(x, z_hi, y, core):
        return ((x * NH + z_hi) * NY + y) * NC + core

    def flip(z_hi, lane):
        return lane + z_hi * (NB - 1 - 2 * lane)

    def half_of(space):
        return lax.rem(lax.div(space, NC * NY), NH)

    chunk = flip(z_hi, lane)
    up_lane = flip(half_of(up), chunk)
    down_lane = flip(half_of(down), chunk)
    sibling = at(x, z_hi, y, 1 - core)

    def lanes_of(chunk):
        return pl.ds(pl.multiple_of(chunk * CHUNK, CHUNK), CHUNK)

    def rows_of(block):
        return pl.ds(pl.multiple_of(block * VB, VB), VB)

    own_in = pltpu.make_async_copy(vec_hbm.at[0], own, local_sem.at[0])
    links_in = pltpu.make_async_copy(link_hbm.at[0, :, :, :, :, lanes_of(chunk)], links, local_sem.at[1])
    mine_in = pltpu.make_async_copy(
        vec_hbm.at[0, :, :, :, lanes_of(chunk)], held.at[:, :, rows_of(lane), :], local_sem.at[2]
    )
    own_in.start()
    links_in.start()
    mine_in.start()

    def z_peer(j):
        near = (j >= NB).astype(jnp.int32)
        return lax.rem(z_hi + 1 - near, NH), lax.rem(lane + j + near, NB)

    barrier = pltpu.get_barrier_semaphore()

    def greet(space, lane):
        pl.semaphore_signal(
            barrier, inc=1, device_id={"space": space, "vec": lane}, device_id_type=pl.DeviceIdType.MESH
        )

    def greet_z(j, carry):
        there, peer = z_peer(j)
        greet(at(x, there, y, core), peer)
        return carry

    lax.fori_loop(0, NH * NB - 1, greet_z, 0)
    for i in range(1, NX * NY):
        greet(at(lax.rem(x + i % NX, NX), z_hi, lax.rem(y + i // NX, NY), core), lane)
    greet(up, up_lane)
    greet(down, down_lane)

    crossing = jnp.logical_and(y == 0, core == 0)
    crossed = jnp.logical_and(y == NY - 1, core == NC - 1)
    relays = jnp.logical_and(y > 0, core == 0)
    beyond = lax.rem(at(x, z_hi, 0, 0) + planes - 1, planes)
    beyond_lane = flip(half_of(beyond), chunk)

    @pl.when(crossed)
    def _():
        for q in range(1, NY):
            greet(up + q * NC, up_lane)

    place = lax.broadcasted_iota(jnp.int32, (16, CHUNK), 1)
    own_in.wait()

    def pack(i, carry):
        to = lax.div(i, 2)
        rows = pl.ds(pl.multiple_of(lax.rem(i, 2) * 16, 16), 16)
        found = jnp.zeros((16, CHUNK), jnp.float32)
        for n in range(6):
            field = own[n // 2, n % 2, rows, lanes_of(lax.rem(to + 1, NB))].astype(jnp.float32)
            found = jnp.where(place // LZ == n, pltpu.roll(field, n * LZ, 1) if n else field, found)
        edges[to, rows, :] = found.astype(jnp.bfloat16)
        return carry

    lax.fori_loop(0, 2 * NB, pack, 0)
    edge[lane] = edges[chunk]
    mine_in.wait()
    links_in.wait()

    pl.semaphore_wait(barrier, NH * NB - 1 + NX * NY - 1 + 2 + relays.astype(jnp.int32))

    def piece(j):
        to = lax.rem(lane + j, NB)
        return send(
            vec_hbm.at[0, :, :, :, lanes_of(flip(z_hi, to))],
            held.at[:, :, rows_of(lane), :],
            vec_send.at[j - 1],
            vec_recv.at[j - 1],
            vec=to,
        )

    def edge_piece(j):
        to = lax.rem(lane + j, NB)
        return send(edges.at[flip(z_hi, to)], edge.at[lane], edge_send.at[j - 1], edge_recv.at[j - 1], vec=to)

    def from_lane(j):
        block = lax.rem(lane + NB - j, NB)
        return (
            send(held.at[:, :, rows_of(block), :], held.at[:, :, rows_of(block), :], vec_send.at[j - 1], vec_recv.at[j - 1], vec=block),
            send(edges.at[0], edge.at[block], edge_send.at[j - 1], edge_recv.at[j - 1], vec=block),
        )

    def start_pieces(j, carry):
        piece(j).start()
        return carry

    def start_edges(j, carry):
        edge_piece(j).start()
        return carry

    lax.fori_loop(1, NB, start_pieces, 0)
    lax.fori_loop(1, NB, start_edges, 0)

    def halo(block):
        rows = rows_of(block)
        return pltpu.make_async_remote_copy(
            src_ref=held.at[:, :, rows, :],
            dst_ref=above.at[:, :, rows, :],
            send_sem=halo_send.at[block],
            recv_sem=halo_recv.at[block],
            device_id={"space": down, "vec": down_lane},
            device_id_type=pl.DeviceIdType.MESH,
        )

    def to_relay(j, block):
        n = lax.div(j, NY)
        return send(
            held.at[:, :, rows_of(block), :],
            hold.at[n],
            halo_send.at[block],
            hold_recv.at[n],
            space=at(x, z_hi, lax.rem(j, NY), core),
        )

    def start_halo(j, block):
        aside = jnp.logical_and(crossing, lax.rem(j, NY) != 0)

        @pl.when(aside)
        def _():
            to_relay(j, block).start()

        @pl.when(jnp.logical_not(aside))
        def _():
            halo(block).start()

    def handed(n):
        block = lax.rem(lane + 2 * NB - y - n * NY, NB)
        return pltpu.make_async_remote_copy(
            src_ref=hold.at[n],
            dst_ref=above.at[:, :, rows_of(block), :],
            send_sem=hold_send.at[n],
            recv_sem=halo_recv.at[block],
            device_id={"space": beyond, "vec": beyond_lane},
            device_id_type=pl.DeviceIdType.MESH,
        )

    def hand_on(n):
        send(hold.at[n], hold.at[n], hold_send.at[n], hold_recv.at[n], space=sibling).wait_recv()
        handed(n).start()

    def forward(mu, rows, vecs):
        for row in range(3):
            real = []
            imag = []
            for col in range(3):
                link_re = links[mu, row, col, pl.ds(0, 1), :]
                link_im = links[mu, row, col, pl.ds(1, 1), :]
                vec_re, vec_im = vecs[col]
                real.append(link_re * vec_re - link_im * vec_im)
                imag.append(link_re * vec_im + link_im * vec_re)
            moved[mu, row, 0, rows, :] = (real[0] + real[1] + real[2]).astype(jnp.bfloat16)
            moved[mu, row, 1, rows, :] = (imag[0] + imag[1] + imag[2]).astype(jnp.bfloat16)

    def move_yz(block):
        def step(i, carry):
            first = pl.multiple_of(i * 16, 16)
            rows = pl.ds(pl.multiple_of(block * VB + first, 16), 16)
            vecs = [[held[c, p, rows, :].astype(jnp.float32) for p in range(2)] for c in range(3)]
            border = edge[block, pl.ds(first, 16), :].astype(jnp.float32)
            along_y = [
                [
                    jnp.where(
                        place < CHUNK - LZ,
                        pltpu.roll(vecs[c][p], CHUNK - LZ, 1),
                        pltpu.roll(border, CHUNK - LZ - LZ * (2 * c + p), 1),
                    )
                    for p in range(2)
                ]
                for c in range(3)
            ]
            forward(1, rows, along_y)
            along_z = [
                [
                    jnp.where(place % LZ == LZ - 1, pltpu.roll(v, LZ - 1, 1), pltpu.roll(v, CHUNK - 1, 1))
                    for v in vecs[c]
                ]
                for c in range(3)
            ]
            forward(2, rows, along_z)
            return carry

        lax.fori_loop(0, 2, step, 0)

    def move_x(block):
        def step(i, carry):
            rows = pl.ds(pl.multiple_of(block * VB + i * 16, 16), 16)
            forward(0, rows, [[above[c, p, rows, :].astype(jnp.float32) for p in range(2)] for c in range(3)])
            return carry

        lax.fori_loop(0, 2, step, 0)

    start_halo(0, lane)
    move_yz(lane)

    def arrive(j, carry):
        block = lax.rem(lane + NB - j, NB)
        for copy in from_lane(j):
            copy.wait_recv()
        start_halo(j, block)
        move_yz(block)

        @pl.when(jnp.logical_and(jnp.logical_and(relays, j > 2), lax.rem(j + 2, NY) == y))
        def _():
            hand_on(lax.div(j - 2, NY))

        return carry

    lax.fori_loop(1, NB, arrive, 0)

    @pl.when(jnp.logical_and(relays, y > 1))
    def _():
        hand_on(1)


    def product(mu):
        left = [
            jnp.concatenate([moved[mu, c, p] for c in range(3)] + [held[c, p] for c in range(3)], axis=1)
            for p in range(2)
        ]
        right = [
            jnp.concatenate([held[c, p] for c in range(3)] + [moved[mu, c, p] for c in range(3)], axis=1)
            for p in range(2)
        ]

        def dot(p, q):
            return lax.dot_general(
                left[p], right[q], (((1,), (1,)), ((), ())), preferred_element_type=jnp.float32
            )

        for t, total in enumerate((dot(0, 0) + dot(1, 1), dot(0, 1) - dot(1, 0))):
            for n in range(2):
                phi[mu, t, n] = total[:, n * 128 : (n + 1) * 128]

    wide = lax.broadcasted_iota(jnp.int32, (8, 128), 1)

    def turned(mu, t, a, yy):
        turn = ((a + NB - 3) % NB) * VB
        first, second = (phi[mu, t, (n + turn // 128) % 2, pl.ds(a * VB + yy, 8, stride=NY), :] for n in range(2))
        stay = 128 - turn % 128
        if stay < 128:
            first, second = pltpu.roll(first, stay, 1), pltpu.roll(second, stay, 1)
            first, second = jnp.where(wide < stay, first, second), jnp.where(wide < stay, second, first)
        return first, second

    def lay(which, t, yy, b, a, rows):
        for xx in range(NX):
            parts[which, t, yy, xx, b, pl.ds(a, NH, stride=NB), :] = rows[NH * xx : NH * (xx + 1)]

    def lay_first():
        for t in range(2):
            for a in range(NB):
                for yy in range(NY):
                    for b in range(2):
                        lay(0, t, yy, b, a, turned(b + 1, t, a, yy)[0])

    def lay_second():
        for t in range(2):
            for a in range(NB):
                for yy in range(NY):
                    last = []
                    for mu in range(3):
                        first, second = turned(mu, t, a, yy)
                        if mu == 0:
                            lay(1, t, yy, 0, a, first)
                        last.append(pltpu.roll(second, (mu * VB + VB) % 128, 1))
                    lay(1, t, yy, 1, a, jnp.where(wide < VB, last[0], jnp.where(wide < 2 * VB, last[1], last[2])))

    def swap(which, i):
        yy = lax.rem(y + i, NY)
        return send(
            parts.at[which, 1 - core, yy],
            swapped.at[which, yy],
            swap_send.at[which, yy],
            swap_recv.at[which, yy],
            space=sibling,
        )

    def to_xy(which, i, j):
        yy, xx = lax.rem(y + i, NY), lax.rem(x + j, NX)
        slot = lax.rem(i, NY) * NX + j - 1
        return send(
            parts.at[which, core, yy, xx],
            got_xy.at[which, slot],
            xy_send.at[which, slot],
            xy_recv.at[which, slot],
            space=at(xx, z_hi, yy, core),
        )

    def sum_cores(which):
        def swap_start(i, carry):
            swap(which, i).start()
            return carry

        def swap_add(i):
            yy = lax.rem(y + i, NY)
            swap(which, i).wait_recv()
            parts[which, core, yy] = parts[which, core, yy] + swapped[which, yy]

        def xy_start(i, carry):
            swap_add(i)
            for j in range(NX):
                to_xy(which, i, j).start()
            return carry

        lax.fori_loop(1, NY + 1, swap_start, 0)
        lax.fori_loop(1, NY, xy_start, 0)
        swap_add(NY)
        for j in range(1, NX):
            to_xy(which, 0, j).start()

    def sum_chips(which):
        def xy_add(slot, totals):
            i, j = lax.div(slot + 1, NX), lax.rem(slot + 1, NX)
            to_xy(which, i, j).wait_recv()
            return tuple(totals[b] + got_xy[which, slot, b] for b in range(2))

        own_part = tuple(parts[which, core, y, x, b] for b in range(2))
        totals = lax.fori_loop(0, NX * NY - 1, xy_add, own_part)
        for b in range(2):
            sum_xy[:, 2 * which + b, :] = totals[b]

    product(1)
    product(2)
    lay_first()
    sum_cores(0)

    def arrive_x(j, carry):
        block = lax.rem(up_lane + NB - j, NB)
        halo(block).wait_recv()
        move_x(block)
        return carry

    lax.fori_loop(0, NB, arrive_x, 0)
    product(0)
    lay_second()
    sum_cores(1)
    sum_chips(0)
    sum_chips(1)

    def to_z(j):
        there, peer = z_peer(j)
        return pltpu.make_async_remote_copy(
            src_ref=sum_xy.at[there * NB + peer],
            dst_ref=got_z.at[j],
            send_sem=z_send.at[j],
            recv_sem=z_recv.at[j],
            device_id={"space": at(x, there, y, core), "vec": peer},
            device_id_type=pl.DeviceIdType.MESH,
        )

    def z_start(j, carry):
        to_z(j).start()
        return carry

    def z_add(j, total):
        to_z(j).wait_recv()
        return total + got_z[j]

    lax.fori_loop(0, NH * NB - 1, z_start, 0)
    both[core] = lax.fori_loop(0, NH * NB - 1, z_add, sum_xy[z_hi * NB + lane]) * scale
    last = send(both.at[core], both.at[core], last_send, last_recv, space=sibling)
    last.start()
    last_in = send(both.at[1 - core], both.at[1 - core], last_send, last_recv, space=sibling)
    last_in.wait_recv()

    half = VB // 2
    for t in range(2):
        total = both[t]
        for mu in range(3):
            for k in range(NK):
                row, first = ((mu + 2) % 3, (3 - k) * VB) if k < 4 else (3, mu * VB)
                low = total[row : row + 1, first : first + half]
                high = total[row : row + 1, first + half : first + VB]
                at_row = (mu * NK + k) * 2 + t
                picked[at_row : at_row + 1, :half] = jnp.where(core == 0, low, high)
    for d in range(3):
        mu = directions[d]
        for q in range(NK):
            rows = pl.ds((mu * NK + offsets[q]) * 2, 2)
            out[d, q, :, 0, :] = picked[rows, :half]

    def drain(j, carry):
        piece(j).wait_send()
        edge_piece(j).wait_send()
        return carry

    def drain_halo(block, carry):
        halo(block).wait_send()
        return carry

    @pl.when(relays)
    def _():
        for n in range(2):
            handed(n).wait_send()

    def drain_z(j, carry):
        to_z(j).wait_send()
        return carry

    lax.fori_loop(1, NB, drain, 0)
    lax.fori_loop(0, NB, drain_halo, 0)
    for which in range(2):

        def drain_swap(i, carry):
            swap(which, i).wait_send()
            return carry

        def drain_xy(slot, carry):
            to_xy(which, lax.div(slot + 1, NX), lax.rem(slot + 1, NX)).wait_send()
            return carry

        lax.fori_loop(1, NY + 1, drain_swap, 0)
        lax.fori_loop(0, NX * NY - 1, drain_xy, 0)
    lax.fori_loop(0, NH * NB - 1, drain_z, 0)
    last.wait_send()


def body(vectors, links, directions, offsets):
    planes = lax.axis_size("space")
    scale = 1.0 / math.sqrt(6.0 * planes * SITES)
    bf16, f32 = jnp.bfloat16, jnp.float32
    dma = pltpu.SemaphoreType.DMA
    zs = NH * NB - 1
    return pl.pallas_call(
        functools.partial(kernel, scale=scale),
        out_shape=jax.ShapeDtypeStruct((3, NK, 2, 1, VB // 2), f32),
        in_specs=[
            pl.BlockSpec(memory_space=pl.ANY),
            pl.BlockSpec(memory_space=pl.ANY),
            pl.BlockSpec(memory_space=pltpu.SMEM),
            pl.BlockSpec(memory_space=pltpu.SMEM),
        ],
        out_specs=pl.BlockSpec(memory_space=pltpu.VMEM),
        scratch_shapes=[
            pltpu.VMEM((3, 2, VB, SITES), bf16),
            pltpu.VMEM((3, 2, NV, CHUNK), bf16),
            pltpu.VMEM((3, 2, NV, CHUNK), bf16),
            pltpu.VMEM((2, 3, 2, VB, CHUNK), bf16),
            pltpu.VMEM((NB, VB, CHUNK), bf16),
            pltpu.VMEM((NB, VB, CHUNK), bf16),
            pltpu.VMEM((3, 3, 3, 2, CHUNK), f32),
            pltpu.VMEM((3, 3, 2, NV, CHUNK), bf16),
            pltpu.VMEM((3, 2, 2, NV, 128), f32),
            pltpu.VMEM((2, 2, NY, NX, 2, 16, 128), f32),
            pltpu.VMEM((2, NY, NX, 2, 16, 128), f32),
            pltpu.VMEM((2, NX * NY - 1, 2, 16, 128), f32),
            pltpu.VMEM((16, 4, 128), f32),
            pltpu.VMEM((zs, 4, 128), f32),
            pltpu.VMEM((2, 4, 128), f32),
            pltpu.VMEM((6 * NK + 2, 128), f32),
            dma((3,)),
            dma((NB - 1,)),
            dma((NB - 1,)),
            dma((NB - 1,)),
            dma((NB - 1,)),
            dma((NB,)),
            dma((NB,)),
            dma((2,)),
            dma((2,)),
            dma((2, NY)),
            dma((2, NY)),
            dma((2, NX * NY - 1)),
            dma((2, NX * NY - 1)),
            dma((zs,)),
            dma((zs,)),
            dma,
            dma,
        ],
        compiler_params=pltpu.CompilerParams(
            collective_id=0, has_side_effects=True, vmem_limit_bytes=63 * 1024 * 1024
        ),
        name="elementals",
    )(vectors, links, directions, offsets)


def solution(mesh):
    placed = (
        P("space", None, None, "vec", None),
        P("space", None, None, None, None, None),
        P(),
        P(),
    )
    return jax.shard_map(
        body,
        mesh=mesh,
        in_specs=placed,
        out_specs=P(None, None, None, "vec", "space"),
        check_vma=False,
    )
```

```python
import functools
import math

import jax
import jax.numpy as jnp
from jax import lax
from jax.experimental import pallas as pl
from jax.experimental.pallas import tpu as pltpu
from jax.sharding import PartitionSpec as P

LZ = 16
SITES = 1024
VB = 32
NV = 256
NB = NV // VB
WINDOW = 7
NK = 5
CHUNK = SITES // NB
NX, NH, NY, NC = 4, 2, 4, 2
ROWS = NX * NH * NY


def send(src, dst, send_sem, recv_sem, **where):
    return pltpu.make_async_remote_copy(
        src_ref=src,
        dst_ref=dst,
        send_sem=send_sem,
        recv_sem=recv_sem,
        device_id=where,
        device_id_type=pl.DeviceIdType.MESH,
    )


def kernel(
    vec_hbm,
    link_hbm,
    directions,
    offsets,
    out,
    own,
    held,
    above,
    hold,
    edges,
    edge,
    links,
    moved,
    order,
    ordered,
    far,
    parts,
    swapped,
    got_xy,
    sum_xy,
    got_z,
    both,
    picked,
    local_sem,
    vec_send,
    vec_recv,
    edge_send,
    edge_recv,
    halo_send,
    halo_recv,
    hold_send,
    hold_recv,
    swap_send,
    swap_recv,
    xy_send,
    xy_recv,
    z_send,
    z_recv,
    last_send,
    last_recv,
    *,
    scale,
):
    space = lax.axis_index("space")
    lane = lax.axis_index("vec")
    planes = lax.axis_size("space")
    core = lax.rem(space, NC)
    y = lax.rem(lax.div(space, NC), NY)
    z_hi = lax.rem(lax.div(space, NC * NY), NH)
    x = lax.div(space, NC * NY * NH)
    up = lax.rem(space + 1, planes)
    down = lax.rem(space + planes - 1, planes)

    def at(x, z_hi, y, core):
        return ((x * NH + z_hi) * NY + y) * NC + core

    def flip(z_hi, lane):
        return lane + z_hi * (NB - 1 - 2 * lane)

    def half_of(space):
        return lax.rem(lax.div(space, NC * NY), NH)

    chunk = flip(z_hi, lane)
    up_lane = flip(half_of(up), chunk)
    down_lane = flip(half_of(down), chunk)
    sibling = at(x, z_hi, y, 1 - core)

    def lanes_of(chunk):
        return pl.ds(pl.multiple_of(chunk * CHUNK, CHUNK), CHUNK)

    def rows_of(block):
        return pl.ds(pl.multiple_of(block * VB, VB), VB)

    own_in = pltpu.make_async_copy(vec_hbm.at[0], own, local_sem.at[0])
    links_in = pltpu.make_async_copy(link_hbm.at[0, :, :, :, :, lanes_of(chunk)], links, local_sem.at[1])
    mine_in = pltpu.make_async_copy(
        vec_hbm.at[0, :, :, :, lanes_of(chunk)], held.at[:, :, rows_of(lane), :], local_sem.at[2]
    )
    own_in.start()
    links_in.start()
    mine_in.start()

    def z_peer(j):
        near = (j >= NB).astype(jnp.int32)
        return lax.rem(z_hi + 1 - near, NH), lax.rem(lane + j + near, NB)

    barrier = pltpu.get_barrier_semaphore()

    def greet(space, lane):
        pl.semaphore_signal(
            barrier, inc=1, device_id={"space": space, "vec": lane}, device_id_type=pl.DeviceIdType.MESH
        )

    def greet_z(j, carry):
        there, peer = z_peer(j)
        greet(at(x, there, y, core), peer)
        return carry

    lax.fori_loop(0, NH * NB - 1, greet_z, 0)
    for i in range(1, NX * NY):
        greet(at(lax.rem(x + i % NX, NX), z_hi, lax.rem(y + i // NX, NY), core), lane)
    greet(up, up_lane)
    greet(down, down_lane)

    crossing = jnp.logical_and(y == 0, core == 0)
    crossed = jnp.logical_and(y == NY - 1, core == NC - 1)
    relays = jnp.logical_and(y > 0, core == 0)
    beyond = lax.rem(at(x, z_hi, 0, 0) + planes - 1, planes)
    beyond_lane = flip(half_of(beyond), chunk)

    @pl.when(crossed)
    def _():
        for q in range(1, NY):
            greet(up + q * NC, up_lane)

    pl.semaphore_wait(barrier, NH * NB - 1 + NX * NY - 1 + 2 + relays.astype(jnp.int32))

    def step_of(n):
        if isinstance(n, int):
            return (NB // 2 + (2 * (n % 2) - 1) * (n // 2)) if n else 0
        return (n > 0).astype(jnp.int32) * (NB // 2 + (2 * lax.rem(n, 2) - 1) * lax.div(n, 2))

    def block_of(lane, n):
        return lax.rem(lane + NB - step_of(n), NB)

    def piece(j):
        to = lax.rem(lane + j, NB)
        return send(
            vec_hbm.at[0, :, :, :, lanes_of(flip(z_hi, to))],
            held.at[:, :, rows_of(lane), :],
            vec_send.at[j - 1],
            vec_recv.at[j - 1],
            vec=to,
        )

    def edge_piece(j):
        to = lax.rem(lane + j, NB)
        return send(edges.at[flip(z_hi, to)], edge.at[lane], edge_send.at[j - 1], edge_recv.at[j - 1], vec=to)

    def from_lane(j):
        block = lax.rem(lane + NB - j, NB)
        return (
            send(held.at[:, :, rows_of(block), :], held.at[:, :, rows_of(block), :], vec_send.at[j - 1], vec_recv.at[j - 1], vec=block),
            send(edges.at[0], edge.at[block], edge_send.at[j - 1], edge_recv.at[j - 1], vec=block),
        )

    for n in range(1, WINDOW + 1):
        piece(step_of(n)).start()

    place = lax.broadcasted_iota(jnp.int32, (16, CHUNK), 1)
    row = lax.broadcasted_iota(jnp.int32, (NV, NV), 0)
    col = lax.broadcasted_iota(jnp.int32, (NV, NV), 1)
    source = (row % NB) * VB + (row // NB % (NX * NH)) * NY + row // (NB * NX * NH)
    order[...] = (col == source).astype(jnp.float32).astype(jnp.bfloat16)

    def in_order(rows):
        return jnp.dot(order[...], rows, preferred_element_type=jnp.float32).astype(jnp.bfloat16)

    own_in.wait()

    def pack(i, carry):
        to = lax.div(i, 2)
        rows = pl.ds(pl.multiple_of(lax.rem(i, 2) * 16, 16), 16)
        found = jnp.zeros((16, CHUNK), jnp.float32)
        for n in range(6):
            field = own[n // 2, n % 2, rows, lanes_of(lax.rem(to + 1, NB))].astype(jnp.float32)
            found = jnp.where(place // LZ == n, pltpu.roll(field, n * LZ, 1) if n else field, found)
        edges[to, rows, :] = found.astype(jnp.bfloat16)
        return carry

    lax.fori_loop(0, 2 * NB, pack, 0)
    edge[lane] = edges[chunk]
    mine_in.wait()
    links_in.wait()

    def start_edges(n, carry):
        edge_piece(step_of(n)).start()
        return carry

    lax.fori_loop(1, NB, start_edges, 0)

    def halo(block):
        rows = rows_of(block)
        return pltpu.make_async_remote_copy(
            src_ref=held.at[:, :, rows, :],
            dst_ref=above.at[:, :, rows, :],
            send_sem=halo_send.at[block],
            recv_sem=halo_recv.at[block],
            device_id={"space": down, "vec": down_lane},
            device_id_type=pl.DeviceIdType.MESH,
        )

    def to_relay(n, block):
        slot = lax.div(n, NY)
        return send(
            held.at[:, :, rows_of(block), :],
            hold.at[slot],
            halo_send.at[block],
            hold_recv.at[slot],
            space=at(x, z_hi, lax.rem(n + 1, NY), core),
        )

    def start_halo(n, block):
        aside = jnp.logical_and(crossing, lax.rem(n + 1, NY) != 0)

        @pl.when(aside)
        def _():
            to_relay(n, block).start()

        @pl.when(jnp.logical_not(aside))
        def _():
            halo(block).start()

    def handed(slot):
        block = block_of(lane, y - 1 + slot * NY)
        return pltpu.make_async_remote_copy(
            src_ref=hold.at[slot],
            dst_ref=above.at[:, :, rows_of(block), :],
            send_sem=hold_send.at[slot],
            recv_sem=halo_recv.at[block],
            device_id={"space": beyond, "vec": beyond_lane},
            device_id_type=pl.DeviceIdType.MESH,
        )

    def hand_on(n):
        send(hold.at[n], hold.at[n], hold_send.at[n], hold_recv.at[n], space=sibling).wait_recv()
        handed(n).start()

    def forward(mu, rows, vecs):
        for row in range(3):
            real = []
            imag = []
            for col in range(3):
                link_re = links[mu, row, col, pl.ds(0, 1), :]
                link_im = links[mu, row, col, pl.ds(1, 1), :]
                vec_re, vec_im = vecs[col]
                real.append(link_re * vec_re - link_im * vec_im)
                imag.append(link_re * vec_im + link_im * vec_re)
            moved[mu, row, 0, rows, :] = (real[0] + real[1] + real[2]).astype(jnp.bfloat16)
            moved[mu, row, 1, rows, :] = (imag[0] + imag[1] + imag[2]).astype(jnp.bfloat16)

    def move_yz(block):
        def step(i, carry):
            first = pl.multiple_of(i * 16, 16)
            rows = pl.ds(pl.multiple_of(block * VB + first, 16), 16)
            vecs = [[held[c, p, rows, :].astype(jnp.float32) for p in range(2)] for c in range(3)]
            border = edge[block, pl.ds(first, 16), :].astype(jnp.float32)
            along_y = [
                [
                    jnp.where(
                        place < CHUNK - LZ,
                        pltpu.roll(vecs[c][p], CHUNK - LZ, 1),
                        pltpu.roll(border, CHUNK - LZ - LZ * (2 * c + p), 1),
                    )
                    for p in range(2)
                ]
                for c in range(3)
            ]
            forward(1, rows, along_y)
            along_z = [
                [
                    jnp.where(place % LZ == LZ - 1, pltpu.roll(v, LZ - 1, 1), pltpu.roll(v, CHUNK - 1, 1))
                    for v in vecs[c]
                ]
                for c in range(3)
            ]
            forward(2, rows, along_z)
            return carry

        lax.fori_loop(0, 2, step, 0)

    def move_x(block):
        def step(i, carry):
            rows = pl.ds(pl.multiple_of(block * VB + i * 16, 16), 16)
            forward(0, rows, [[above[c, p, rows, :].astype(jnp.float32) for p in range(2)] for c in range(3)])
            return carry

        lax.fori_loop(0, 2, step, 0)

    start_halo(0, lane)
    move_yz(lane)

    def arrive(n, carry):
        piece(step_of(n)).wait_send()

        @pl.when(n + WINDOW < NB)
        def _():
            piece(step_of(n + WINDOW)).start()

        for copy in from_lane(step_of(n)):
            copy.wait_recv()
        block = block_of(lane, n)
        start_halo(n, block)
        move_yz(block)

        @pl.when(jnp.logical_and(jnp.logical_and(relays, n > 1), lax.rem(n + NY - 1, NY) == y))
        def _():
            hand_on(lax.div(n - 2, NY))

        return carry

    lax.fori_loop(1, NB, arrive, 0)

    @pl.when(jnp.logical_and(relays, y == NY - 1))
    def _():
        hand_on(1)


    tile = (NV, 128)
    row_a = lax.broadcasted_iota(jnp.int32, tile, 0) % NB
    slot = lax.broadcasted_iota(jnp.int32, tile, 1) // VB
    low_tile = (row_a - slot + NB) % NB < NB // 2

    def spread(rows):
        return rows.reshape(NY, NX, 16, 128)

    def product(mu, which, b):
        moved_mu = [jnp.concatenate([moved[mu, c, p] for c in range(3)], axis=1) for p in range(2)]
        held_all = [jnp.concatenate([held[c, p] for c in range(3)], axis=1) for p in range(2)]
        left = [jnp.concatenate([in_order(moved_mu[p]), ordered[p]], axis=1) for p in range(2)]
        right = [jnp.concatenate([held_all[p], moved_mu[p]], axis=1) for p in range(2)]

        def dot(p, q):
            return lax.dot_general(
                left[p], right[q], (((1,), (1,)), ((), ())), preferred_element_type=jnp.float32
            )

        for t, total in enumerate((dot(0, 0) + dot(1, 1), dot(0, 1) - dot(1, 0))):
            low, high = total[:, :128], total[:, 128:]
            parts[which, t, :, :, b] = spread(jnp.where(low_tile, low, high))
            rest = jnp.where(low_tile, high, low)
            if mu == 1:
                far[t] = pltpu.roll(rest, VB, 1)
            elif mu == 2:
                far[t] = jnp.where(slot == (row_a + 1) % 4, far[t], pltpu.roll(rest, 2 * VB, 1))
            else:
                parts[which, t, :, :, 1] = spread(jnp.where(slot == row_a % 4, rest, far[t]))

    def swap(which, i):
        yy = lax.rem(y + i, NY)
        return send(
            parts.at[which, 1 - core, yy],
            swapped.at[which, yy],
            swap_send.at[which, yy],
            swap_recv.at[which, yy],
            space=sibling,
        )

    def to_xy(which, i, j):
        yy, xx = lax.rem(y + i, NY), lax.rem(x + j, NX)
        slot = lax.rem(i, NY) * NX + j - 1
        return send(
            parts.at[which, core, yy, xx],
            got_xy.at[which, slot],
            xy_send.at[which, slot],
            xy_recv.at[which, slot],
            space=at(xx, z_hi, yy, core),
        )

    def sum_cores(which):
        def swap_start(i, carry):
            swap(which, i).start()
            return carry

        def swap_add(i):
            yy = lax.rem(y + i, NY)
            swap(which, i).wait_recv()
            parts[which, core, yy] = parts[which, core, yy] + swapped[which, yy]

        def xy_start(i, carry):
            swap_add(i)
            for j in range(NX):
                to_xy(which, i, j).start()
            return carry

        lax.fori_loop(1, NY + 1, swap_start, 0)
        lax.fori_loop(1, NY, xy_start, 0)
        swap_add(NY)
        for j in range(1, NX):
            to_xy(which, 0, j).start()

    def sum_chips(which):
        def xy_add(slot, totals):
            i, j = lax.div(slot + 1, NX), lax.rem(slot + 1, NX)
            to_xy(which, i, j).wait_recv()
            return tuple(totals[b] + got_xy[which, slot, b] for b in range(2))

        own_part = tuple(parts[which, core, y, x, b] for b in range(2))
        totals = lax.fori_loop(0, NX * NY - 1, xy_add, own_part)
        for b in range(2):
            sum_xy[:, 2 * which + b, :] = totals[b]

    for p in range(2):
        ordered[p] = in_order(jnp.concatenate([held[c, p] for c in range(3)], axis=1))
    product(1, 0, 0)
    product(2, 0, 1)
    sum_cores(0)

    def arrive_x(n, carry):
        block = block_of(up_lane, n)
        halo(block).wait_recv()
        move_x(block)
        return carry

    lax.fori_loop(0, NB, arrive_x, 0)
    product(0, 1, 0)
    sum_cores(1)
    sum_chips(0)
    sum_chips(1)

    def to_z(j):
        there, peer = z_peer(j)
        return pltpu.make_async_remote_copy(
            src_ref=sum_xy.at[there * NB + peer],
            dst_ref=got_z.at[j],
            send_sem=z_send.at[j],
            recv_sem=z_recv.at[j],
            device_id={"space": at(x, there, y, core), "vec": peer},
            device_id_type=pl.DeviceIdType.MESH,
        )

    def z_start(j, carry):
        to_z(j).start()
        return carry

    def z_add(j, total):
        to_z(j).wait_recv()
        return total + got_z[j]

    lax.fori_loop(0, NH * NB - 1, z_start, 0)
    both[core] = lax.fori_loop(0, NH * NB - 1, z_add, sum_xy[z_hi * NB + lane]) * scale
    last = send(both.at[core], both.at[core], last_send, last_recv, space=sibling)
    last.start()
    last_in = send(both.at[1 - core], both.at[1 - core], last_send, last_recv, space=sibling)
    last_in.wait_recv()

    half = VB // 2
    for t in range(2):
        total = pltpu.roll(both[t], (4 - lane % 4) % 4 * VB, 1)
        for mu in range(3):
            for k in range(NK):
                row, first = ((mu + 2) % 3, (4 - k) % 4 * VB) if k < 4 else (3, mu * VB)
                low = total[row : row + 1, first : first + half]
                high = total[row : row + 1, first + half : first + VB]
                at_row = (mu * NK + k) * 2 + t
                picked[at_row : at_row + 1, :half] = jnp.where(core == 0, low, high)
    for d in range(3):
        mu = directions[d]
        for q in range(NK):
            rows = pl.ds((mu * NK + offsets[q]) * 2, 2)
            out[d, q, :, 0, :] = picked[rows, :half]

    def drain(n, carry):
        edge_piece(n).wait_send()
        return carry

    def drain_halo(block, carry):
        halo(block).wait_send()
        return carry

    @pl.when(relays)
    def _():
        for n in range(2):
            handed(n).wait_send()

    def drain_z(j, carry):
        to_z(j).wait_send()
        return carry

    lax.fori_loop(1, NB, drain, 0)
    lax.fori_loop(0, NB, drain_halo, 0)
    for which in range(2):

        def drain_swap(i, carry):
            swap(which, i).wait_send()
            return carry

        def drain_xy(slot, carry):
            to_xy(which, lax.div(slot + 1, NX), lax.rem(slot + 1, NX)).wait_send()
            return carry

        lax.fori_loop(1, NY + 1, drain_swap, 0)
        lax.fori_loop(0, NX * NY - 1, drain_xy, 0)
    lax.fori_loop(0, NH * NB - 1, drain_z, 0)
    last.wait_send()


def body(vectors, links, directions, offsets):
    planes = lax.axis_size("space")
    scale = 1.0 / math.sqrt(6.0 * planes * SITES)
    bf16, f32 = jnp.bfloat16, jnp.float32
    dma = pltpu.SemaphoreType.DMA
    zs = NH * NB - 1
    return pl.pallas_call(
        functools.partial(kernel, scale=scale),
        out_shape=jax.ShapeDtypeStruct((3, NK, 2, 1, VB // 2), f32),
        in_specs=[
            pl.BlockSpec(memory_space=pl.ANY),
            pl.BlockSpec(memory_space=pl.ANY),
            pl.BlockSpec(memory_space=pltpu.SMEM),
            pl.BlockSpec(memory_space=pltpu.SMEM),
        ],
        out_specs=pl.BlockSpec(memory_space=pltpu.VMEM),
        scratch_shapes=[
            pltpu.VMEM((3, 2, VB, SITES), bf16),
            pltpu.VMEM((3, 2, NV, CHUNK), bf16),
            pltpu.VMEM((3, 2, NV, CHUNK), bf16),
            pltpu.VMEM((2, 3, 2, VB, CHUNK), bf16),
            pltpu.VMEM((NB, VB, CHUNK), bf16),
            pltpu.VMEM((NB, VB, CHUNK), bf16),
            pltpu.VMEM((3, 3, 3, 2, CHUNK), f32),
            pltpu.VMEM((3, 3, 2, NV, CHUNK), bf16),
            pltpu.VMEM((NV, NV), bf16),
            pltpu.VMEM((2, NV, 3 * CHUNK), bf16),
            pltpu.VMEM((2, NV, 128), f32),
            pltpu.VMEM((2, 2, NY, NX, 2, 16, 128), f32),
            pltpu.VMEM((2, NY, NX, 2, 16, 128), f32),
            pltpu.VMEM((2, NX * NY - 1, 2, 16, 128), f32),
            pltpu.VMEM((16, 4, 128), f32),
            pltpu.VMEM((zs, 4, 128), f32),
            pltpu.VMEM((2, 4, 128), f32),
            pltpu.VMEM((6 * NK + 2, 128), f32),
            dma((3,)),
            dma((NB - 1,)),
            dma((NB - 1,)),
            dma((NB - 1,)),
            dma((NB - 1,)),
            dma((NB,)),
            dma((NB,)),
            dma((2,)),
            dma((2,)),
            dma((2, NY)),
            dma((2, NY)),
            dma((2, NX * NY - 1)),
            dma((2, NX * NY - 1)),
            dma((zs,)),
            dma((zs,)),
            dma,
            dma,
        ],
        compiler_params=pltpu.CompilerParams(
            collective_id=0, has_side_effects=True, vmem_limit_bytes=63 * 1024 * 1024
        ),
        name="elementals",
    )(vectors, links, directions, offsets)


def solution(mesh):
    placed = (
        P("space", None, None, "vec", None),
        P("space", None, None, None, None, None),
        P(),
        P(),
    )
    return jax.shard_map(
        body,
        mesh=mesh,
        in_specs=placed,
        out_specs=P(None, None, None, "vec", "space"),
        check_vma=False,
    )
```

```python
import functools
import math

import jax
import jax.numpy as jnp
from jax import lax
from jax.experimental import pallas as pl
from jax.experimental.pallas import tpu as pltpu
from jax.sharding import PartitionSpec as P

LZ = 16
SITES = 1024
VB = 32
NV = 256
NB = NV // VB
NK = 5
CHUNK = SITES // NB
NX, NH, NY, NC = 4, 2, 4, 2
ROWS = NX * NH * NY


def send(src, dst, send_sem, recv_sem, **where):
    return pltpu.make_async_remote_copy(
        src_ref=src,
        dst_ref=dst,
        send_sem=send_sem,
        recv_sem=recv_sem,
        device_id=where,
        device_id_type=pl.DeviceIdType.MESH,
    )


def kernel(
    vec_hbm,
    link_hbm,
    directions,
    offsets,
    out,
    own,
    held,
    above,
    hold,
    edges,
    edge,
    links,
    moved,
    order,
    ordered,
    far,
    parts,
    swapped,
    got_xy,
    sum_xy,
    got_z,
    picked,
    local_sem,
    vec_send,
    vec_recv,
    edge_send,
    edge_recv,
    halo_send,
    halo_recv,
    hold_send,
    hold_recv,
    swap_send,
    swap_recv,
    xy_send,
    xy_recv,
    z_send,
    z_recv,
    *,
    scale,
):
    space = lax.axis_index("space")
    lane = lax.axis_index("vec")
    planes = lax.axis_size("space")
    core = lax.rem(space, NC)
    y = lax.rem(lax.div(space, NC), NY)
    z_hi = lax.rem(lax.div(space, NC * NY), NH)
    x = lax.div(space, NC * NY * NH)
    up = lax.rem(space + 1, planes)
    down = lax.rem(space + planes - 1, planes)

    def at(x, z_hi, y, core):
        return ((x * NH + z_hi) * NY + y) * NC + core

    def flip(z_hi, lane):
        return lane + z_hi * (NB - 1 - 2 * lane)

    def half_of(space):
        return lax.rem(lax.div(space, NC * NY), NH)

    chunk = flip(z_hi, lane)
    up_lane = flip(half_of(up), chunk)
    down_lane = flip(half_of(down), chunk)
    sibling = at(x, z_hi, y, 1 - core)

    def lanes_of(chunk):
        return pl.ds(pl.multiple_of(chunk * CHUNK, CHUNK), CHUNK)

    def rows_of(block):
        return pl.ds(pl.multiple_of(block * VB, VB), VB)

    own_in = pltpu.make_async_copy(vec_hbm.at[0], own, local_sem.at[0])
    links_in = pltpu.make_async_copy(link_hbm.at[0, :, :, :, :, lanes_of(chunk)], links, local_sem.at[1])
    mine_in = pltpu.make_async_copy(
        vec_hbm.at[0, :, :, :, lanes_of(chunk)], held.at[:, :, rows_of(lane), :], local_sem.at[2]
    )
    own_in.start()
    links_in.start()
    mine_in.start()

    def z_peer(j):
        near = (j >= NB).astype(jnp.int32)
        return lax.rem(z_hi + 1 - near, NH), lax.rem(lane + j + near, NB)

    barrier = pltpu.get_barrier_semaphore()

    def greet(space, lane):
        pl.semaphore_signal(
            barrier, inc=1, device_id={"space": space, "vec": lane}, device_id_type=pl.DeviceIdType.MESH
        )

    crossing = jnp.logical_and(y == 0, core == 0)
    crossed = jnp.logical_and(y == NY - 1, core == NC - 1)
    relays = jnp.logical_and(y > 0, core == 0)
    beyond = lax.rem(at(x, z_hi, 0, 0) + planes - 1, planes)
    beyond_lane = flip(half_of(beyond), chunk)

    lower_half = z_hi == 0

    def greet_near(j, carry):
        greet(space, lax.rem(lane + j, NB))
        return carry

    def greet_far():
        def greet_z(j, carry):
            greet(at(x, 1 - z_hi, y, core), j)
            return carry

        lax.fori_loop(0, NB, greet_z, 0)

        @pl.when(crossing)
        def _():
            greet(down, down_lane)

        @pl.when(crossed)
        def _():
            for q in range(NY):
                greet(up + q * NC, up_lane)

        @pl.when(relays)
        def _():
            greet(beyond, beyond_lane)

    lax.fori_loop(1, NB, greet_near, 0)

    @pl.when(jnp.logical_not(crossed))
    def _():
        greet(up, up_lane)

    @pl.when(jnp.logical_not(crossing))
    def _():
        greet(down, down_lane)

    for i in range(1, NX * NY):
        greet(at(lax.rem(x + i % NX, NX), z_hi, lax.rem(y + i // NX, NY), core), lane)

    def one(flag):
        return flag.astype(jnp.int32)

    near_count = NB - 1 + NX * NY - 1 + 2 - one(crossed) - one(crossing)
    far_count = NB + one(crossing) + one(relays) + NY * one(crossed)

    @pl.when(lower_half)
    def _():
        pl.semaphore_wait(barrier, near_count)
        greet_far()

    @pl.when(jnp.logical_not(lower_half))
    def _():
        pl.semaphore_wait(barrier, near_count + far_count)

    def step_of(n):
        if isinstance(n, int):
            return (NB // 2 + (2 * (n % 2) - 1) * (n // 2)) if n else 0
        return (n > 0).astype(jnp.int32) * (NB // 2 + (2 * lax.rem(n, 2) - 1) * lax.div(n, 2))

    def block_of(lane, n):
        return lax.rem(lane + NB - step_of(n), NB)

    def piece(j):
        to = lax.rem(lane + j, NB)
        return send(
            vec_hbm.at[0, :, :, :, lanes_of(flip(z_hi, to))],
            held.at[:, :, rows_of(lane), :],
            vec_send.at[j - 1],
            vec_recv.at[j - 1],
            vec=to,
        )

    def edge_piece(j):
        to = lax.rem(lane + j, NB)
        return send(edges.at[flip(z_hi, to)], edge.at[lane], edge_send.at[j - 1], edge_recv.at[j - 1], vec=to)

    def from_lane(j):
        block = lax.rem(lane + NB - j, NB)
        return (
            send(held.at[:, :, rows_of(block), :], held.at[:, :, rows_of(block), :], vec_send.at[j - 1], vec_recv.at[j - 1], vec=block),
            send(edges.at[0], edge.at[block], edge_send.at[j - 1], edge_recv.at[j - 1], vec=block),
        )

    for n in range(1, NB):
        piece(step_of(n)).start()

    @pl.when(jnp.logical_not(lower_half))
    def _():
        greet_far()

    place = lax.broadcasted_iota(jnp.int32, (16, CHUNK), 1)
    row = lax.broadcasted_iota(jnp.int32, (NV, NV), 0)
    col = lax.broadcasted_iota(jnp.int32, (NV, NV), 1)
    source = (row % NB) * VB + (row // NB % (NX * NH)) * NY + row // (NB * NX * NH)
    order[...] = (col == source).astype(jnp.float32).astype(jnp.bfloat16)

    def in_order(rows):
        return jnp.dot(order[...], rows, preferred_element_type=jnp.float32).astype(jnp.bfloat16)

    own_in.wait()

    def pack(i, carry):
        to = lax.div(i, 2)
        rows = pl.ds(pl.multiple_of(lax.rem(i, 2) * 16, 16), 16)
        found = jnp.zeros((16, CHUNK), jnp.float32)
        for n in range(6):
            field = own[n // 2, n % 2, rows, lanes_of(lax.rem(to + 1, NB))].astype(jnp.float32)
            found = jnp.where(place // LZ == n, pltpu.roll(field, n * LZ, 1) if n else field, found)
        edges[to, rows, :] = found.astype(jnp.bfloat16)
        return carry

    lax.fori_loop(0, 2 * NB, pack, 0)
    edge[lane] = edges[chunk]
    mine_in.wait()
    links_in.wait()

    def start_edges(n, carry):
        edge_piece(step_of(n)).start()
        return carry

    lax.fori_loop(1, NB, start_edges, 0)

    @pl.when(lower_half)
    def _():
        pl.semaphore_wait(barrier, far_count)

    def halo(block):
        rows = rows_of(block)
        return pltpu.make_async_remote_copy(
            src_ref=held.at[:, :, rows, :],
            dst_ref=above.at[:, :, rows, :],
            send_sem=halo_send.at[block],
            recv_sem=halo_recv.at[block],
            device_id={"space": down, "vec": down_lane},
            device_id_type=pl.DeviceIdType.MESH,
        )

    def to_relay(n, block):
        slot = lax.div(n, NY)
        return send(
            held.at[:, :, rows_of(block), :],
            hold.at[slot],
            halo_send.at[block],
            hold_recv.at[slot],
            space=at(x, z_hi, lax.rem(n + 1, NY), core),
        )

    def start_halo(n, block):
        aside = jnp.logical_and(crossing, lax.rem(n + 1, NY) != 0)

        @pl.when(aside)
        def _():
            to_relay(n, block).start()

        @pl.when(jnp.logical_not(aside))
        def _():
            halo(block).start()

    def handed(slot):
        block = block_of(lane, y - 1 + slot * NY)
        return pltpu.make_async_remote_copy(
            src_ref=hold.at[slot],
            dst_ref=above.at[:, :, rows_of(block), :],
            send_sem=hold_send.at[slot],
            recv_sem=halo_recv.at[block],
            device_id={"space": beyond, "vec": beyond_lane},
            device_id_type=pl.DeviceIdType.MESH,
        )

    def hand_on(n):
        send(hold.at[n], hold.at[n], hold_send.at[n], hold_recv.at[n], space=sibling).wait_recv()
        handed(n).start()

    def forward(mu, rows, vecs):
        for row in range(3):
            real = []
            imag = []
            for col in range(3):
                link_re = links[mu, row, col, pl.ds(0, 1), :]
                link_im = links[mu, row, col, pl.ds(1, 1), :]
                vec_re, vec_im = vecs[col]
                real.append(link_re * vec_re - link_im * vec_im)
                imag.append(link_re * vec_im + link_im * vec_re)
            moved[mu, row, 0, rows, :] = (real[0] + real[1] + real[2]).astype(jnp.bfloat16)
            moved[mu, row, 1, rows, :] = (imag[0] + imag[1] + imag[2]).astype(jnp.bfloat16)

    def move_yz(block):
        def step(i, carry):
            first = pl.multiple_of(i * 16, 16)
            rows = pl.ds(pl.multiple_of(block * VB + first, 16), 16)
            vecs = [[held[c, p, rows, :].astype(jnp.float32) for p in range(2)] for c in range(3)]
            border = edge[block, pl.ds(first, 16), :].astype(jnp.float32)
            along_y = [
                [
                    jnp.where(
                        place < CHUNK - LZ,
                        pltpu.roll(vecs[c][p], CHUNK - LZ, 1),
                        pltpu.roll(border, CHUNK - LZ - LZ * (2 * c + p), 1),
                    )
                    for p in range(2)
                ]
                for c in range(3)
            ]
            forward(1, rows, along_y)
            along_z = [
                [
                    jnp.where(place % LZ == LZ - 1, pltpu.roll(v, LZ - 1, 1), pltpu.roll(v, CHUNK - 1, 1))
                    for v in vecs[c]
                ]
                for c in range(3)
            ]
            forward(2, rows, along_z)
            return carry

        lax.fori_loop(0, 2, step, 0)

    def move_x(block):
        def step(i, carry):
            rows = pl.ds(pl.multiple_of(block * VB + i * 16, 16), 16)
            forward(0, rows, [[above[c, p, rows, :].astype(jnp.float32) for p in range(2)] for c in range(3)])
            return carry

        lax.fori_loop(0, 2, step, 0)

    start_halo(0, lane)
    move_yz(lane)

    def arrive(n, carry):
        for copy in from_lane(step_of(n)):
            copy.wait_recv()
        block = block_of(lane, n)
        start_halo(n, block)
        move_yz(block)

        @pl.when(jnp.logical_and(jnp.logical_and(relays, n > 1), lax.rem(n + NY - 1, NY) == y))
        def _():
            hand_on(lax.div(n - 2, NY))

        return carry

    lax.fori_loop(1, NB, arrive, 0)

    @pl.when(jnp.logical_and(relays, y == NY - 1))
    def _():
        hand_on(1)


    tile = (NV, 128)
    row_a = lax.broadcasted_iota(jnp.int32, tile, 0) % NB
    slot = lax.broadcasted_iota(jnp.int32, tile, 1) // VB
    low_tile = (row_a - slot + NB) % NB < NB // 2

    first_half = lax.broadcasted_iota(jnp.int32, tile, 1) % VB < VB // 2

    def lay(which, b, real, imag):
        halves = (
            jnp.where(first_half, real, pltpu.roll(imag, VB // 2, 1)),
            jnp.where(first_half, pltpu.roll(real, 128 - VB // 2, 1), imag),
        )
        for h in range(NC):
            parts[which, h, :, :, b] = halves[h].reshape(NY, NX, 16, 128)

    def product(mu, which, b):
        moved_mu = [jnp.concatenate([moved[mu, c, p] for c in range(3)], axis=1) for p in range(2)]
        held_all = [jnp.concatenate([held[c, p] for c in range(3)], axis=1) for p in range(2)]
        left = [jnp.concatenate([in_order(moved_mu[p]), ordered[p]], axis=1) for p in range(2)]
        right = [jnp.concatenate([held_all[p], moved_mu[p]], axis=1) for p in range(2)]

        def dot(p, q):
            return lax.dot_general(
                left[p], right[q], (((1,), (1,)), ((), ())), preferred_element_type=jnp.float32
            )

        near = []
        for t, total in enumerate((dot(0, 0) + dot(1, 1), dot(0, 1) - dot(1, 0))):
            low, high = total[:, :128], total[:, 128:]
            near.append(jnp.where(low_tile, low, high))
            rest = jnp.where(low_tile, high, low)
            if mu == 1:
                far[t] = pltpu.roll(rest, VB, 1)
            elif mu == 2:
                far[t] = jnp.where(slot == (row_a + 1) % 4, far[t], pltpu.roll(rest, 2 * VB, 1))
            else:
                far[t] = jnp.where(slot == row_a % 4, rest, far[t])
        lay(which, b, near[0], near[1])
        if mu == 0:
            lay(which, 1, far[0], far[1])

    def swap(which, i):
        yy = lax.rem(y + i, NY)
        return send(
            parts.at[which, 1 - core, yy],
            swapped.at[which, yy],
            swap_send.at[which, yy],
            swap_recv.at[which, yy],
            space=sibling,
        )

    def to_xy(which, i, j):
        yy, xx = lax.rem(y + i, NY), lax.rem(x + j, NX)
        slot = lax.rem(i, NY) * NX + j - 1
        return send(
            parts.at[which, core, yy, xx],
            got_xy.at[which, slot],
            xy_send.at[which, slot],
            xy_recv.at[which, slot],
            space=at(xx, z_hi, yy, core),
        )

    def sum_cores(which):
        def swap_start(i, carry):
            swap(which, i).start()
            return carry

        def swap_add(i):
            yy = lax.rem(y + i, NY)
            swap(which, i).wait_recv()
            parts[which, core, yy] = parts[which, core, yy] + swapped[which, yy]

        def xy_start(i, carry):
            swap_add(i)
            for j in range(NX):
                to_xy(which, i, j).start()
            return carry

        lax.fori_loop(1, NY + 1, swap_start, 0)
        lax.fori_loop(1, NY, xy_start, 0)
        swap_add(NY)
        for j in range(1, NX):
            to_xy(which, 0, j).start()

    def sum_chips(which):
        def xy_add(slot, totals):
            i, j = lax.div(slot + 1, NX), lax.rem(slot + 1, NX)
            to_xy(which, i, j).wait_recv()
            return tuple(totals[b] + got_xy[which, slot, b] for b in range(2))

        own_part = tuple(parts[which, core, y, x, b] for b in range(2))
        totals = lax.fori_loop(0, NX * NY - 1, xy_add, own_part)
        for b in range(2):
            sum_xy[:, 2 * which + b, :] = totals[b]

    for p in range(2):
        ordered[p] = in_order(jnp.concatenate([held[c, p] for c in range(3)], axis=1))
    product(1, 0, 0)
    product(2, 0, 1)
    sum_cores(0)

    def arrive_x(n, carry):
        block = block_of(up_lane, n)
        halo(block).wait_recv()
        move_x(block)
        return carry

    lax.fori_loop(0, NB, arrive_x, 0)
    product(0, 1, 0)
    sum_cores(1)
    sum_chips(0)
    sum_chips(1)

    def to_z(j):
        there, peer = z_peer(j)
        return pltpu.make_async_remote_copy(
            src_ref=sum_xy.at[there * NB + peer],
            dst_ref=got_z.at[j],
            send_sem=z_send.at[j],
            recv_sem=z_recv.at[j],
            device_id={"space": at(x, there, y, core), "vec": peer},
            device_id_type=pl.DeviceIdType.MESH,
        )

    def z_start(j, carry):
        to_z(j).start()
        return carry

    def z_add(j, total):
        to_z(j).wait_recv()
        return total + got_z[j]

    lax.fori_loop(0, NH * NB - 1, z_start, 0)

    def drain(n, carry):
        piece(n).wait_send()
        edge_piece(n).wait_send()
        return carry

    def drain_halo(block, carry):
        halo(block).wait_send()
        return carry

    @pl.when(relays)
    def _():
        for n in range(2):
            handed(n).wait_send()

    lax.fori_loop(1, NB, drain, 0)
    lax.fori_loop(0, NB, drain_halo, 0)
    for which in range(2):

        def drain_swap(i, carry):
            swap(which, i).wait_send()
            return carry

        def drain_xy(slot, carry):
            to_xy(which, lax.div(slot + 1, NX), lax.rem(slot + 1, NX)).wait_send()
            return carry

        lax.fori_loop(1, NY + 1, drain_swap, 0)
        lax.fori_loop(0, NX * NY - 1, drain_xy, 0)

    total = lax.fori_loop(0, NH * NB - 1, z_add, sum_xy[z_hi * NB + lane]) * scale
    total = pltpu.roll(total, (4 - lane % 4) % 4 * VB, 1)

    half = VB // 2
    for t in range(2):
        for mu in range(3):
            for k in range(NK):
                row, slot_k = ((mu + 2) % 3, (4 - k) % 4) if k < 4 else (3, mu)
                first = slot_k * VB + t * half
                at_row = (mu * NK + k) * 2 + t
                picked[at_row : at_row + 1, :half] = total[row : row + 1, first : first + half]
    for d in range(3):
        mu = directions[d]
        for q in range(NK):
            rows = pl.ds((mu * NK + offsets[q]) * 2, 2)
            out[d, q, :, 0, :] = picked[rows, :half]

    def drain_z(j, carry):
        to_z(j).wait_send()
        return carry

    lax.fori_loop(0, NH * NB - 1, drain_z, 0)


def body(vectors, links, directions, offsets):
    planes = lax.axis_size("space")
    scale = 1.0 / math.sqrt(6.0 * planes * SITES)
    bf16, f32 = jnp.bfloat16, jnp.float32
    dma = pltpu.SemaphoreType.DMA
    zs = NH * NB - 1
    return pl.pallas_call(
        functools.partial(kernel, scale=scale),
        out_shape=jax.ShapeDtypeStruct((3, NK, 2, 1, VB // 2), f32),
        in_specs=[
            pl.BlockSpec(memory_space=pl.ANY),
            pl.BlockSpec(memory_space=pl.ANY),
            pl.BlockSpec(memory_space=pltpu.SMEM),
            pl.BlockSpec(memory_space=pltpu.SMEM),
        ],
        out_specs=pl.BlockSpec(memory_space=pltpu.VMEM),
        scratch_shapes=[
            pltpu.VMEM((3, 2, VB, SITES), bf16),
            pltpu.VMEM((3, 2, NV, CHUNK), bf16),
            pltpu.VMEM((3, 2, NV, CHUNK), bf16),
            pltpu.VMEM((2, 3, 2, VB, CHUNK), bf16),
            pltpu.VMEM((NB, VB, CHUNK), bf16),
            pltpu.VMEM((NB, VB, CHUNK), bf16),
            pltpu.VMEM((3, 3, 3, 2, CHUNK), f32),
            pltpu.VMEM((3, 3, 2, NV, CHUNK), bf16),
            pltpu.VMEM((NV, NV), bf16),
            pltpu.VMEM((2, NV, 3 * CHUNK), bf16),
            pltpu.VMEM((2, NV, 128), f32),
            pltpu.VMEM((2, 2, NY, NX, 2, 16, 128), f32),
            pltpu.VMEM((2, NY, NX, 2, 16, 128), f32),
            pltpu.VMEM((2, NX * NY - 1, 2, 16, 128), f32),
            pltpu.VMEM((16, 4, 128), f32),
            pltpu.VMEM((zs, 4, 128), f32),
            pltpu.VMEM((6 * NK + 2, 128), f32),
            dma((3,)),
            dma((NB - 1,)),
            dma((NB - 1,)),
            dma((NB - 1,)),
            dma((NB - 1,)),
            dma((NB,)),
            dma((NB,)),
            dma((2,)),
            dma((2,)),
            dma((2, NY)),
            dma((2, NY)),
            dma((2, NX * NY - 1)),
            dma((2, NX * NY - 1)),
            dma((zs,)),
            dma((zs,)),
        ],
        compiler_params=pltpu.CompilerParams(
            collective_id=0, has_side_effects=True, vmem_limit_bytes=63 * 1024 * 1024
        ),
        name="elementals",
    )(vectors, links, directions, offsets)


def solution(mesh):
    placed = (
        P("space", None, None, "vec", None),
        P("space", None, None, None, None, None),
        P(),
        P(),
    )
    return jax.shard_map(
        body,
        mesh=mesh,
        in_specs=placed,
        out_specs=P(None, None, None, "vec", "space"),
        check_vma=False,
    )
```

```python
import functools
import math

import jax
import jax.numpy as jnp
from jax import lax
from jax.experimental import pallas as pl
from jax.experimental.pallas import tpu as pltpu
from jax.sharding import PartitionSpec as P

LZ = 16
SITES = 1024
VB = 32
NV = 256
NB = NV // VB
NK = 5
CHUNK = SITES // NB
NX, NH, NY, NC = 4, 2, 4, 2
ROWS = NX * NH * NY


def send(src, dst, send_sem, recv_sem, **where):
    return pltpu.make_async_remote_copy(
        src_ref=src,
        dst_ref=dst,
        send_sem=send_sem,
        recv_sem=recv_sem,
        device_id=where,
        device_id_type=pl.DeviceIdType.MESH,
    )


def kernel(
    vec_hbm,
    link_hbm,
    directions,
    offsets,
    out,
    own,
    held,
    above,
    hold,
    edges,
    edge,
    links,
    moved,
    order,
    ordered,
    far,
    parts,
    swapped,
    got_xy,
    sum_xy,
    got_z,
    picked,
    local_sem,
    own_sem,
    vec_send,
    vec_recv,
    edge_send,
    edge_recv,
    halo_send,
    halo_recv,
    hold_send,
    hold_recv,
    swap_send,
    swap_recv,
    xy_send,
    xy_recv,
    z_send,
    z_recv,
    *,
    scale,
):
    space = lax.axis_index("space")
    lane = lax.axis_index("vec")
    planes = lax.axis_size("space")
    core = lax.rem(space, NC)
    y = lax.rem(lax.div(space, NC), NY)
    z_hi = lax.rem(lax.div(space, NC * NY), NH)
    x = lax.div(space, NC * NY * NH)
    up = lax.rem(space + 1, planes)
    down = lax.rem(space + planes - 1, planes)

    def at(x, z_hi, y, core):
        return ((x * NH + z_hi) * NY + y) * NC + core

    def flip(z_hi, lane):
        return lane + z_hi * (NB - 1 - 2 * lane)

    def half_of(space):
        return lax.rem(lax.div(space, NC * NY), NH)

    chunk = flip(z_hi, lane)
    up_lane = flip(half_of(up), chunk)
    down_lane = flip(half_of(down), chunk)
    sibling = at(x, z_hi, y, 1 - core)

    def lanes_of(chunk):
        return pl.ds(pl.multiple_of(chunk * CHUNK, CHUNK), CHUNK)

    own_in = [
        pltpu.make_async_copy(vec_hbm.at[0, :, :, :, pl.ds(c * CHUNK, CHUNK)], own.at[c], own_sem.at[c])
        for c in range(NB)
    ]
    links_in = pltpu.make_async_copy(link_hbm.at[0, :, :, :, :, lanes_of(chunk)], links, local_sem.at[1])
    mine_in = pltpu.make_async_copy(
        vec_hbm.at[0, :, :, :, lanes_of(chunk)], held.at[lane], local_sem.at[0]
    )
    for copy in own_in:
        copy.start()
    links_in.start()
    mine_in.start()

    def z_peer(j):
        near = (j >= NB).astype(jnp.int32)
        return lax.rem(z_hi + 1 - near, NH), lax.rem(lane + j + near, NB)

    barrier = pltpu.get_barrier_semaphore()

    def greet(space, lane):
        pl.semaphore_signal(
            barrier, inc=1, device_id={"space": space, "vec": lane}, device_id_type=pl.DeviceIdType.MESH
        )

    crossing = jnp.logical_and(y == 0, core == 0)
    crossed = jnp.logical_and(y == NY - 1, core == NC - 1)
    relays = jnp.logical_and(y > 0, core == 0)
    beyond = lax.rem(at(x, z_hi, 0, 0) + planes - 1, planes)
    beyond_lane = flip(half_of(beyond), chunk)

    lower_half = z_hi == 0

    def greet_near(j, carry):
        greet(space, lax.rem(lane + j, NB))
        return carry

    def greet_far():
        def greet_z(j, carry):
            greet(at(x, 1 - z_hi, y, core), j)
            return carry

        lax.fori_loop(0, NB, greet_z, 0)

        @pl.when(crossing)
        def _():
            greet(down, down_lane)

        @pl.when(crossed)
        def _():
            for q in range(NY):
                greet(up + q * NC, up_lane)

        @pl.when(relays)
        def _():
            greet(beyond, beyond_lane)

    lax.fori_loop(1, NB, greet_near, 0)

    @pl.when(jnp.logical_not(crossed))
    def _():
        greet(up, up_lane)

    @pl.when(jnp.logical_not(crossing))
    def _():
        greet(down, down_lane)

    for i in range(1, NX * NY):
        greet(at(lax.rem(x + i % NX, NX), z_hi, lax.rem(y + i // NX, NY), core), lane)

    def one(flag):
        return flag.astype(jnp.int32)

    near_count = NB - 1 + NX * NY - 1 + 2 - one(crossed) - one(crossing)
    far_count = NB + one(crossing) + one(relays) + NY * one(crossed)

    for copy in own_in:
        copy.wait()

    place = lax.broadcasted_iota(jnp.int32, (16, CHUNK), 1)
    row = lax.broadcasted_iota(jnp.int32, (NV, NV), 0)
    col = lax.broadcasted_iota(jnp.int32, (NV, NV), 1)
    source = (row % NB) * VB + (row // NB % (NX * NH)) * NY + row // (NB * NX * NH)
    order[...] = (col == source).astype(jnp.float32).astype(jnp.bfloat16)

    def in_order(rows):
        return jnp.dot(order[...], rows, preferred_element_type=jnp.float32).astype(jnp.bfloat16)


    def pack(i, carry):
        to = lax.div(i, 2)
        rows = pl.ds(pl.multiple_of(lax.rem(i, 2) * 16, 16), 16)
        found = jnp.zeros((16, CHUNK), jnp.float32)
        for n in range(6):
            field = own[lax.rem(to + 1, NB), n // 2, n % 2, rows, :].astype(jnp.float32)
            found = jnp.where(place // LZ == n, pltpu.roll(field, n * LZ, 1) if n else field, found)
        edges[to, rows, :] = found.astype(jnp.bfloat16)
        return carry

    lax.fori_loop(0, 2 * NB, pack, 0)
    @pl.when(lower_half)
    def _():
        pl.semaphore_wait(barrier, near_count)
        greet_far()

    @pl.when(jnp.logical_not(lower_half))
    def _():
        pl.semaphore_wait(barrier, near_count + far_count)

    def step_of(n):
        if isinstance(n, int):
            return (NB // 2 + (2 * (n % 2) - 1) * (n // 2)) if n else 0
        return (n > 0).astype(jnp.int32) * (NB // 2 + (2 * lax.rem(n, 2) - 1) * lax.div(n, 2))

    def block_of(lane, n):
        return lax.rem(lane + NB - step_of(n), NB)

    def piece(j):
        to = lax.rem(lane + j, NB)
        return send(
            own.at[flip(z_hi, to)],
            held.at[lane],
            vec_send.at[j - 1],
            vec_recv.at[j - 1],
            vec=to,
        )

    def edge_piece(j):
        to = lax.rem(lane + j, NB)
        return send(edges.at[flip(z_hi, to)], edge.at[lane], edge_send.at[j - 1], edge_recv.at[j - 1], vec=to)

    def from_lane(j):
        block = lax.rem(lane + NB - j, NB)
        return (
            send(held.at[block], held.at[block], vec_send.at[j - 1], vec_recv.at[j - 1], vec=block),
            send(edges.at[0], edge.at[block], edge_send.at[j - 1], edge_recv.at[j - 1], vec=block),
        )

    for n in range(1, NB):
        piece(step_of(n)).start()

    @pl.when(jnp.logical_not(lower_half))
    def _():
        greet_far()

    edge[lane] = edges[chunk]
    mine_in.wait()
    links_in.wait()

    def start_edges(n, carry):
        edge_piece(step_of(n)).start()
        return carry

    lax.fori_loop(1, NB, start_edges, 0)

    @pl.when(lower_half)
    def _():
        pl.semaphore_wait(barrier, far_count)

    def halo(block):
        return pltpu.make_async_remote_copy(
            src_ref=held.at[block],
            dst_ref=above.at[block],
            send_sem=halo_send.at[block],
            recv_sem=halo_recv.at[block],
            device_id={"space": down, "vec": down_lane},
            device_id_type=pl.DeviceIdType.MESH,
        )

    def to_relay(n, block):
        slot = lax.div(n, NY)
        return send(
            held.at[block],
            hold.at[slot],
            halo_send.at[block],
            hold_recv.at[slot],
            space=at(x, z_hi, lax.rem(n + 1, NY), core),
        )

    def start_halo(n, block):
        aside = jnp.logical_and(crossing, lax.rem(n + 1, NY) != 0)

        @pl.when(aside)
        def _():
            to_relay(n, block).start()

        @pl.when(jnp.logical_not(aside))
        def _():
            halo(block).start()

    def handed(slot):
        block = block_of(lane, y - 1 + slot * NY)
        return pltpu.make_async_remote_copy(
            src_ref=hold.at[slot],
            dst_ref=above.at[block],
            send_sem=hold_send.at[slot],
            recv_sem=halo_recv.at[block],
            device_id={"space": beyond, "vec": beyond_lane},
            device_id_type=pl.DeviceIdType.MESH,
        )

    def hand_on(n):
        send(hold.at[n], hold.at[n], hold_send.at[n], hold_recv.at[n], space=sibling).wait_recv()
        handed(n).start()

    def forward(mu, rows, vecs):
        for row in range(3):
            real = []
            imag = []
            for col in range(3):
                link_re = links[mu, row, col, pl.ds(0, 1), :]
                link_im = links[mu, row, col, pl.ds(1, 1), :]
                vec_re, vec_im = vecs[col]
                real.append(link_re * vec_re - link_im * vec_im)
                imag.append(link_re * vec_im + link_im * vec_re)
            moved[mu, row, 0, rows, :] = (real[0] + real[1] + real[2]).astype(jnp.bfloat16)
            moved[mu, row, 1, rows, :] = (imag[0] + imag[1] + imag[2]).astype(jnp.bfloat16)

    def move_yz(block):
        def step(i, carry):
            first = pl.multiple_of(i * 16, 16)
            rows = pl.ds(pl.multiple_of(block * VB + first, 16), 16)
            vecs = [[held[block, c, p, pl.ds(first, 16), :].astype(jnp.float32) for p in range(2)] for c in range(3)]
            border = edge[block, pl.ds(first, 16), :].astype(jnp.float32)
            along_y = [
                [
                    jnp.where(
                        place < CHUNK - LZ,
                        pltpu.roll(vecs[c][p], CHUNK - LZ, 1),
                        pltpu.roll(border, CHUNK - LZ - LZ * (2 * c + p), 1),
                    )
                    for p in range(2)
                ]
                for c in range(3)
            ]
            forward(1, rows, along_y)
            along_z = [
                [
                    jnp.where(place % LZ == LZ - 1, pltpu.roll(v, LZ - 1, 1), pltpu.roll(v, CHUNK - 1, 1))
                    for v in vecs[c]
                ]
                for c in range(3)
            ]
            forward(2, rows, along_z)
            return carry

        lax.fori_loop(0, 2, step, 0)

    def move_x(block):
        def step(i, carry):
            rows = pl.ds(pl.multiple_of(block * VB + i * 16, 16), 16)
            half = pl.ds(pl.multiple_of(i * 16, 16), 16)
            forward(0, rows, [[above[block, c, p, half, :].astype(jnp.float32) for p in range(2)] for c in range(3)])
            return carry

        lax.fori_loop(0, 2, step, 0)

    start_halo(0, lane)

    def arrive(n, carry):
        from_lane(step_of(n))[0].wait_recv()
        start_halo(n, block_of(lane, n))

        @pl.when(jnp.logical_and(jnp.logical_and(relays, n > 1), lax.rem(n + NY - 1, NY) == y))
        def _():
            hand_on(lax.div(n - 2, NY))

        return carry

    lax.fori_loop(1, NB, arrive, 0)

    @pl.when(jnp.logical_and(relays, y == NY - 1))
    def _():
        hand_on(1)

    def move(n, carry):
        from_lane(step_of(n))[1].wait_recv()
        move_yz(block_of(lane, n))
        return carry

    move_yz(lane)
    lax.fori_loop(1, NB, move, 0)


    tile = (NV, 128)
    row_a = lax.broadcasted_iota(jnp.int32, tile, 0) % NB
    slot = lax.broadcasted_iota(jnp.int32, tile, 1) // VB
    low_tile = (row_a - slot + NB) % NB < NB // 2

    first_half = lax.broadcasted_iota(jnp.int32, tile, 1) % VB < VB // 2

    def lay(which, b, real, imag):
        halves = (
            jnp.where(first_half, real, pltpu.roll(imag, VB // 2, 1)),
            jnp.where(first_half, pltpu.roll(real, 128 - VB // 2, 1), imag),
        )
        for h in range(NC):
            parts[which, h, :, :, b] = halves[h].reshape(NY, NX, 16, 128)

    def product(mu, which, b):
        moved_mu = [jnp.concatenate([moved[mu, c, p] for c in range(3)], axis=1) for p in range(2)]
        held_all = [jnp.concatenate([held[:, c, p].reshape(NV, CHUNK) for c in range(3)], axis=1) for p in range(2)]
        left = [jnp.concatenate([in_order(moved_mu[p]), ordered[p]], axis=1) for p in range(2)]
        right = [jnp.concatenate([held_all[p], moved_mu[p]], axis=1) for p in range(2)]

        def dot(p, q):
            return lax.dot_general(
                left[p], right[q], (((1,), (1,)), ((), ())), preferred_element_type=jnp.float32
            )

        near = []
        for t, total in enumerate((dot(0, 0) + dot(1, 1), dot(0, 1) - dot(1, 0))):
            low, high = total[:, :128], total[:, 128:]
            near.append(jnp.where(low_tile, low, high))
            rest = jnp.where(low_tile, high, low)
            if mu == 1:
                far[t] = pltpu.roll(rest, VB, 1)
            elif mu == 2:
                far[t] = jnp.where(slot == (row_a + 1) % 4, far[t], pltpu.roll(rest, 2 * VB, 1))
            else:
                far[t] = jnp.where(slot == row_a % 4, rest, far[t])
        lay(which, b, near[0], near[1])
        if mu == 0:
            lay(which, 1, far[0], far[1])

    def swap(which, i):
        yy = lax.rem(y + i, NY)
        return send(
            parts.at[which, 1 - core, yy],
            swapped.at[which, yy],
            swap_send.at[which, yy],
            swap_recv.at[which, yy],
            space=sibling,
        )

    def to_xy(which, i, j):
        yy, xx = lax.rem(y + i, NY), lax.rem(x + j, NX)
        slot = lax.rem(i, NY) * NX + j - 1
        return send(
            parts.at[which, core, yy, xx],
            got_xy.at[which, slot],
            xy_send.at[which, slot],
            xy_recv.at[which, slot],
            space=at(xx, z_hi, yy, core),
        )

    def sum_cores(which):
        def swap_start(i, carry):
            swap(which, i).start()
            return carry

        def swap_add(i):
            yy = lax.rem(y + i, NY)
            swap(which, i).wait_recv()
            parts[which, core, yy] = parts[which, core, yy] + swapped[which, yy]

        def xy_start(i, carry):
            swap_add(i)
            for j in range(NX):
                to_xy(which, i, j).start()
            return carry

        lax.fori_loop(1, NY + 1, swap_start, 0)
        lax.fori_loop(1, NY, xy_start, 0)
        swap_add(NY)
        for j in range(1, NX):
            to_xy(which, 0, j).start()

    def sum_chips(which):
        def xy_add(slot, totals):
            i, j = lax.div(slot + 1, NX), lax.rem(slot + 1, NX)
            to_xy(which, i, j).wait_recv()
            return tuple(totals[b] + got_xy[which, slot, b] for b in range(2))

        own_part = tuple(parts[which, core, y, x, b] for b in range(2))
        totals = lax.fori_loop(0, NX * NY - 1, xy_add, own_part)
        for b in range(2):
            sum_xy[:, 2 * which + b, :] = totals[b]

    for p in range(2):
        ordered[p] = in_order(jnp.concatenate([held[:, c, p].reshape(NV, CHUNK) for c in range(3)], axis=1))
    product(1, 0, 0)
    product(2, 0, 1)
    sum_cores(0)

    def arrive_x(n, carry):
        block = block_of(up_lane, n)
        halo(block).wait_recv()
        move_x(block)
        return carry

    lax.fori_loop(0, NB, arrive_x, 0)
    product(0, 1, 0)
    sum_cores(1)
    sum_chips(0)
    sum_chips(1)

    def to_z(j):
        there, peer = z_peer(j)
        return pltpu.make_async_remote_copy(
            src_ref=sum_xy.at[there * NB + peer],
            dst_ref=got_z.at[j],
            send_sem=z_send.at[j],
            recv_sem=z_recv.at[j],
            device_id={"space": at(x, there, y, core), "vec": peer},
            device_id_type=pl.DeviceIdType.MESH,
        )

    def z_start(j, carry):
        to_z(j).start()
        return carry

    def z_add(j, total):
        to_z(j).wait_recv()
        return total + got_z[j]

    lax.fori_loop(0, NH * NB - 1, z_start, 0)

    def drain(n, carry):
        piece(n).wait_send()
        edge_piece(n).wait_send()
        return carry

    def drain_halo(block, carry):
        halo(block).wait_send()
        return carry

    @pl.when(relays)
    def _():
        for n in range(2):
            handed(n).wait_send()

    lax.fori_loop(1, NB, drain, 0)
    lax.fori_loop(0, NB, drain_halo, 0)
    for which in range(2):

        def drain_swap(i, carry):
            swap(which, i).wait_send()
            return carry

        def drain_xy(slot, carry):
            to_xy(which, lax.div(slot + 1, NX), lax.rem(slot + 1, NX)).wait_send()
            return carry

        lax.fori_loop(1, NY + 1, drain_swap, 0)
        lax.fori_loop(0, NX * NY - 1, drain_xy, 0)

    total = lax.fori_loop(0, NH * NB - 1, z_add, sum_xy[z_hi * NB + lane]) * scale
    total = pltpu.roll(total, (4 - lane % 4) % 4 * VB, 1)

    half = VB // 2
    for t in range(2):
        for mu in range(3):
            for k in range(NK):
                row, slot_k = ((mu + 2) % 3, (4 - k) % 4) if k < 4 else (3, mu)
                first = slot_k * VB + t * half
                at_row = (mu * NK + k) * 2 + t
                picked[at_row : at_row + 1, :half] = total[row : row + 1, first : first + half]
    for d in range(3):
        mu = directions[d]
        for q in range(NK):
            rows = pl.ds((mu * NK + offsets[q]) * 2, 2)
            out[d, q, :, 0, :] = picked[rows, :half]

    def drain_z(j, carry):
        to_z(j).wait_send()
        return carry

    lax.fori_loop(0, NH * NB - 1, drain_z, 0)


def body(vectors, links, directions, offsets):
    planes = lax.axis_size("space")
    scale = 1.0 / math.sqrt(6.0 * planes * SITES)
    bf16, f32 = jnp.bfloat16, jnp.float32
    dma = pltpu.SemaphoreType.DMA
    zs = NH * NB - 1
    return pl.pallas_call(
        functools.partial(kernel, scale=scale),
        out_shape=jax.ShapeDtypeStruct((3, NK, 2, 1, VB // 2), f32),
        in_specs=[
            pl.BlockSpec(memory_space=pl.ANY),
            pl.BlockSpec(memory_space=pl.ANY),
            pl.BlockSpec(memory_space=pltpu.SMEM),
            pl.BlockSpec(memory_space=pltpu.SMEM),
        ],
        out_specs=pl.BlockSpec(memory_space=pltpu.VMEM),
        scratch_shapes=[
            pltpu.VMEM((NB, 3, 2, VB, CHUNK), bf16),
            pltpu.VMEM((NB, 3, 2, VB, CHUNK), bf16),
            pltpu.VMEM((NB, 3, 2, VB, CHUNK), bf16),
            pltpu.VMEM((2, 3, 2, VB, CHUNK), bf16),
            pltpu.VMEM((NB, VB, CHUNK), bf16),
            pltpu.VMEM((NB, VB, CHUNK), bf16),
            pltpu.VMEM((3, 3, 3, 2, CHUNK), f32),
            pltpu.VMEM((3, 3, 2, NV, CHUNK), bf16),
            pltpu.VMEM((NV, NV), bf16),
            pltpu.VMEM((2, NV, 3 * CHUNK), bf16),
            pltpu.VMEM((2, NV, 128), f32),
            pltpu.VMEM((2, 2, NY, NX, 2, 16, 128), f32),
            pltpu.VMEM((2, NY, NX, 2, 16, 128), f32),
            pltpu.VMEM((2, NX * NY - 1, 2, 16, 128), f32),
            pltpu.VMEM((16, 4, 128), f32),
            pltpu.VMEM((zs, 4, 128), f32),
            pltpu.VMEM((6 * NK + 2, 128), f32),
            dma((2,)),
            dma((NB,)),
            dma((NB - 1,)),
            dma((NB - 1,)),
            dma((NB - 1,)),
            dma((NB - 1,)),
            dma((NB,)),
            dma((NB,)),
            dma((2,)),
            dma((2,)),
            dma((2, NY)),
            dma((2, NY)),
            dma((2, NX * NY - 1)),
            dma((2, NX * NY - 1)),
            dma((zs,)),
            dma((zs,)),
        ],
        compiler_params=pltpu.CompilerParams(
            collective_id=0, has_side_effects=True, vmem_limit_bytes=63 * 1024 * 1024
        ),
        name="elementals",
    )(vectors, links, directions, offsets)


def solution(mesh):
    placed = (
        P("space", None, None, "vec", None),
        P("space", None, None, None, None, None),
        P(),
        P(),
    )
    return jax.shard_map(
        body,
        mesh=mesh,
        in_specs=placed,
        out_specs=P(None, None, None, "vec", "space"),
        check_vma=False,
    )
```

```python
import functools
import math

import jax
import jax.numpy as jnp
from jax import lax
from jax.experimental import pallas as pl
from jax.experimental.pallas import tpu as pltpu
from jax.sharding import PartitionSpec as P

LZ = 16
SITES = 1024
VB = 32
NV = 256
NB = NV // VB
NK = 5
CHUNK = SITES // NB
NX, NH, NY, NC = 4, 2, 4, 2
ROWS = NX * NH * NY


def send(src, dst, send_sem, recv_sem, **where):
    return pltpu.make_async_remote_copy(
        src_ref=src,
        dst_ref=dst,
        send_sem=send_sem,
        recv_sem=recv_sem,
        device_id=where,
        device_id_type=pl.DeviceIdType.MESH,
    )


def kernel(
    vec_hbm,
    link_hbm,
    directions,
    offsets,
    out,
    own,
    held,
    above,
    hold,
    edges,
    edge,
    links,
    moved,
    order,
    ordered,
    far,
    parts,
    swapped,
    got_xy,
    sum_xy,
    got_z,
    picked,
    local_sem,
    own_sem,
    vec_send,
    vec_recv,
    edge_send,
    edge_recv,
    halo_send,
    halo_recv,
    hold_send,
    hold_recv,
    swap_send,
    swap_recv,
    xy_send,
    xy_recv,
    z_send,
    z_recv,
    *,
    scale,
):
    space = lax.axis_index("space")
    lane = lax.axis_index("vec")
    planes = lax.axis_size("space")
    core = lax.rem(space, NC)
    y = lax.rem(lax.div(space, NC), NY)
    z_hi = lax.rem(lax.div(space, NC * NY), NH)
    x = lax.div(space, NC * NY * NH)
    up = lax.rem(space + 1, planes)
    down = lax.rem(space + planes - 1, planes)

    def at(x, z_hi, y, core):
        return ((x * NH + z_hi) * NY + y) * NC + core

    def flip(z_hi, lane):
        return lane + z_hi * (NB - 1 - 2 * lane)

    def half_of(space):
        return lax.rem(lax.div(space, NC * NY), NH)

    chunk = flip(z_hi, lane)
    up_lane = flip(half_of(up), chunk)
    down_lane = flip(half_of(down), chunk)
    sibling = at(x, z_hi, y, 1 - core)

    def lanes_of(chunk):
        return pl.ds(pl.multiple_of(chunk * CHUNK, CHUNK), CHUNK)

    own_in = [
        pltpu.make_async_copy(vec_hbm.at[0, :, :, :, pl.ds(c * CHUNK, CHUNK)], own.at[c], own_sem.at[c])
        for c in range(NB)
    ]
    links_in = pltpu.make_async_copy(link_hbm.at[0, :, :, :, :, lanes_of(chunk)], links, local_sem.at[1])
    mine_in = pltpu.make_async_copy(
        vec_hbm.at[0, :, :, :, lanes_of(chunk)], held.at[lane], local_sem.at[0]
    )

    def z_peer(j):
        near = (j >= NB).astype(jnp.int32)
        return lax.rem(z_hi + 1 - near, NH), lax.rem(lane + j + near, NB)

    barrier = pltpu.get_barrier_semaphore()

    def greet(space, lane):
        pl.semaphore_signal(
            barrier, inc=1, device_id={"space": space, "vec": lane}, device_id_type=pl.DeviceIdType.MESH
        )

    crossing = jnp.logical_and(y == 0, core == 0)
    crossed = jnp.logical_and(y == NY - 1, core == NC - 1)
    relays = jnp.logical_and(y > 0, core == 0)
    beyond = lax.rem(at(x, z_hi, 0, 0) + planes - 1, planes)
    beyond_lane = flip(half_of(beyond), chunk)

    lower_half = z_hi == 0

    def greet_near(j, carry):
        greet(space, lax.rem(lane + j, NB))
        return carry

    def greet_far():
        def greet_z(j, carry):
            greet(at(x, 1 - z_hi, y, core), j)
            return carry

        lax.fori_loop(0, NB, greet_z, 0)

        @pl.when(crossing)
        def _():
            greet(down, down_lane)

        @pl.when(crossed)
        def _():
            for q in range(NY):
                greet(up + q * NC, up_lane)

        @pl.when(relays)
        def _():
            greet(beyond, beyond_lane)

    lax.fori_loop(1, NB, greet_near, 0)

    @pl.when(jnp.logical_not(crossed))
    def _():
        greet(up, up_lane)

    @pl.when(jnp.logical_not(crossing))
    def _():
        greet(down, down_lane)

    for i in range(1, NX * NY):
        greet(at(lax.rem(x + i % NX, NX), z_hi, lax.rem(y + i // NX, NY), core), lane)

    for copy in own_in:
        copy.start()
    links_in.start()
    mine_in.start()

    def one(flag):
        return flag.astype(jnp.int32)

    near_count = NB - 1 + NX * NY - 1 + 2 - one(crossed) - one(crossing)
    far_count = NB + one(crossing) + one(relays) + NY * one(crossed)

    for copy in own_in:
        copy.wait()

    place = lax.broadcasted_iota(jnp.int32, (16, CHUNK), 1)
    row = lax.broadcasted_iota(jnp.int32, (NV, NV), 0)
    col = lax.broadcasted_iota(jnp.int32, (NV, NV), 1)
    source = (row % NB) * VB + (row // NB % (NX * NH)) * NY + row // (NB * NX * NH)
    order[...] = (col == source).astype(jnp.float32).astype(jnp.bfloat16)

    def in_order(rows):
        return jnp.dot(order[...], rows, preferred_element_type=jnp.float32).astype(jnp.bfloat16)


    def pack(i, carry):
        to = lax.div(i, 2)
        rows = pl.ds(pl.multiple_of(lax.rem(i, 2) * 16, 16), 16)
        found = jnp.zeros((16, CHUNK), jnp.float32)
        for n in range(6):
            field = own[lax.rem(to + 1, NB), n // 2, n % 2, rows, :].astype(jnp.float32)
            found = jnp.where(place // LZ == n, pltpu.roll(field, n * LZ, 1) if n else field, found)
        edges[to, rows, :] = found.astype(jnp.bfloat16)
        return carry

    lax.fori_loop(0, 2 * NB, pack, 0)
    @pl.when(lower_half)
    def _():
        pl.semaphore_wait(barrier, near_count)
        greet_far()

    @pl.when(jnp.logical_not(lower_half))
    def _():
        pl.semaphore_wait(barrier, near_count + far_count)

    def step_of(n):
        if isinstance(n, int):
            return (NB // 2 + (2 * (n % 2) - 1) * (n // 2)) if n else 0
        return (n > 0).astype(jnp.int32) * (NB // 2 + (2 * lax.rem(n, 2) - 1) * lax.div(n, 2))

    def block_of(lane, n):
        return lax.rem(lane + NB - step_of(n), NB)

    def piece(j):
        to = lax.rem(lane + j, NB)
        return send(
            own.at[flip(z_hi, to)],
            held.at[lane],
            vec_send.at[j - 1],
            vec_recv.at[j - 1],
            vec=to,
        )

    def edge_piece(j):
        to = lax.rem(lane + j, NB)
        return send(edges.at[flip(z_hi, to)], edge.at[lane], edge_send.at[j - 1], edge_recv.at[j - 1], vec=to)

    def from_lane(j):
        block = lax.rem(lane + NB - j, NB)
        return (
            send(held.at[block], held.at[block], vec_send.at[j - 1], vec_recv.at[j - 1], vec=block),
            send(edges.at[0], edge.at[block], edge_send.at[j - 1], edge_recv.at[j - 1], vec=block),
        )

    yields = jnp.logical_and(y == 0, core == NC - 1)
    for n in range(1, NB):

        @pl.when(jnp.logical_or(jnp.logical_not(yields), n <= 5))
        def _():
            piece(step_of(n)).start()

    @pl.when(jnp.logical_not(lower_half))
    def _():
        greet_far()

    edge[lane] = edges[chunk]
    mine_in.wait()
    links_in.wait()

    def start_edges(n, carry):
        edge_piece(step_of(n)).start()
        return carry

    lax.fori_loop(1, NB, start_edges, 0)

    @pl.when(lower_half)
    def _():
        pl.semaphore_wait(barrier, far_count)

    def halo(block):
        return pltpu.make_async_remote_copy(
            src_ref=held.at[block],
            dst_ref=above.at[block],
            send_sem=halo_send.at[block],
            recv_sem=halo_recv.at[block],
            device_id={"space": down, "vec": down_lane},
            device_id_type=pl.DeviceIdType.MESH,
        )

    def to_relay(n, block):
        slot = lax.div(n, NY)
        return send(
            held.at[block],
            hold.at[slot],
            halo_send.at[block],
            hold_recv.at[slot],
            space=at(x, z_hi, lax.rem(n + 1, NY), core),
        )

    def start_halo(n, block):
        aside = jnp.logical_and(crossing, lax.rem(n + 1, NY) != 0)

        @pl.when(aside)
        def _():
            to_relay(n, block).start()

        @pl.when(jnp.logical_not(aside))
        def _():
            halo(block).start()

    def handed(slot):
        block = block_of(lane, y - 1 + slot * NY)
        return pltpu.make_async_remote_copy(
            src_ref=hold.at[slot],
            dst_ref=above.at[block],
            send_sem=hold_send.at[slot],
            recv_sem=halo_recv.at[block],
            device_id={"space": beyond, "vec": beyond_lane},
            device_id_type=pl.DeviceIdType.MESH,
        )

    def hand_on(n):
        send(hold.at[n], hold.at[n], hold_send.at[n], hold_recv.at[n], space=sibling).wait_recv()
        handed(n).start()

    def forward(mu, rows, vecs):
        for row in range(3):
            real = []
            imag = []
            for col in range(3):
                link_re = links[mu, row, col, pl.ds(0, 1), :]
                link_im = links[mu, row, col, pl.ds(1, 1), :]
                vec_re, vec_im = vecs[col]
                real.append(link_re * vec_re - link_im * vec_im)
                imag.append(link_re * vec_im + link_im * vec_re)
            moved[mu, row, 0, rows, :] = (real[0] + real[1] + real[2]).astype(jnp.bfloat16)
            moved[mu, row, 1, rows, :] = (imag[0] + imag[1] + imag[2]).astype(jnp.bfloat16)

    def move_yz(block):
        def step(i, carry):
            first = pl.multiple_of(i * 16, 16)
            rows = pl.ds(pl.multiple_of(block * VB + first, 16), 16)
            vecs = [[held[block, c, p, pl.ds(first, 16), :].astype(jnp.float32) for p in range(2)] for c in range(3)]
            border = edge[block, pl.ds(first, 16), :].astype(jnp.float32)
            along_y = [
                [
                    jnp.where(
                        place < CHUNK - LZ,
                        pltpu.roll(vecs[c][p], CHUNK - LZ, 1),
                        pltpu.roll(border, CHUNK - LZ - LZ * (2 * c + p), 1),
                    )
                    for p in range(2)
                ]
                for c in range(3)
            ]
            forward(1, rows, along_y)
            along_z = [
                [
                    jnp.where(place % LZ == LZ - 1, pltpu.roll(v, LZ - 1, 1), pltpu.roll(v, CHUNK - 1, 1))
                    for v in vecs[c]
                ]
                for c in range(3)
            ]
            forward(2, rows, along_z)
            return carry

        lax.fori_loop(0, 2, step, 0)

    def move_x(block):
        def step(i, carry):
            rows = pl.ds(pl.multiple_of(block * VB + i * 16, 16), 16)
            half = pl.ds(pl.multiple_of(i * 16, 16), 16)
            forward(0, rows, [[above[block, c, p, half, :].astype(jnp.float32) for p in range(2)] for c in range(3)])
            return carry

        lax.fori_loop(0, 2, step, 0)

    start_halo(0, lane)

    def arrive(n, carry):
        from_lane(step_of(n))[0].wait_recv()
        start_halo(n, block_of(lane, n))

        @pl.when(jnp.logical_and(jnp.logical_and(relays, n > 1), lax.rem(n + NY - 1, NY) == y))
        def _():
            hand_on(lax.div(n - 2, NY))

        return carry

    @pl.when(yields)
    def _():
        for n in range(1, 6):
            piece(step_of(n)).wait_send()
        for n in range(6, NB):
            piece(step_of(n)).start()

    lax.fori_loop(1, NB, arrive, 0)

    @pl.when(jnp.logical_and(relays, y == NY - 1))
    def _():
        hand_on(1)

    def move(n, carry):
        from_lane(step_of(n))[1].wait_recv()
        move_yz(block_of(lane, n))
        return carry

    move_yz(lane)
    lax.fori_loop(1, NB, move, 0)


    tile = (NV, 128)
    row_a = lax.broadcasted_iota(jnp.int32, tile, 0) % NB
    slot = lax.broadcasted_iota(jnp.int32, tile, 1) // VB
    low_tile = (row_a - slot + NB) % NB < NB // 2

    first_half = lax.broadcasted_iota(jnp.int32, tile, 1) % VB < VB // 2

    def lay(which, b, real, imag):
        halves = (
            jnp.where(first_half, real, pltpu.roll(imag, VB // 2, 1)),
            jnp.where(first_half, pltpu.roll(real, 128 - VB // 2, 1), imag),
        )
        for h in range(NC):
            parts[which, h, :, :, b] = halves[h].reshape(NY, NX, 16, 128)

    def product(mu, which, b):
        moved_mu = [jnp.concatenate([moved[mu, c, p] for c in range(3)], axis=1) for p in range(2)]
        held_all = [jnp.concatenate([held[:, c, p].reshape(NV, CHUNK) for c in range(3)], axis=1) for p in range(2)]
        left = [jnp.concatenate([in_order(moved_mu[p]), ordered[p]], axis=1) for p in range(2)]
        right = [jnp.concatenate([held_all[p], moved_mu[p]], axis=1) for p in range(2)]

        def dot(p, q):
            return lax.dot_general(
                left[p], right[q], (((1,), (1,)), ((), ())), preferred_element_type=jnp.float32
            )

        near = []
        for t, total in enumerate((dot(0, 0) + dot(1, 1), dot(0, 1) - dot(1, 0))):
            low, high = total[:, :128], total[:, 128:]
            near.append(jnp.where(low_tile, low, high))
            rest = jnp.where(low_tile, high, low)
            if mu == 1:
                far[t] = pltpu.roll(rest, VB, 1)
            elif mu == 2:
                far[t] = jnp.where(slot == (row_a + 1) % 4, far[t], pltpu.roll(rest, 2 * VB, 1))
            else:
                far[t] = jnp.where(slot == row_a % 4, rest, far[t])
        lay(which, b, near[0], near[1])
        if mu == 0:
            lay(which, 1, far[0], far[1])

    def swap(which, i):
        yy = lax.rem(y + i, NY)
        return send(
            parts.at[which, 1 - core, yy],
            swapped.at[which, yy],
            swap_send.at[which, yy],
            swap_recv.at[which, yy],
            space=sibling,
        )

    def to_xy(which, i, j):
        yy, xx = lax.rem(y + i, NY), lax.rem(x + j, NX)
        slot = lax.rem(i, NY) * NX + j - 1
        return send(
            parts.at[which, core, yy, xx],
            got_xy.at[which, slot],
            xy_send.at[which, slot],
            xy_recv.at[which, slot],
            space=at(xx, z_hi, yy, core),
        )

    def sum_cores(which):
        def swap_start(i, carry):
            swap(which, i).start()
            return carry

        def swap_add(i):
            yy = lax.rem(y + i, NY)
            swap(which, i).wait_recv()
            parts[which, core, yy] = parts[which, core, yy] + swapped[which, yy]

        def xy_start(i, carry):
            swap_add(i)
            for j in range(NX):
                to_xy(which, i, j).start()
            return carry

        lax.fori_loop(1, NY + 1, swap_start, 0)
        lax.fori_loop(1, NY, xy_start, 0)
        swap_add(NY)
        for j in range(1, NX):
            to_xy(which, 0, j).start()

    def sum_chips(which):
        def xy_add(slot, totals):
            i, j = lax.div(slot + 1, NX), lax.rem(slot + 1, NX)
            to_xy(which, i, j).wait_recv()
            return tuple(totals[b] + got_xy[which, slot, b] for b in range(2))

        own_part = tuple(parts[which, core, y, x, b] for b in range(2))
        totals = lax.fori_loop(0, NX * NY - 1, xy_add, own_part)
        for b in range(2):
            sum_xy[:, 2 * which + b, :] = totals[b]

    for p in range(2):
        ordered[p] = in_order(jnp.concatenate([held[:, c, p].reshape(NV, CHUNK) for c in range(3)], axis=1))
    product(1, 0, 0)
    product(2, 0, 1)
    sum_cores(0)

    def arrive_x(n, carry):
        block = block_of(up_lane, n)
        halo(block).wait_recv()
        move_x(block)
        return carry

    lax.fori_loop(0, NB, arrive_x, 0)
    product(0, 1, 0)
    sum_cores(1)
    sum_chips(0)
    sum_chips(1)

    def to_z(j):
        there, peer = z_peer(j)
        return pltpu.make_async_remote_copy(
            src_ref=sum_xy.at[there * NB + peer],
            dst_ref=got_z.at[j],
            send_sem=z_send.at[j],
            recv_sem=z_recv.at[j],
            device_id={"space": at(x, there, y, core), "vec": peer},
            device_id_type=pl.DeviceIdType.MESH,
        )

    def z_start(j, carry):
        to_z(j).start()
        return carry

    def z_add(j, total):
        to_z(j).wait_recv()
        return total + got_z[j]

    lax.fori_loop(0, NH * NB - 1, z_start, 0)

    def drain(n, carry):
        @pl.when(jnp.logical_or(jnp.logical_not(yields), n > 5))
        def _():
            piece(step_of(n)).wait_send()

        edge_piece(n).wait_send()
        return carry

    def drain_halo(block, carry):
        halo(block).wait_send()
        return carry

    @pl.when(relays)
    def _():
        for n in range(2):
            handed(n).wait_send()

    lax.fori_loop(1, NB, drain, 0)
    lax.fori_loop(0, NB, drain_halo, 0)
    for which in range(2):

        def drain_swap(i, carry):
            swap(which, i).wait_send()
            return carry

        def drain_xy(slot, carry):
            to_xy(which, lax.div(slot + 1, NX), lax.rem(slot + 1, NX)).wait_send()
            return carry

        lax.fori_loop(1, NY + 1, drain_swap, 0)
        lax.fori_loop(0, NX * NY - 1, drain_xy, 0)

    total = lax.fori_loop(0, NH * NB - 1, z_add, sum_xy[z_hi * NB + lane]) * scale
    total = pltpu.roll(total, (4 - lane % 4) % 4 * VB, 1)

    half = VB // 2
    for t in range(2):
        for mu in range(3):
            for k in range(NK):
                row, slot_k = ((mu + 2) % 3, (4 - k) % 4) if k < 4 else (3, mu)
                first = slot_k * VB + t * half
                at_row = (mu * NK + k) * 2 + t
                picked[at_row : at_row + 1, :half] = total[row : row + 1, first : first + half]
    for d in range(3):
        mu = directions[d]
        for q in range(NK):
            rows = pl.ds((mu * NK + offsets[q]) * 2, 2)
            out[d, q, :, 0, :] = picked[rows, :half]

    def drain_z(j, carry):
        to_z(j).wait_send()
        return carry

    lax.fori_loop(0, NH * NB - 1, drain_z, 0)


def body(vectors, links, directions, offsets):
    planes = lax.axis_size("space")
    scale = 1.0 / math.sqrt(6.0 * planes * SITES)
    bf16, f32 = jnp.bfloat16, jnp.float32
    dma = pltpu.SemaphoreType.DMA
    zs = NH * NB - 1
    return pl.pallas_call(
        functools.partial(kernel, scale=scale),
        out_shape=jax.ShapeDtypeStruct((3, NK, 2, 1, VB // 2), f32),
        in_specs=[
            pl.BlockSpec(memory_space=pl.ANY),
            pl.BlockSpec(memory_space=pl.ANY),
            pl.BlockSpec(memory_space=pltpu.SMEM),
            pl.BlockSpec(memory_space=pltpu.SMEM),
        ],
        out_specs=pl.BlockSpec(memory_space=pltpu.VMEM),
        scratch_shapes=[
            pltpu.VMEM((NB, 3, 2, VB, CHUNK), bf16),
            pltpu.VMEM((NB, 3, 2, VB, CHUNK), bf16),
            pltpu.VMEM((NB, 3, 2, VB, CHUNK), bf16),
            pltpu.VMEM((2, 3, 2, VB, CHUNK), bf16),
            pltpu.VMEM((NB, VB, CHUNK), bf16),
            pltpu.VMEM((NB, VB, CHUNK), bf16),
            pltpu.VMEM((3, 3, 3, 2, CHUNK), f32),
            pltpu.VMEM((3, 3, 2, NV, CHUNK), bf16),
            pltpu.VMEM((NV, NV), bf16),
            pltpu.VMEM((2, NV, 3 * CHUNK), bf16),
            pltpu.VMEM((2, NV, 128), f32),
            pltpu.VMEM((2, 2, NY, NX, 2, 16, 128), f32),
            pltpu.VMEM((2, NY, NX, 2, 16, 128), f32),
            pltpu.VMEM((2, NX * NY - 1, 2, 16, 128), f32),
            pltpu.VMEM((16, 4, 128), f32),
            pltpu.VMEM((zs, 4, 128), f32),
            pltpu.VMEM((6 * NK + 2, 128), f32),
            dma((2,)),
            dma((NB,)),
            dma((NB - 1,)),
            dma((NB - 1,)),
            dma((NB - 1,)),
            dma((NB - 1,)),
            dma((NB,)),
            dma((NB,)),
            dma((2,)),
            dma((2,)),
            dma((2, NY)),
            dma((2, NY)),
            dma((2, NX * NY - 1)),
            dma((2, NX * NY - 1)),
            dma((zs,)),
            dma((zs,)),
        ],
        compiler_params=pltpu.CompilerParams(
            collective_id=0, has_side_effects=True, vmem_limit_bytes=63 * 1024 * 1024
        ),
        name="elementals",
    )(vectors, links, directions, offsets)


def solution(mesh):
    placed = (
        P("space", None, None, "vec", None),
        P("space", None, None, None, None, None),
        P(),
        P(),
    )
    return jax.shard_map(
        body,
        mesh=mesh,
        in_specs=placed,
        out_specs=P(None, None, None, "vec", "space"),
        check_vma=False,
    )
```

```python
import functools
import math

import jax
import jax.numpy as jnp
from jax import lax
from jax.experimental import pallas as pl
from jax.experimental.pallas import tpu as pltpu
from jax.sharding import PartitionSpec as P

LZ = 16
SITES = 1024
VB = 32
NV = 256
NB = NV // VB
NK = 5
CHUNK = SITES // NB
NX, NH, NY, NC = 4, 2, 4, 2
ROWS = NX * NH * NY


def send(src, dst, send_sem, recv_sem, **where):
    return pltpu.make_async_remote_copy(
        src_ref=src,
        dst_ref=dst,
        send_sem=send_sem,
        recv_sem=recv_sem,
        device_id=where,
        device_id_type=pl.DeviceIdType.MESH,
    )


def kernel(
    vec_hbm,
    link_hbm,
    directions,
    offsets,
    out,
    own,
    held,
    above,
    hold,
    edges,
    edge,
    links,
    moved,
    order,
    ordered,
    far,
    parts,
    swapped,
    got_xy,
    sum_xy,
    got_z,
    picked,
    local_sem,
    own_sem,
    vec_send,
    vec_recv,
    edge_send,
    edge_recv,
    halo_send,
    halo_recv,
    hold_send,
    hold_recv,
    swap_send,
    swap_recv,
    xy_send,
    xy_recv,
    z_send,
    z_recv,
    *,
    scale,
):
    space = lax.axis_index("space")
    lane = lax.axis_index("vec")
    planes = lax.axis_size("space")
    core = lax.rem(space, NC)
    y = lax.rem(lax.div(space, NC), NY)
    z_hi = lax.rem(lax.div(space, NC * NY), NH)
    x = lax.div(space, NC * NY * NH)
    up = lax.rem(space + 1, planes)
    down = lax.rem(space + planes - 1, planes)

    def at(x, z_hi, y, core):
        return ((x * NH + z_hi) * NY + y) * NC + core

    def flip(z_hi, lane):
        return lane + z_hi * (NB - 1 - 2 * lane)

    def half_of(space):
        return lax.rem(lax.div(space, NC * NY), NH)

    chunk = flip(z_hi, lane)
    up_lane = flip(half_of(up), chunk)
    down_lane = flip(half_of(down), chunk)
    sibling = at(x, z_hi, y, 1 - core)

    def lanes_of(chunk):
        return pl.ds(pl.multiple_of(chunk * CHUNK, CHUNK), CHUNK)

    own_in = [
        pltpu.make_async_copy(vec_hbm.at[0, :, :, :, pl.ds(c * CHUNK, CHUNK)], own.at[c], own_sem.at[c])
        for c in range(NB)
    ]
    links_in = pltpu.make_async_copy(link_hbm.at[0, :, :, :, :, lanes_of(chunk)], links, local_sem.at[1])
    mine_in = pltpu.make_async_copy(
        vec_hbm.at[0, :, :, :, lanes_of(chunk)], held.at[lane], local_sem.at[0]
    )

    def z_peer(j):
        near = (j >= NB).astype(jnp.int32)
        return lax.rem(z_hi + 1 - near, NH), lax.rem(lane + j + near, NB)

    barrier = pltpu.get_barrier_semaphore()

    def greet(space, lane):
        pl.semaphore_signal(
            barrier, inc=1, device_id={"space": space, "vec": lane}, device_id_type=pl.DeviceIdType.MESH
        )

    crossing = jnp.logical_and(y == 0, core == 0)
    crossed = jnp.logical_and(y == NY - 1, core == NC - 1)
    relays = jnp.logical_and(y > 0, core == 0)
    beyond = lax.rem(at(x, z_hi, 0, 0) + planes - 1, planes)
    beyond_lane = flip(half_of(beyond), chunk)

    lower_half = z_hi == 0

    def greet_near(j, carry):
        greet(space, lax.rem(lane + j, NB))
        return carry

    def greet_far():
        def greet_z(j, carry):
            greet(at(x, 1 - z_hi, y, core), j)
            return carry

        lax.fori_loop(0, NB, greet_z, 0)

        @pl.when(crossing)
        def _():
            greet(down, down_lane)

        @pl.when(crossed)
        def _():
            for q in range(NY):
                greet(up + q * NC, up_lane)

        @pl.when(relays)
        def _():
            greet(beyond, beyond_lane)

    lax.fori_loop(1, NB, greet_near, 0)

    @pl.when(jnp.logical_not(crossed))
    def _():
        greet(up, up_lane)

    @pl.when(jnp.logical_not(crossing))
    def _():
        greet(down, down_lane)

    for i in range(1, NX * NY):
        greet(at(lax.rem(x + i % NX, NX), z_hi, lax.rem(y + i // NX, NY), core), lane)

    for copy in own_in:
        copy.start()
    links_in.start()
    mine_in.start()

    def one(flag):
        return flag.astype(jnp.int32)

    near_count = NB - 1 + NX * NY - 1 + 2 - one(crossed) - one(crossing)
    far_count = NB + one(crossing) + one(relays) + NY * one(crossed)

    for copy in own_in:
        copy.wait()

    place = lax.broadcasted_iota(jnp.int32, (16, CHUNK), 1)
    row = lax.broadcasted_iota(jnp.int32, (NV, NV), 0)
    col = lax.broadcasted_iota(jnp.int32, (NV, NV), 1)
    source = (row % NB) * VB + (row // NB % (NX * NH)) * NY + row // (NB * NX * NH)
    order[...] = (col == source).astype(jnp.float32).astype(jnp.bfloat16)

    def in_order(rows):
        return jnp.dot(order[...], rows, preferred_element_type=jnp.float32).astype(jnp.bfloat16)


    def pack(i, carry):
        to = lax.div(i, 2)
        rows = pl.ds(pl.multiple_of(lax.rem(i, 2) * 16, 16), 16)
        found = jnp.zeros((16, CHUNK), jnp.float32)
        for n in range(6):
            field = own[lax.rem(to + 1, NB), n // 2, n % 2, rows, :].astype(jnp.float32)
            found = jnp.where(place // LZ == n, pltpu.roll(field, n * LZ, 1) if n else field, found)
        edges[to, rows, :] = found.astype(jnp.bfloat16)
        return carry

    lax.fori_loop(0, 2 * NB, pack, 0)
    @pl.when(lower_half)
    def _():
        pl.semaphore_wait(barrier, near_count)
        greet_far()

    @pl.when(jnp.logical_not(lower_half))
    def _():
        pl.semaphore_wait(barrier, near_count + far_count)

    def step_of(n):
        if isinstance(n, int):
            return (NB // 2 + (2 * (n % 2) - 1) * (n // 2)) if n else 0
        return (n > 0).astype(jnp.int32) * (NB // 2 + (2 * lax.rem(n, 2) - 1) * lax.div(n, 2))

    def block_of(lane, n):
        return lax.rem(lane + NB - step_of(n), NB)

    def piece(j):
        to = lax.rem(lane + j, NB)
        return send(
            own.at[flip(z_hi, to)],
            held.at[lane],
            vec_send.at[j - 1],
            vec_recv.at[j - 1],
            vec=to,
        )

    def edge_piece(j):
        to = lax.rem(lane + j, NB)
        return send(edges.at[flip(z_hi, to)], edge.at[lane], edge_send.at[j - 1], edge_recv.at[j - 1], vec=to)

    def from_lane(j):
        block = lax.rem(lane + NB - j, NB)
        return (
            send(held.at[block], held.at[block], vec_send.at[j - 1], vec_recv.at[j - 1], vec=block),
            send(edges.at[0], edge.at[block], edge_send.at[j - 1], edge_recv.at[j - 1], vec=block),
        )

    yields = jnp.logical_and(y == 0, core == NC - 1)
    for n in range(1, NB):

        @pl.when(jnp.logical_or(jnp.logical_not(yields), n <= 5))
        def _():
            piece(step_of(n)).start()

    @pl.when(jnp.logical_not(lower_half))
    def _():
        greet_far()

    edge[lane] = edges[chunk]
    mine_in.wait()
    links_in.wait()

    def start_edges(n, carry):
        edge_piece(step_of(n)).start()
        return carry

    lax.fori_loop(1, NB, start_edges, 0)

    @pl.when(lower_half)
    def _():
        pl.semaphore_wait(barrier, far_count)

    def halo(block):
        return pltpu.make_async_remote_copy(
            src_ref=held.at[block],
            dst_ref=above.at[block],
            send_sem=halo_send.at[block],
            recv_sem=halo_recv.at[block],
            device_id={"space": down, "vec": down_lane},
            device_id_type=pl.DeviceIdType.MESH,
        )

    def to_relay(n, block):
        slot = lax.div(n, NY)
        return send(
            held.at[block],
            hold.at[slot],
            halo_send.at[block],
            hold_recv.at[slot],
            space=at(x, z_hi, lax.rem(n + 1, NY), core),
        )

    def start_halo(n, block):
        aside = jnp.logical_and(crossing, lax.rem(n + 1, NY) != 0)

        @pl.when(aside)
        def _():
            to_relay(n, block).start()

        @pl.when(jnp.logical_not(aside))
        def _():
            halo(block).start()

    def handed(slot):
        block = block_of(lane, y - 1 + slot * NY)
        return pltpu.make_async_remote_copy(
            src_ref=hold.at[slot],
            dst_ref=above.at[block],
            send_sem=hold_send.at[slot],
            recv_sem=halo_recv.at[block],
            device_id={"space": beyond, "vec": beyond_lane},
            device_id_type=pl.DeviceIdType.MESH,
        )

    def hand_on(n):
        send(hold.at[n], hold.at[n], hold_send.at[n], hold_recv.at[n], space=sibling).wait_recv()
        handed(n).start()

    def forward(mu, rows, vecs):
        for row in range(3):
            real = []
            imag = []
            for col in range(3):
                link_re = links[mu, row, col, pl.ds(0, 1), :]
                link_im = links[mu, row, col, pl.ds(1, 1), :]
                vec_re, vec_im = vecs[col]
                real.append(link_re * vec_re - link_im * vec_im)
                imag.append(link_re * vec_im + link_im * vec_re)
            moved[mu, row, 0, rows, :] = (real[0] + real[1] + real[2]).astype(jnp.bfloat16)
            moved[mu, row, 1, rows, :] = (imag[0] + imag[1] + imag[2]).astype(jnp.bfloat16)

    def move_yz(block):
        def step(i, carry):
            first = pl.multiple_of(i * 16, 16)
            rows = pl.ds(pl.multiple_of(block * VB + first, 16), 16)
            vecs = [[held[block, c, p, pl.ds(first, 16), :].astype(jnp.float32) for p in range(2)] for c in range(3)]
            border = edge[block, pl.ds(first, 16), :].astype(jnp.float32)
            along_y = [
                [
                    jnp.where(
                        place < CHUNK - LZ,
                        pltpu.roll(vecs[c][p], CHUNK - LZ, 1),
                        pltpu.roll(border, CHUNK - LZ - LZ * (2 * c + p), 1),
                    )
                    for p in range(2)
                ]
                for c in range(3)
            ]
            forward(1, rows, along_y)
            along_z = [
                [
                    jnp.where(place % LZ == LZ - 1, pltpu.roll(v, LZ - 1, 1), pltpu.roll(v, CHUNK - 1, 1))
                    for v in vecs[c]
                ]
                for c in range(3)
            ]
            forward(2, rows, along_z)
            return carry

        lax.fori_loop(0, 2, step, 0)

    def move_x(block):
        def step(i, carry):
            rows = pl.ds(pl.multiple_of(block * VB + i * 16, 16), 16)
            half = pl.ds(pl.multiple_of(i * 16, 16), 16)
            forward(0, rows, [[above[block, c, p, half, :].astype(jnp.float32) for p in range(2)] for c in range(3)])
            return carry

        lax.fori_loop(0, 2, step, 0)

    start_halo(0, lane)

    def arrive(n, carry):
        from_lane(step_of(n))[0].wait_recv()
        start_halo(n, block_of(lane, n))

        @pl.when(jnp.logical_and(jnp.logical_and(relays, n > 1), lax.rem(n + NY - 1, NY) == y))
        def _():
            hand_on(lax.div(n - 2, NY))

        return carry

    @pl.when(yields)
    def _():
        for n in range(1, 6):
            piece(step_of(n)).wait_send()
        for n in range(6, NB):
            piece(step_of(n)).start()

    lax.fori_loop(1, NB, arrive, 0)

    @pl.when(jnp.logical_and(relays, y == NY - 1))
    def _():
        hand_on(1)

    def move(n, carry):
        from_lane(step_of(n))[1].wait_recv()
        move_yz(block_of(lane, n))
        return carry

    move_yz(lane)
    lax.fori_loop(1, NB, move, 0)


    tile = (NV, 128)
    row_a = lax.broadcasted_iota(jnp.int32, tile, 0) % NB
    slot = lax.broadcasted_iota(jnp.int32, tile, 1) // VB
    low_tile = (row_a - slot + NB) % NB < NB // 2

    first_half = lax.broadcasted_iota(jnp.int32, tile, 1) % VB < VB // 2

    def lay(which, b, real, imag):
        halves = (
            jnp.where(first_half, real, pltpu.roll(imag, VB // 2, 1)),
            jnp.where(first_half, pltpu.roll(real, 128 - VB // 2, 1), imag),
        )
        for h in range(NC):
            parts[which, h, :, :, b] = halves[h].reshape(NY, NX, 16, 128)

    def product(mu, which, b):
        moved_mu = [jnp.concatenate([moved[mu, c, p] for c in range(3)], axis=1) for p in range(2)]
        held_all = [jnp.concatenate([held[:, c, p].reshape(NV, CHUNK) for c in range(3)], axis=1) for p in range(2)]
        left = [jnp.concatenate([in_order(moved_mu[p]), ordered[p]], axis=1) for p in range(2)]
        right = [jnp.concatenate([held_all[p], moved_mu[p]], axis=1) for p in range(2)]

        def dot(p, q):
            return lax.dot_general(
                left[p], right[q], (((1,), (1,)), ((), ())), preferred_element_type=jnp.float32
            )

        def both_parts():
            return lax.dot_general(
                jnp.concatenate(left, axis=1),
                jnp.concatenate(right, axis=1),
                (((1,), (1,)), ((), ())),
                preferred_element_type=jnp.float32,
            )

        near = []
        for t, total in enumerate((both_parts(), dot(0, 1) - dot(1, 0))):
            low, high = total[:, :128], total[:, 128:]
            near.append(jnp.where(low_tile, low, high))
            rest = jnp.where(low_tile, high, low)
            if mu == 1:
                far[t] = pltpu.roll(rest, VB, 1)
            elif mu == 2:
                far[t] = jnp.where(slot == (row_a + 1) % 4, far[t], pltpu.roll(rest, 2 * VB, 1))
            else:
                far[t] = jnp.where(slot == row_a % 4, rest, far[t])
        lay(which, b, near[0], near[1])
        if mu == 0:
            lay(which, 1, far[0], far[1])

    def line(i):
        return i + (i == 1).astype(jnp.int32) - (i == 2).astype(jnp.int32)

    def swap(which, i):
        yy = lax.rem(y + i, NY)
        return send(
            parts.at[which, 1 - core, yy],
            swapped.at[which, yy],
            swap_send.at[which, yy],
            swap_recv.at[which, yy],
            space=sibling,
        )

    def to_xy(which, i, j):
        yy, xx = lax.rem(y + i, NY), lax.rem(x + j, NX)
        slot = lax.rem(i, NY) * NX + j - 1
        return send(
            parts.at[which, core, yy, xx],
            got_xy.at[which, slot],
            xy_send.at[which, slot],
            xy_recv.at[which, slot],
            space=at(xx, z_hi, yy, core),
        )

    def sum_cores(which):
        def swap_start(i, carry):
            swap(which, line(i)).start()
            return carry

        def swap_add(i):
            yy = lax.rem(y + i, NY)
            swap(which, i).wait_recv()
            parts[which, core, yy] = parts[which, core, yy] + swapped[which, yy]

        def xy_start(i, carry):
            far_i = line(i)
            swap_add(far_i)
            for j in (2, 1, 3, 0):
                to_xy(which, far_i, j).start()
            return carry

        lax.fori_loop(1, NY + 1, swap_start, 0)
        lax.fori_loop(1, NY, xy_start, 0)
        swap_add(NY)
        for j in range(1, NX):
            to_xy(which, 0, j).start()

    def sum_chips(which):
        def xy_add(slot, totals):
            i, j = lax.div(slot + 1, NX), lax.rem(slot + 1, NX)
            to_xy(which, i, j).wait_recv()
            return tuple(totals[b] + got_xy[which, slot, b] for b in range(2))

        own_part = tuple(parts[which, core, y, x, b] for b in range(2))
        totals = lax.fori_loop(0, NX * NY - 1, xy_add, own_part)
        for b in range(2):
            sum_xy[:, 2 * which + b, :] = totals[b]

    for p in range(2):
        ordered[p] = in_order(jnp.concatenate([held[:, c, p].reshape(NV, CHUNK) for c in range(3)], axis=1))
    product(1, 0, 0)
    product(2, 0, 1)
    sum_cores(0)

    def arrive_x(n, carry):
        block = block_of(up_lane, n)
        halo(block).wait_recv()
        move_x(block)
        return carry

    lax.fori_loop(0, NB, arrive_x, 0)
    product(0, 1, 0)
    sum_cores(1)
    sum_chips(0)
    sum_chips(1)

    def to_z(j):
        there, peer = z_peer(j)
        return pltpu.make_async_remote_copy(
            src_ref=sum_xy.at[there * NB + peer],
            dst_ref=got_z.at[j],
            send_sem=z_send.at[j],
            recv_sem=z_recv.at[j],
            device_id={"space": at(x, there, y, core), "vec": peer},
            device_id_type=pl.DeviceIdType.MESH,
        )

    def z_start(j, carry):
        to_z(j).start()
        return carry

    def z_add(j, total):
        to_z(j).wait_recv()
        return total + got_z[j]

    lax.fori_loop(0, NH * NB - 1, z_start, 0)

    def drain(n, carry):
        @pl.when(jnp.logical_or(jnp.logical_not(yields), n > 5))
        def _():
            piece(step_of(n)).wait_send()

        edge_piece(n).wait_send()
        return carry

    def drain_halo(block, carry):
        halo(block).wait_send()
        return carry

    @pl.when(relays)
    def _():
        for n in range(2):
            handed(n).wait_send()

    lax.fori_loop(1, NB, drain, 0)
    lax.fori_loop(0, NB, drain_halo, 0)
    for which in range(2):

        def drain_swap(i, carry):
            swap(which, i).wait_send()
            return carry

        def drain_xy(slot, carry):
            to_xy(which, lax.div(slot + 1, NX), lax.rem(slot + 1, NX)).wait_send()
            return carry

        lax.fori_loop(1, NY + 1, drain_swap, 0)
        lax.fori_loop(0, NX * NY - 1, drain_xy, 0)

    total = lax.fori_loop(0, NH * NB - 1, z_add, sum_xy[z_hi * NB + lane]) * scale
    total = pltpu.roll(total, (4 - lane % 4) % 4 * VB, 1)

    half = VB // 2
    for t in range(2):
        for mu in range(3):
            for k in range(NK):
                row, slot_k = ((mu + 2) % 3, (4 - k) % 4) if k < 4 else (3, mu)
                first = slot_k * VB + t * half
                at_row = (mu * NK + k) * 2 + t
                picked[at_row : at_row + 1, :half] = total[row : row + 1, first : first + half]
    for d in range(3):
        mu = directions[d]
        for q in range(NK):
            rows = pl.ds((mu * NK + offsets[q]) * 2, 2)
            out[d, q, :, 0, :] = picked[rows, :half]

    def drain_z(j, carry):
        to_z(j).wait_send()
        return carry

    lax.fori_loop(0, NH * NB - 1, drain_z, 0)


def body(vectors, links, directions, offsets):
    planes = lax.axis_size("space")
    scale = 1.0 / math.sqrt(6.0 * planes * SITES)
    bf16, f32 = jnp.bfloat16, jnp.float32
    dma = pltpu.SemaphoreType.DMA
    zs = NH * NB - 1
    return pl.pallas_call(
        functools.partial(kernel, scale=scale),
        out_shape=jax.ShapeDtypeStruct((3, NK, 2, 1, VB // 2), f32),
        in_specs=[
            pl.BlockSpec(memory_space=pl.ANY),
            pl.BlockSpec(memory_space=pl.ANY),
            pl.BlockSpec(memory_space=pltpu.SMEM),
            pl.BlockSpec(memory_space=pltpu.SMEM),
        ],
        out_specs=pl.BlockSpec(memory_space=pltpu.VMEM),
        scratch_shapes=[
            pltpu.VMEM((NB, 3, 2, VB, CHUNK), bf16),
            pltpu.VMEM((NB, 3, 2, VB, CHUNK), bf16),
            pltpu.VMEM((NB, 3, 2, VB, CHUNK), bf16),
            pltpu.VMEM((2, 3, 2, VB, CHUNK), bf16),
            pltpu.VMEM((NB, VB, CHUNK), bf16),
            pltpu.VMEM((NB, VB, CHUNK), bf16),
            pltpu.VMEM((3, 3, 3, 2, CHUNK), f32),
            pltpu.VMEM((3, 3, 2, NV, CHUNK), bf16),
            pltpu.VMEM((NV, NV), bf16),
            pltpu.VMEM((2, NV, 3 * CHUNK), bf16),
            pltpu.VMEM((2, NV, 128), f32),
            pltpu.VMEM((2, 2, NY, NX, 2, 16, 128), f32),
            pltpu.VMEM((2, NY, NX, 2, 16, 128), f32),
            pltpu.VMEM((2, NX * NY - 1, 2, 16, 128), f32),
            pltpu.VMEM((16, 4, 128), f32),
            pltpu.VMEM((zs, 4, 128), f32),
            pltpu.VMEM((6 * NK + 2, 128), f32),
            dma((2,)),
            dma((NB,)),
            dma((NB - 1,)),
            dma((NB - 1,)),
            dma((NB - 1,)),
            dma((NB - 1,)),
            dma((NB,)),
            dma((NB,)),
            dma((2,)),
            dma((2,)),
            dma((2, NY)),
            dma((2, NY)),
            dma((2, NX * NY - 1)),
            dma((2, NX * NY - 1)),
            dma((zs,)),
            dma((zs,)),
        ],
        compiler_params=pltpu.CompilerParams(
            collective_id=0, has_side_effects=True, vmem_limit_bytes=63 * 1024 * 1024
        ),
        name="elementals",
    )(vectors, links, directions, offsets)


def solution(mesh):
    placed = (
        P("space", None, None, "vec", None),
        P("space", None, None, None, None, None),
        P(),
        P(),
    )
    return jax.shard_map(
        body,
        mesh=mesh,
        in_specs=placed,
        out_specs=P(None, None, None, "vec", "space"),
        check_vma=False,
    )
```

```python
import functools
import math

import jax
import jax.numpy as jnp
from jax import lax
from jax.experimental import pallas as pl
from jax.experimental.pallas import tpu as pltpu
from jax.sharding import PartitionSpec as P

LZ = 16
SITES = 1024
VB = 32
NV = 256
NB = NV // VB
NK = 5
CHUNK = SITES // NB
NX, NH, NY, NC = 4, 2, 4, 2
ROWS = NX * NH * NY


def send(src, dst, send_sem, recv_sem, **where):
    return pltpu.make_async_remote_copy(
        src_ref=src,
        dst_ref=dst,
        send_sem=send_sem,
        recv_sem=recv_sem,
        device_id=where,
        device_id_type=pl.DeviceIdType.MESH,
    )


def kernel(
    vec_hbm,
    link_hbm,
    directions,
    offsets,
    out,
    own,
    held,
    above,
    hold,
    edges,
    edge,
    links,
    moved,
    order,
    ordered,
    far,
    parts,
    swapped,
    got_xy,
    sum_xy,
    got_z,
    picked,
    local_sem,
    own_sem,
    vec_send,
    vec_recv,
    edge_send,
    edge_recv,
    halo_send,
    halo_recv,
    hold_send,
    hold_recv,
    swap_send,
    swap_recv,
    xy_send,
    xy_recv,
    z_send,
    z_recv,
    *,
    scale,
):
    space = lax.axis_index("space")
    lane = lax.axis_index("vec")
    planes = lax.axis_size("space")
    core = lax.rem(space, NC)
    y = lax.rem(lax.div(space, NC), NY)
    z_hi = lax.rem(lax.div(space, NC * NY), NH)
    x = lax.div(space, NC * NY * NH)
    up = lax.rem(space + 1, planes)
    down = lax.rem(space + planes - 1, planes)

    def at(x, z_hi, y, core):
        return ((x * NH + z_hi) * NY + y) * NC + core

    def flip(z_hi, lane):
        return lane + z_hi * (NB - 1 - 2 * lane)

    def half_of(space):
        return lax.rem(lax.div(space, NC * NY), NH)

    chunk = flip(z_hi, lane)
    up_lane = flip(half_of(up), chunk)
    down_lane = flip(half_of(down), chunk)
    sibling = at(x, z_hi, y, 1 - core)

    def lanes_of(chunk):
        return pl.ds(pl.multiple_of(chunk * CHUNK, CHUNK), CHUNK)

    own_in = [
        pltpu.make_async_copy(vec_hbm.at[0, :, :, :, pl.ds(c * CHUNK, CHUNK)], own.at[c], own_sem.at[c])
        for c in range(NB)
    ]
    links_in = pltpu.make_async_copy(link_hbm.at[0, :, :, :, :, lanes_of(chunk)], links, local_sem.at[1])
    mine_in = pltpu.make_async_copy(
        vec_hbm.at[0, :, :, :, lanes_of(chunk)], held.at[lane], local_sem.at[0]
    )

    def z_peer(j):
        near = (j >= NB).astype(jnp.int32)
        return lax.rem(z_hi + 1 - near, NH), lax.rem(lane + j + near, NB)

    barrier = pltpu.get_barrier_semaphore()

    def greet(space, lane):
        pl.semaphore_signal(
            barrier, inc=1, device_id={"space": space, "vec": lane}, device_id_type=pl.DeviceIdType.MESH
        )

    crossing = jnp.logical_and(y == 0, core == 0)
    crossed = jnp.logical_and(y == NY - 1, core == NC - 1)
    relays = jnp.logical_and(y > 0, core == 0)
    beyond = lax.rem(at(x, z_hi, 0, 0) + planes - 1, planes)
    beyond_lane = flip(half_of(beyond), chunk)

    lower_half = z_hi == 0

    def greet_near(j, carry):
        greet(space, lax.rem(lane + j, NB))
        return carry

    def greet_far():
        def greet_z(j, carry):
            greet(at(x, 1 - z_hi, y, core), j)
            return carry

        lax.fori_loop(0, NB, greet_z, 0)

        @pl.when(crossing)
        def _():
            greet(down, down_lane)

        @pl.when(crossed)
        def _():
            for q in range(NY):
                greet(up + q * NC, up_lane)

        @pl.when(relays)
        def _():
            greet(beyond, beyond_lane)

    lax.fori_loop(1, NB, greet_near, 0)

    @pl.when(jnp.logical_not(crossed))
    def _():
        greet(up, up_lane)

    @pl.when(jnp.logical_not(crossing))
    def _():
        greet(down, down_lane)

    for i in range(1, NX * NY):
        greet(at(lax.rem(x + i % NX, NX), z_hi, lax.rem(y + i // NX, NY), core), lane)

    for copy in own_in:
        copy.start()
    links_in.start()
    mine_in.start()

    def one(flag):
        return flag.astype(jnp.int32)

    near_count = NB - 1 + NX * NY - 1 + 2 - one(crossed) - one(crossing)
    far_count = NB + one(crossing) + one(relays) + NY * one(crossed)

    for copy in own_in:
        copy.wait()

    place = lax.broadcasted_iota(jnp.int32, (16, CHUNK), 1)
    row = lax.broadcasted_iota(jnp.int32, (NV, NV), 0)
    col = lax.broadcasted_iota(jnp.int32, (NV, NV), 1)
    source = (row % NB) * VB + (row // NB % (NX * NH)) * NY + row // (NB * NX * NH)
    order[...] = (col == source).astype(jnp.float32).astype(jnp.bfloat16)

    def in_order(rows):
        return jnp.dot(order[...], rows, preferred_element_type=jnp.float32).astype(jnp.bfloat16)


    def pack(i, carry):
        to = lax.div(i, 2)
        rows = pl.ds(pl.multiple_of(lax.rem(i, 2) * 16, 16), 16)
        found = jnp.zeros((16, CHUNK), jnp.float32)
        for n in range(6):
            field = own[lax.rem(to + 1, NB), n // 2, n % 2, rows, :].astype(jnp.float32)
            found = jnp.where(place // LZ == n, pltpu.roll(field, n * LZ, 1) if n else field, found)
        edges[to, rows, :] = found.astype(jnp.bfloat16)
        return carry

    lax.fori_loop(0, 2 * NB, pack, 0)
    @pl.when(lower_half)
    def _():
        pl.semaphore_wait(barrier, near_count)
        greet_far()

    @pl.when(jnp.logical_not(lower_half))
    def _():
        pl.semaphore_wait(barrier, near_count + far_count)

    def step_of(n):
        if isinstance(n, int):
            return (NB // 2 + (2 * (n % 2) - 1) * (n // 2)) if n else 0
        return (n > 0).astype(jnp.int32) * (NB // 2 + (2 * lax.rem(n, 2) - 1) * lax.div(n, 2))

    def block_of(lane, n):
        return lax.rem(lane + NB - step_of(n), NB)

    def piece(j):
        to = lax.rem(lane + j, NB)
        return send(
            own.at[flip(z_hi, to)],
            held.at[lane],
            vec_send.at[j - 1],
            vec_recv.at[j - 1],
            vec=to,
        )

    def edge_piece(j):
        to = lax.rem(lane + j, NB)
        return send(edges.at[flip(z_hi, to)], edge.at[lane], edge_send.at[j - 1], edge_recv.at[j - 1], vec=to)

    def from_lane(j):
        block = lax.rem(lane + NB - j, NB)
        return (
            send(held.at[block], held.at[block], vec_send.at[j - 1], vec_recv.at[j - 1], vec=block),
            send(edges.at[0], edge.at[block], edge_send.at[j - 1], edge_recv.at[j - 1], vec=block),
        )

    yields = jnp.logical_and(y == 0, core == NC - 1)
    for n in range(1, NB):

        @pl.when(jnp.logical_or(jnp.logical_not(yields), n <= 5))
        def _():
            piece(step_of(n)).start()

    @pl.when(jnp.logical_not(lower_half))
    def _():
        greet_far()

    edge[lane] = edges[chunk]
    mine_in.wait()
    links_in.wait()

    def start_edges(n, carry):
        edge_piece(step_of(n)).start()
        return carry

    lax.fori_loop(1, NB, start_edges, 0)

    @pl.when(lower_half)
    def _():
        pl.semaphore_wait(barrier, far_count)

    def halo(block):
        return pltpu.make_async_remote_copy(
            src_ref=held.at[block],
            dst_ref=above.at[block],
            send_sem=halo_send.at[block],
            recv_sem=halo_recv.at[block],
            device_id={"space": down, "vec": down_lane},
            device_id_type=pl.DeviceIdType.MESH,
        )

    def to_relay(n, block):
        slot = lax.div(n, NY)
        return send(
            held.at[block],
            hold.at[slot],
            halo_send.at[block],
            hold_recv.at[slot],
            space=at(x, z_hi, lax.rem(n + 1, NY), core),
        )

    def start_halo(n, block):
        aside = jnp.logical_and(crossing, lax.rem(n + 1, NY) != 0)

        @pl.when(aside)
        def _():
            to_relay(n, block).start()

        @pl.when(jnp.logical_not(aside))
        def _():
            halo(block).start()

    def handed(slot):
        block = block_of(lane, y - 1 + slot * NY)
        return pltpu.make_async_remote_copy(
            src_ref=hold.at[slot],
            dst_ref=above.at[block],
            send_sem=hold_send.at[slot],
            recv_sem=halo_recv.at[block],
            device_id={"space": beyond, "vec": beyond_lane},
            device_id_type=pl.DeviceIdType.MESH,
        )

    def hand_on(n):
        send(hold.at[n], hold.at[n], hold_send.at[n], hold_recv.at[n], space=sibling).wait_recv()
        handed(n).start()

    def forward(mu, rows, vecs):
        for row in range(3):
            real = []
            imag = []
            for col in range(3):
                link_re = links[mu, row, col, pl.ds(0, 1), :]
                link_im = links[mu, row, col, pl.ds(1, 1), :]
                vec_re, vec_im = vecs[col]
                real.append(link_re * vec_re - link_im * vec_im)
                imag.append(link_re * vec_im + link_im * vec_re)
            moved[mu, row, 0, rows, :] = (real[0] + real[1] + real[2]).astype(jnp.bfloat16)
            moved[mu, row, 1, rows, :] = (imag[0] + imag[1] + imag[2]).astype(jnp.bfloat16)

    def move_yz(block):
        def step(i, carry):
            first = pl.multiple_of(i * 16, 16)
            rows = pl.ds(pl.multiple_of(block * VB + first, 16), 16)
            vecs = [[held[block, c, p, pl.ds(first, 16), :].astype(jnp.float32) for p in range(2)] for c in range(3)]
            border = edge[block, pl.ds(first, 16), :].astype(jnp.float32)
            along_y = [
                [
                    jnp.where(
                        place < CHUNK - LZ,
                        pltpu.roll(vecs[c][p], CHUNK - LZ, 1),
                        pltpu.roll(border, CHUNK - LZ - LZ * (2 * c + p), 1),
                    )
                    for p in range(2)
                ]
                for c in range(3)
            ]
            forward(1, rows, along_y)
            along_z = [
                [
                    jnp.where(place % LZ == LZ - 1, pltpu.roll(v, LZ - 1, 1), pltpu.roll(v, CHUNK - 1, 1))
                    for v in vecs[c]
                ]
                for c in range(3)
            ]
            forward(2, rows, along_z)
            return carry

        lax.fori_loop(0, 2, step, 0)

    def move_x(block):
        def step(i, carry):
            rows = pl.ds(pl.multiple_of(block * VB + i * 16, 16), 16)
            half = pl.ds(pl.multiple_of(i * 16, 16), 16)
            forward(0, rows, [[above[block, c, p, half, :].astype(jnp.float32) for p in range(2)] for c in range(3)])
            return carry

        lax.fori_loop(0, 2, step, 0)

    start_halo(0, lane)

    def arrive(n, carry):
        from_lane(step_of(n))[0].wait_recv()
        start_halo(n, block_of(lane, n))

        @pl.when(jnp.logical_and(jnp.logical_and(relays, n > 1), lax.rem(n + NY - 1, NY) == y))
        def _():
            hand_on(lax.div(n - 2, NY))

        return carry

    @pl.when(yields)
    def _():
        for n in range(1, 6):
            piece(step_of(n)).wait_send()
        for n in range(6, NB):
            piece(step_of(n)).start()

    lax.fori_loop(1, NB, arrive, 0)

    @pl.when(jnp.logical_and(relays, y == NY - 1))
    def _():
        hand_on(1)

    def move(n, carry):
        from_lane(step_of(n))[1].wait_recv()
        move_yz(block_of(lane, n))
        return carry

    move_yz(lane)
    lax.fori_loop(1, NB, move, 0)


    tile = (NV, 128)
    row_a = lax.broadcasted_iota(jnp.int32, tile, 0) % NB
    slot = lax.broadcasted_iota(jnp.int32, tile, 1) // VB
    low_tile = (row_a - slot + NB) % NB < NB // 2

    first_half = lax.broadcasted_iota(jnp.int32, tile, 1) % VB < VB // 2

    def lay(which, b, real, imag):
        halves = (
            jnp.where(first_half, real, pltpu.roll(imag, VB // 2, 1)),
            jnp.where(first_half, pltpu.roll(real, 128 - VB // 2, 1), imag),
        )
        for h in range(NC):
            parts[which, h, :, :, b] = halves[h].reshape(NY, NX, 16, 128)

    def product(mu, which, b):
        moved_mu = [jnp.concatenate([moved[mu, c, p] for c in range(3)], axis=1) for p in range(2)]
        held_all = [jnp.concatenate([held[:, c, p].reshape(NV, CHUNK) for c in range(3)], axis=1) for p in range(2)]
        left = [jnp.concatenate([in_order(moved_mu[p]), ordered[p]], axis=1) for p in range(2)]
        right = [jnp.concatenate([held_all[p], moved_mu[p]], axis=1) for p in range(2)]

        def dot(p, q):
            return lax.dot_general(
                left[p], right[q], (((1,), (1,)), ((), ())), preferred_element_type=jnp.float32
            )

        def both_parts():
            return lax.dot_general(
                jnp.concatenate(left, axis=1),
                jnp.concatenate(right, axis=1),
                (((1,), (1,)), ((), ())),
                preferred_element_type=jnp.float32,
            )

        near = []
        for t, total in enumerate((both_parts(), dot(0, 1) - dot(1, 0))):
            low, high = total[:, :128], total[:, 128:]
            near.append(jnp.where(low_tile, low, high))
            rest = jnp.where(low_tile, high, low)
            if mu == 1:
                far[t] = pltpu.roll(rest, VB, 1)
            elif mu == 2:
                far[t] = jnp.where(slot == (row_a + 1) % 4, far[t], pltpu.roll(rest, 2 * VB, 1))
            else:
                far[t] = jnp.where(slot == row_a % 4, rest, far[t])
        lay(which, b, near[0], near[1])
        if mu == 0:
            lay(which, 1, far[0], far[1])

    def line(i):
        return i + (i == 1).astype(jnp.int32) - (i == 2).astype(jnp.int32)

    def swap(which, i):
        yy = lax.rem(y + i, NY)
        return send(
            parts.at[which, 1 - core, yy],
            swapped.at[which, yy],
            swap_send.at[which, yy],
            swap_recv.at[which, yy],
            space=sibling,
        )

    def to_xy(which, i, j):
        yy, xx = lax.rem(y + i, NY), lax.rem(x + j, NX)
        slot = lax.rem(i, NY) * NX + j - 1
        return send(
            parts.at[which, core, yy, xx],
            got_xy.at[which, slot],
            xy_send.at[which, slot],
            xy_recv.at[which, slot],
            space=at(xx, z_hi, yy, core),
        )

    def sum_cores(which):
        def swap_start(i, carry):
            swap(which, line(i)).start()
            return carry

        def swap_add(i):
            yy = lax.rem(y + i, NY)
            swap(which, i).wait_recv()
            parts[which, core, yy] = parts[which, core, yy] + swapped[which, yy]

        def xy_start(i, carry):
            far_i = line(i)
            swap_add(far_i)
            for j in (2, 1, 3, 0):
                to_xy(which, far_i, j).start()
            return carry

        lax.fori_loop(1, NY + 1, swap_start, 0)
        lax.fori_loop(1, NY, xy_start, 0)
        swap_add(NY)
        for j in range(1, NX):
            to_xy(which, 0, j).start()

    def sum_chips(which):
        def xy_add(slot, totals):
            i, j = lax.div(slot + 1, NX), lax.rem(slot + 1, NX)
            to_xy(which, i, j).wait_recv()
            return tuple(totals[b] + got_xy[which, slot, b] for b in range(2))

        own_part = tuple(parts[which, core, y, x, b] for b in range(2))
        totals = lax.fori_loop(0, NX * NY - 1, xy_add, own_part)
        for b in range(2):
            sum_xy[:, 2 * which + b, :] = totals[b]

    for p in range(2):
        ordered[p] = in_order(jnp.concatenate([held[:, c, p].reshape(NV, CHUNK) for c in range(3)], axis=1))
    product(1, 0, 0)
    product(2, 0, 1)
    sum_cores(0)

    def arrive_x(n, carry):
        block = block_of(up_lane, n)
        halo(block).wait_recv()
        move_x(block)
        return carry

    lax.fori_loop(0, NB, arrive_x, 0)
    product(0, 1, 0)
    sum_cores(1)
    sum_chips(0)
    sum_chips(1)

    def to_z(j):
        there, peer = z_peer(j)
        return pltpu.make_async_remote_copy(
            src_ref=sum_xy.at[there * NB + peer],
            dst_ref=got_z.at[j],
            send_sem=z_send.at[j],
            recv_sem=z_recv.at[j],
            device_id={"space": at(x, there, y, core), "vec": peer},
            device_id_type=pl.DeviceIdType.MESH,
        )

    def z_start(j, carry):
        to_z(j).start()
        return carry

    def z_add(j, total):
        to_z(j).wait_recv()
        return total + got_z[j]

    lax.fori_loop(0, NH * NB - 1, z_start, 0, unroll=True)

    def drain(n, carry):
        @pl.when(jnp.logical_or(jnp.logical_not(yields), n > 5))
        def _():
            piece(step_of(n)).wait_send()

        edge_piece(n).wait_send()
        return carry

    def drain_halo(block, carry):
        halo(block).wait_send()
        return carry

    @pl.when(relays)
    def _():
        for n in range(2):
            handed(n).wait_send()

    lax.fori_loop(1, NB, drain, 0)
    lax.fori_loop(0, NB, drain_halo, 0)
    for which in range(2):

        def drain_swap(i, carry):
            swap(which, i).wait_send()
            return carry

        def drain_xy(slot, carry):
            to_xy(which, lax.div(slot + 1, NX), lax.rem(slot + 1, NX)).wait_send()
            return carry

        lax.fori_loop(1, NY + 1, drain_swap, 0)
        lax.fori_loop(0, NX * NY - 1, drain_xy, 0)

    total = lax.fori_loop(0, NH * NB - 1, z_add, sum_xy[z_hi * NB + lane], unroll=True) * scale
    total = pltpu.roll(total, (4 - lane % 4) % 4 * VB, 1)

    half = VB // 2
    for t in range(2):
        for mu in range(3):
            for k in range(NK):
                row, slot_k = ((mu + 2) % 3, (4 - k) % 4) if k < 4 else (3, mu)
                first = slot_k * VB + t * half
                at_row = (mu * NK + k) * 2 + t
                picked[at_row : at_row + 1, :half] = total[row : row + 1, first : first + half]
    for d in range(3):
        mu = directions[d]
        for q in range(NK):
            rows = pl.ds((mu * NK + offsets[q]) * 2, 2)
            out[d, q, :, 0, :] = picked[rows, :half]

    def drain_z(j, carry):
        to_z(j).wait_send()
        return carry

    lax.fori_loop(0, NH * NB - 1, drain_z, 0)


def body(vectors, links, directions, offsets):
    planes = lax.axis_size("space")
    scale = 1.0 / math.sqrt(6.0 * planes * SITES)
    bf16, f32 = jnp.bfloat16, jnp.float32
    dma = pltpu.SemaphoreType.DMA
    zs = NH * NB - 1
    return pl.pallas_call(
        functools.partial(kernel, scale=scale),
        out_shape=jax.ShapeDtypeStruct((3, NK, 2, 1, VB // 2), f32),
        in_specs=[
            pl.BlockSpec(memory_space=pl.ANY),
            pl.BlockSpec(memory_space=pl.ANY),
            pl.BlockSpec(memory_space=pltpu.SMEM),
            pl.BlockSpec(memory_space=pltpu.SMEM),
        ],
        out_specs=pl.BlockSpec(memory_space=pltpu.VMEM),
        scratch_shapes=[
            pltpu.VMEM((NB, 3, 2, VB, CHUNK), bf16),
            pltpu.VMEM((NB, 3, 2, VB, CHUNK), bf16),
            pltpu.VMEM((NB, 3, 2, VB, CHUNK), bf16),
            pltpu.VMEM((2, 3, 2, VB, CHUNK), bf16),
            pltpu.VMEM((NB, VB, CHUNK), bf16),
            pltpu.VMEM((NB, VB, CHUNK), bf16),
            pltpu.VMEM((3, 3, 3, 2, CHUNK), f32),
            pltpu.VMEM((3, 3, 2, NV, CHUNK), bf16),
            pltpu.VMEM((NV, NV), bf16),
            pltpu.VMEM((2, NV, 3 * CHUNK), bf16),
            pltpu.VMEM((2, NV, 128), f32),
            pltpu.VMEM((2, 2, NY, NX, 2, 16, 128), f32),
            pltpu.VMEM((2, NY, NX, 2, 16, 128), f32),
            pltpu.VMEM((2, NX * NY - 1, 2, 16, 128), f32),
            pltpu.VMEM((16, 4, 128), f32),
            pltpu.VMEM((zs, 4, 128), f32),
            pltpu.VMEM((6 * NK + 2, 128), f32),
            dma((2,)),
            dma((NB,)),
            dma((NB - 1,)),
            dma((NB - 1,)),
            dma((NB - 1,)),
            dma((NB - 1,)),
            dma((NB,)),
            dma((NB,)),
            dma((2,)),
            dma((2,)),
            dma((2, NY)),
            dma((2, NY)),
            dma((2, NX * NY - 1)),
            dma((2, NX * NY - 1)),
            dma((zs,)),
            dma((zs,)),
        ],
        compiler_params=pltpu.CompilerParams(
            collective_id=0, has_side_effects=True, vmem_limit_bytes=63 * 1024 * 1024
        ),
        name="elementals",
    )(vectors, links, directions, offsets)


def solution(mesh):
    placed = (
        P("space", None, None, "vec", None),
        P("space", None, None, None, None, None),
        P(),
        P(),
    )
    return jax.shard_map(
        body,
        mesh=mesh,
        in_specs=placed,
        out_specs=P(None, None, None, "vec", "space"),
        check_vma=False,
    )
```
